32 devices in a mesh: dp: 16 (over z, y, core), tensor: 2 (over x).
Axes of the slice: x: 2, y: 2, z: 4, core: 2. Of those that a mesh axis runs over, the one named last changes fastest.
Arguments:
- tokens: bfloat16 [16, 1024, 1024], P('dp', 'tensor'), may hold values from -6 to 6
- segment_ids: int32 [16, 1024], P('dp'), may hold values from 0 to 2, as said below
- norm_gains: float32 [2, 1024], replicated, may hold values from 0.25 to 1.75
- w_mixer_in: bfloat16 [1024, 4, 8, 128], P('dp', None, 'tensor'), may hold values from -0.1875 to 0.1875
- w_rates: bfloat16 [1024, 2, 8], P('dp', None, 'tensor'), may hold values from -0.1875 to 0.1875
- conv_weight: bfloat16 [3, 4, 8, 128], P(None, None, 'tensor', 'dp'), may hold values from -3 to 3
- a_log: float32 [8], replicated, may hold values from -7 to -3
- out_gain: float32 [128], replicated, may hold values from 0.25 to 1.75
- w_output: bfloat16 [1024, 1024], P('tensor', 'dp'), may hold values from -0.25 to 0.25
- w_gate_up: bfloat16 [1024, 2, 2816], P('dp', None, 'tensor'), may hold values from -0.1875 to 0.1875
- w_down: bfloat16 [2816, 1024], P('tensor', 'dp'), may hold values from -0.21875 to 0.21875
- cotangent: bfloat16 [16, 1024, 1024], P('dp', 'tensor'), may hold values from -6 to 6
Outputs:
- out_tokens: bfloat16 [16, 1024, 1024], P('dp', 'tensor')
- grad_tokens: bfloat16 [16, 1024, 1024], P('dp', 'tensor')
- grad_norm_gains: float32 [2, 1024], replicated
- grad_w_mixer_in: float32 [1024, 4, 8, 128], P('dp', None, 'tensor')
- grad_w_rates: float32 [1024, 2, 8], P('dp', None, 'tensor')
- grad_conv_weight: float32 [3, 4, 8, 128], P(None, None, 'tensor', 'dp')
- grad_a_log: float32 [8], replicated
- grad_out_gain: float32 [128], replicated
- grad_w_output: float32 [1024, 1024], P('tensor', 'dp')
- grad_w_gate_up: float32 [1024, 2, 2816], P('dp', None, 'tensor')
- grad_w_down: float32 [2816, 1024], P('tensor', 'dp')
The draws below stay inside these ranges and needn't reach their ends.
Inputs may be any that keep to these rules, and one draw needn't show every extreme that they name: `segment_ids`: each sequence holds exactly three documents, numbered 0, 1 and 2 in order along it, each of 200 tokens or more; document numbers never fall along a sequence.
All inputs are finite; a program needn't handle non-finite values.
Results may differ from the reference program's by a relative error of at most 0.022.
Values may be sent and summed in bfloat16 or wider, within the bound.
No kernel may reach another device: no remote copies, remote signals or barrier semaphores. Data moves between devices by JAX's collectives and lax.ppermute only.
A program may use at most 256 MiB of HBM per device.

```python
import jax
import jax.numpy as jnp
from jax import lax

D = 1024
H = 8
DH = 128
FF = 2816
CONV = 4
SPAN = 64
DOC_MIN = 200
SEQ = 1024
SEQS = 16


def draw_segment_ids(key, part):
    key = jax.random.fold_in(key, 7)
    first_key, second_key = jax.random.split(key)
    first_cut = jax.random.randint(first_key, (SEQS, 1), DOC_MIN, SEQ - 2 * DOC_MIN + 1)
    second_cut = jax.random.randint(second_key, (SEQS, 1), first_cut + DOC_MIN, SEQ - DOC_MIN + 1)
    position = jnp.arange(SEQ, dtype=jnp.int32)[None, :]
    return (position >= first_cut).astype(jnp.int32) + (position >= second_cut).astype(jnp.int32)


def level_of(key, dims, pieces, least, high):
    loudness = 1.0
    for axis_at, blocks in pieces:
        heights = jax.random.uniform(jax.random.fold_in(jax.random.fold_in(key, 6), axis_at), (blocks,), jnp.float32, least / len(pieces), high / len(pieces))
        loudness = loudness * jnp.repeat(jnp.exp(heights), dims[axis_at] // blocks).reshape((-1,) + (1,) * (len(dims) - 1 - axis_at))
    return loudness


def gaussian(key, shape, deviation, most, pieces=(), kind=jnp.bfloat16):
    factor_of = level_of(key, shape, pieces, -0.22, 0.18) if pieces else 1.0
    values = jax.random.normal(key, shape, jnp.float32) * deviation * factor_of
    return jnp.minimum(jnp.maximum(values, -most), most).astype(kind)


def setup_inputs(seed: int = 0) -> dict:
    splits = jax.random.split(jax.random.key(seed), 13)
    return {
        "tokens": gaussian(splits[0], (SEQS, SEQ, D), 1.0, 6.0, ((0, 16), (1, 2))),
        "segment_ids": draw_segment_ids(jax.random.fold_in(splits[12], 71), 0),
        "norm_gains": jnp.clip(1.0 + 0.15 * jax.random.normal(splits[2], (2, D), jnp.float32), 0.25, 1.75),
        "w_mixer_in": gaussian(splits[3], (D, 4, H, DH), D ** -0.5, 0.1875, ((0, 16), (2, 2))),
        "w_rates": gaussian(splits[4], (D, 2, H), D ** -0.5, 0.1875, ((0, 16), (2, 2))),
        "conv_weight": gaussian(splits[5], (3, CONV, H, DH), CONV ** -0.5, 3.0, ((2, 2), (3, 16))),
        "a_log": jnp.clip(jax.random.uniform(splits[6], (H,), jnp.float32, -7.0, -3.0), -7.0, -3.0),
        "out_gain": jnp.clip(1.0 + 0.15 * jax.random.normal(splits[7], (DH,), jnp.float32), 0.25, 1.75),
        "w_output": gaussian(splits[8], (H * DH, D), (H * DH // 2) ** -0.5, 0.25, ((0, 2), (1, 16))),
        "w_gate_up": gaussian(splits[9], (D, 2, FF), D ** -0.5, 0.1875, ((0, 16), (2, 2))),
        "w_down": gaussian(splits[10], (FF, D), (FF // 4) ** -0.5, 0.21875, ((0, 2), (1, 16))),
        "cotangent": gaussian(splits[11], (SEQS, SEQ, D), 1.0, 6.0, ((0, 16), (1, 2))),
    }


highest = lax.Precision.HIGHEST
norm_eps = 1e-05
unit_eps = 1e-06

@jax.custom_vjp
def low(v):
    return lax.optimization_barrier(v.astype(jnp.bfloat16)).astype(jnp.float32)

@jax.custom_vjp
def low_back(v):
    return v

def low_keep(v):
    return (low(v), None)

def low_pass(kept, grad):
    return (grad,)

def back_keep(v):
    return (v, None)

def back_low(kept, grad):
    return (low(grad),)
low.defvjp(low_keep, low_pass)
low_back.defvjp(back_keep, back_low)

def rms_norm(values, scales):
    return values * lax.rsqrt(lax.optimization_barrier(jnp.mean(values * values, axis=-1, keepdims=True)) + norm_eps) * scales

def short_conv(signal, weight, segment):
    length = signal.shape[0]
    tap_count = weight.shape[0]
    result = jnp.zeros_like(signal)
    for offset in range(tap_count):
        shifted = jnp.concatenate([jnp.zeros((offset,) + signal.shape[1:], signal.dtype), signal[:length - offset]], axis=0)
        earlier = jnp.concatenate([jnp.full((offset,), -1, jnp.int32), segment[:length - offset]], axis=0)
        same_doc = jnp.where(earlier == segment, 1.0, 0.0).astype(signal.dtype)
        result = result + weight[tap_count - 1 - offset] * shifted * same_doc[:, None, None]
    return result

def span_step(state_pair, blocks):
    memory, last_seen = state_pair
    queries, key_rows, value_rows, decays, beta_rows, segment = blocks
    block_len = segment.shape[0]
    cumulative = jnp.cumsum(decays, axis=0)
    same_doc = segment[:, None] == segment[None, :]
    row_index = lax.broadcasted_iota(jnp.int32, (block_len, block_len), 0)
    col_index = lax.broadcasted_iota(jnp.int32, (block_len, block_len), 1)
    strict_mask = (same_doc & (row_index > col_index))[:, :, None]
    within_mask = (same_doc & (row_index >= col_index))[:, :, None]
    log_gap = cumulative[:, None, :] - cumulative[None, :, :]
    strict_decay = jnp.where(strict_mask, jnp.exp(jnp.where(strict_mask, log_gap, 0.0)), 0.0)
    within_decay = jnp.where(within_mask, jnp.exp(jnp.where(within_mask, log_gap, 0.0)), 0.0)
    carry_on = segment == last_seen
    start_scale = jnp.where(carry_on[:, None], jnp.exp(cumulative), 0.0)
    key_dots = jnp.einsum('ihd,jhd->hij', key_rows, key_rows, precision=highest)
    lower_part = key_dots * (strict_decay * beta_rows[:, None, :]).transpose(2, 0, 1)
    system = jnp.eye(block_len, dtype=lower_part.dtype)[None] + lower_part
    carried = jnp.einsum('ihk,hvk->ihv', key_rows, memory, precision=highest)
    target = beta_rows[:, :, None] * (value_rows - start_scale[:, :, None] * carried)
    pseudo = jax.scipy.linalg.solve_triangular(system, target.transpose(1, 0, 2), lower=True, unit_diagonal=True)
    scores = jnp.einsum('ihd,jhd->hij', queries, key_rows, precision=highest) * within_decay.transpose(2, 0, 1)
    output = jnp.einsum('hij,hjv->ihv', scores, pseudo, precision=highest)
    output = output + start_scale[:, :, None] * jnp.einsum('ihk,hvk->ihv', queries, memory, precision=highest)
    last_doc = segment[block_len - 1]
    end_scale = jnp.where((segment == last_doc)[:, None], jnp.exp(cumulative[block_len - 1][None, :] - cumulative), 0.0)
    whole_keep = jnp.where(carry_on[block_len - 1], jnp.exp(cumulative[block_len - 1]), 0.0)
    memory = whole_keep[:, None, None] * memory + jnp.einsum('hiv,ih,ihk->hvk', pseudo, end_scale, key_rows, precision=highest)
    return ((memory, last_doc), output)

def delta_rule(queries, key_rows, value_rows, decays, beta_rows, segment):
    full_length, head_count, value_width = value_rows.shape
    block_count = full_length // SPAN

    def to_blocks(stacked):
        return stacked.reshape((block_count, SPAN) + stacked.shape[1:])
    memory = jnp.zeros((head_count, value_width, key_rows.shape[2]), value_rows.dtype)
    no_doc = jnp.full((), -1, jnp.int32)
    last_pair, outputs = lax.scan(jax.checkpoint(span_step), (memory, no_doc), (to_blocks(queries), to_blocks(key_rows), to_blocks(value_rows), to_blocks(decays), to_blocks(beta_rows), to_blocks(segment)))
    return outputs.reshape(full_length, head_count, value_width)

def mixer(projected, rate_logits, conv_weight, a_log, out_gain, segment):
    queries = jax.nn.silu(short_conv(projected[:, 0], conv_weight[0], segment))
    key_rows = jax.nn.silu(short_conv(projected[:, 1], conv_weight[1], segment))
    value_rows = jax.nn.silu(short_conv(projected[:, 2], conv_weight[2], segment))
    queries = queries * lax.rsqrt(lax.optimization_barrier(jnp.sum(queries * queries, axis=-1, keepdims=True)) + unit_eps) * queries.shape[-1] ** (-0.5)
    key_rows = key_rows * lax.rsqrt(lax.optimization_barrier(jnp.sum(key_rows * key_rows, axis=-1, keepdims=True)) + unit_eps)
    beta_rows = jax.nn.sigmoid(rate_logits[:, 1])
    decays = -jnp.exp(a_log) * jax.nn.softplus(rate_logits[:, 0])
    mixed_out = delta_rule(queries, key_rows, value_rows, decays, beta_rows, segment)
    mixed_out = mixed_out * lax.rsqrt(lax.optimization_barrier(jnp.mean(mixed_out * mixed_out, axis=-1, keepdims=True)) + norm_eps) * out_gain * jax.nn.silu(projected[:, 3])
    return mixed_out.reshape(mixed_out.shape[0], -1)

def block(block_in, weights, segment):
    norm_gains, w_mixer_in, w_rates, conv_weight, a_log, out_gain, w_output, w_gate_up, w_down = weights
    batch_size, length, model_width = block_in.shape
    head_count = w_rates.shape[2]
    flat_rows = block_in.reshape(batch_size * length, model_width)
    normed = low(rms_norm(flat_rows, norm_gains[0]))
    projected = low_back(jnp.dot(normed.astype(jnp.float32), w_mixer_in.reshape(model_width, -1).astype(jnp.float32), precision=highest, preferred_element_type=jnp.float32))
    rate_logits = low_back(jnp.dot(normed.astype(jnp.float32), w_rates.reshape(model_width, -1).astype(jnp.float32), precision=highest, preferred_element_type=jnp.float32))
    projected = projected.reshape(batch_size, length, 4, head_count, -1)
    rate_logits = rate_logits.reshape(batch_size, length, 2, head_count)
    mixed_out = jax.vmap(mixer, in_axes=(0, 0, None, None, None, 0))(projected, rate_logits, conv_weight, a_log, out_gain, segment)
    mixed_low = low(mixed_out.reshape(batch_size * length, -1))
    residual = flat_rows + low_back(jnp.dot(mixed_low.astype(jnp.float32), w_output.astype(jnp.float32), precision=highest, preferred_element_type=jnp.float32))
    normed_ffn = low(rms_norm(residual, norm_gains[1]))
    gate_up = low_back(jnp.dot(normed_ffn.astype(jnp.float32), w_gate_up.reshape(model_width, -1).astype(jnp.float32), precision=highest, preferred_element_type=jnp.float32))
    hidden_units = w_down.shape[0]
    hidden = low(jax.nn.silu(gate_up[:, :hidden_units]) * gate_up[:, hidden_units:])
    result = residual + jnp.dot(hidden.astype(jnp.float32), w_down.astype(jnp.float32), precision=highest, preferred_element_type=jnp.float32)
    return result.reshape(batch_size, length, model_width)

def reference(tokens, segment_ids, norm_gains, w_mixer_in, w_rates, conv_weight, a_log, out_gain, w_output, w_gate_up, w_down, cotangent):
    weights = tuple((weight.astype(jnp.float32) for weight in (norm_gains, w_mixer_in, w_rates, conv_weight, a_log, out_gain, w_output, w_gate_up, w_down)))
    group_size = 4
    group_count = tokens.shape[0] // group_size

    def grouped(stacked):
        return stacked.reshape((group_count, group_size) + stacked.shape[1:])

    def one_group(grad_sum, inputs):
        block_in, segment, block_cot = inputs

        def forward(values, params):
            return block(values, params, segment)
        block_out, pullback = jax.vjp(forward, block_in.astype(jnp.float32), weights)
        block_dx, param_grads = pullback(block_cot.astype(jnp.float32))
        grad_sum = jax.tree.map(lambda first, second: first + second, grad_sum, param_grads)
        return (grad_sum, (block_out.astype(jnp.bfloat16), block_dx.astype(jnp.bfloat16)))
    zero_grads = jax.tree.map(jnp.zeros_like, weights)
    grad_sum, (outputs, input_grads) = lax.scan(one_group, zero_grads, (grouped(tokens), grouped(segment_ids), grouped(cotangent)))
    return (outputs.reshape(tokens.shape), input_grads.reshape(tokens.shape), grad_sum[0], grad_sum[1], grad_sum[2], grad_sum[3], grad_sum[4], grad_sum[5], grad_sum[6], grad_sum[7], grad_sum[8])
```

```python
import functools

import jax
import jax.numpy as jnp
from jax import lax
from jax.experimental import pallas as pl
from jax.experimental.pallas import tpu as pltpu
from jax.sharding import PartitionSpec as P

CHUNK = 128
WIDTH = 128
HALO = 8
norm_eps = 1e-05
unit_eps = 1e-06
f32 = jnp.float32
bf16 = jnp.bfloat16

NN = ((1,), (0,))
NT = ((1,), (1,))
TN = ((0,), (0,))


def dot(left, right, dims):
    return lax.dot_general(
        left.astype(bf16), right.astype(bf16), (dims, ((), ())), preferred_element_type=f32
    )


def dot_exact(left, right, dims):
    return lax.dot_general(
        left, right, (dims, ((), ())), precision=lax.Precision.HIGHEST, preferred_element_type=f32
    )


def sigmoid(value):
    return 1.0 / (1.0 + jnp.exp(-value))


def softplus(value):
    return jnp.maximum(value, 0.0) + jnp.log(1.0 + jnp.exp(-jnp.abs(value)))


def shifted(rows, offset):
    return pltpu.roll(rows, offset, 0)[HALO:] if offset else rows[HALO:]


def conv_terms(rows, keeps):
    return [rows[HALO:]] + [
        jnp.where(keeps[offset], shifted(rows, offset), 0.0) for offset in range(1, 4)
    ]


def conv_sum(terms, conv_ref, part, lanes):
    total = None
    for offset in range(4):
        weight = conv_ref[pl.ds(part * 4 + 3 - offset, 1), lanes]
        term = weight * terms[offset]
        total = term if total is None else total + term
    return total


def lane_column(values, lane):
    return jnp.broadcast_to(values[:, lane : lane + 1], values.shape)


def grids():
    row = lax.broadcasted_iota(jnp.int32, (CHUNK, CHUNK), 0)
    col = lax.broadcasted_iota(jnp.int32, (CHUNK, CHUNK), 1)
    return row, col


def level_masks(row, col):
    masks = []
    shift = 0
    while (1 << shift) < CHUNK:
        near = (row >> (shift + 1)) == (col >> (shift + 1))
        apart = (row >> shift) != (col >> shift)
        masks.append(near & apart)
        shift += 1
    return masks


def unit_lower_inverses(lowers, row, col):
    masks = level_masks(row, col)
    identity = jnp.where(row == col, 1.0, 0.0).astype(f32)
    inverses = [identity - jnp.where(masks[0], lower, 0.0) for lower in lowers]
    for mask in masks[1:]:
        blocks = [jnp.where(mask, lower, 0.0) for lower in lowers]
        firsts = [dot(inverse, block, NN) for inverse, block in zip(inverses, blocks)]
        inverses = [inverse - dot(first, inverse, NN) for first, inverse in zip(firsts, inverses)]
    return inverses


def chunk_scales(heads, rates, neg_rate, seg, last_seen, row, col):
    steps = neg_rate * softplus(rates)
    lower_ones = jnp.where(row >= col, 1.0, 0.0).astype(f32)
    cumulative = dot_exact(lower_ones, steps, NN)
    cumulative_rows = cumulative.T
    betas = sigmoid(rates)
    seg_rows = seg.T
    same = seg == seg_rows
    within = same & (row >= col)
    strict = same & (row > col)
    carry = seg == last_seen
    ends = seg == seg[CHUNK - 1 :, :]
    scales = []
    for head in range(heads):
        cum = lane_column(cumulative, head)
        cum_row = cumulative_rows[head : head + 1, :]
        gap = jnp.exp(jnp.minimum(cum - cum_row, 0.0))
        last = cum[CHUNK - 1 :, :]
        scales.append(
            dict(
                beta=lane_column(betas, heads + head),
                within=jnp.where(within, gap, 0.0),
                strict=jnp.where(strict, gap, 0.0),
                start=jnp.where(carry, jnp.exp(cum), 0.0),
                end=jnp.where(ends, jnp.exp(jnp.minimum(last - cum, 0.0)), 0.0),
                keep=jnp.where(carry[CHUNK - 1 :, :], jnp.exp(last), 0.0),
            )
        )
    return scales, steps, betas


def forward_kernel(
    heads, proj_ref, seg_ref, conv_ref, rate_ref, gain_ref,
    mixed_ref, inverse_ref, w_ref, pseudo_ref, out_ref, state_ref,
    state, halo, seg_halo,
):
    step = pl.program_id(0)

    @pl.when(step == 0)
    def _():
        state[...] = jnp.zeros_like(state)
        halo[...] = jnp.zeros_like(halo)
        seg_halo[...] = jnp.full_like(seg_halo, -1.0)

    row, col = grids()
    seg = seg_ref[...]
    seg_rows = jnp.concatenate([seg_halo[...], seg], axis=0)
    keeps = [None] + [shifted(seg_rows, offset) == seg for offset in range(1, 4)]
    last_seen = seg_halo[HALO - 1 :, :]
    wide = heads * WIDTH
    rates = proj_ref[:, 4 * wide : 4 * wide + WIDTH]
    scales, _, _ = chunk_scales(heads, rates, rate_ref[...], seg, last_seen, row, col)

    queries, keys, values = [], [], []
    for head in range(heads):
        for part, into in ((0, queries), (1, keys), (2, values)):
            at = part * wide + head * WIDTH
            lanes = slice(at, at + WIDTH)
            rows = jnp.concatenate([halo[:, lanes], proj_ref[:, lanes]], axis=0)
            terms = conv_terms(rows, keeps)
            total = conv_sum(terms, conv_ref, part, slice(head * WIDTH, (head + 1) * WIDTH))
            into.append(total * sigmoid(total))
    for head in range(heads):
        query, key = queries[head], keys[head]
        queries[head] = query * (
            lax.rsqrt(jnp.sum(query * query, axis=-1, keepdims=True) + unit_eps) * WIDTH**-0.5
        )
        keys[head] = key * lax.rsqrt(jnp.sum(key * key, axis=-1, keepdims=True) + unit_eps)
    halo[...] = proj_ref[CHUNK - HALO :, : 3 * wide]
    seg_halo[...] = seg[CHUNK - HALO :, :]

    lowers, scores = [], []
    for head in range(heads):
        scale = scales[head]
        both = dot(jnp.concatenate([keys[head], queries[head]], axis=0), keys[head], NT)
        lowers.append(both[:CHUNK] * scale["strict"] * scale["beta"])
        scores.append(both[CHUNK:] * scale["within"])
    inverses = unit_lower_inverses(lowers, row, col)
    for head in range(heads):
        scale = scales[head]
        lanes = slice(head * WIDTH, (head + 1) * WIDTH)
        inverse = inverses[head].astype(bf16)
        inverse_ref[:, lanes] = inverse
        memory = state[head]
        state_ref[0, head] = memory.astype(state_ref.dtype)
        target = jnp.concatenate(
            [scale["beta"] * values[head], scale["beta"] * scale["start"] * keys[head]], axis=1
        )
        solved = dot(inverse, target, NN)
        carried = solved[:, WIDTH:]
        w_ref[:, lanes] = carried.astype(bf16)
        read = dot(
            jnp.concatenate([carried, scale["start"] * queries[head]], axis=0), memory, NN
        )
        pseudo = solved[:, :WIDTH] - read[:CHUNK]
        pseudo_ref[:, lanes] = pseudo.astype(bf16)
        output = dot(scores[head], pseudo, NN) + read[CHUNK:]
        out_ref[:, lanes] = output
        state[head] = scale["keep"] * memory + dot(scale["end"] * keys[head], pseudo, TN)
        gate = proj_ref[:, 3 * wide + head * WIDTH : 3 * wide + (head + 1) * WIDTH]
        unit = output * lax.rsqrt(jnp.mean(output * output, axis=-1, keepdims=True) + norm_eps)
        mixed_ref[:, lanes] = (unit * gain_ref[...] * gate * sigmoid(gate)).astype(bf16)


def backward_kernel(
    heads, proj_ref, seg_ref, seg_before_ref, before_ref, conv_ref, rate_ref, gain_ref, grad_ref,
    inverse_ref, w_ref, pseudo_ref, out_ref, state_ref,
    dproj_ref, dconv_ref, drate_ref, dgain_ref,
    dstate, carry_halo,
):
    step = pl.program_id(0)
    first = step == pl.num_programs(0) - 1

    @pl.when(step == 0)
    def _():
        dstate[...] = jnp.zeros_like(dstate)
        carry_halo[...] = jnp.zeros_like(carry_halo)
        dconv_ref[...] = jnp.zeros_like(dconv_ref)
        drate_ref[...] = jnp.zeros_like(drate_ref)
        dgain_ref[...] = jnp.zeros_like(dgain_ref)

    row, col = grids()
    seg = seg_ref[...]
    seg_before = jnp.where(first, -1.0, seg_before_ref[...])
    seg_rows = jnp.concatenate([seg_before, seg], axis=0)
    keeps = [None] + [shifted(seg_rows, offset) == seg for offset in range(1, 4)]
    last_seen = seg_before[HALO - 1 :, :]
    wide = heads * WIDTH
    rates = proj_ref[:, 4 * wide : 4 * wide + WIDTH]
    neg_rate = rate_ref[...]
    scales, steps, betas = chunk_scales(heads, rates, neg_rate, seg, last_seen, row, col)

    def rows_of(part, head):
        at = part * wide + head * WIDTH
        lanes = slice(at, at + WIDTH)
        return jnp.concatenate([before_ref[:, lanes], proj_ref[:, lanes]], axis=0)

    def signal(part, head):
        terms = conv_terms(rows_of(part, head), keeps)
        total = conv_sum(terms, conv_ref, part, slice(head * WIDTH, (head + 1) * WIDTH))
        gate = sigmoid(total)
        return terms, total, gate

    def signal_back(part, head, terms, total, gate, grad):
        grad = grad * (gate * (1.0 + total * (1.0 - gate)))
        lanes = slice(head * WIDTH, (head + 1) * WIDTH)
        spread = None
        for offset in range(4):
            tap = pl.ds(part * 4 + 3 - offset, 1)
            dconv_ref[tap, lanes] += jnp.sum(grad * terms[offset], axis=0, keepdims=True)
            back = conv_ref[tap, lanes] * grad
            if offset:
                back = jnp.where(keeps[offset], back, 0.0)
            back = jnp.concatenate([jnp.zeros((HALO, WIDTH), f32), back], axis=0)
            if offset:
                back = pltpu.roll(back, CHUNK + HALO - offset, 0)
            spread = back if spread is None else spread + back
        at = part * wide + head * WIDTH
        lanes = slice(at, at + WIDTH)
        tail = jnp.concatenate(
            [jnp.zeros((CHUNK - HALO, WIDTH), f32), carry_halo[:, lanes]], axis=0
        )
        dproj_ref[:, lanes] = (spread[HALO:] + tail).astype(bf16)
        carry_halo[:, lanes] = spread[:HALO]

    lane = col
    cum_columns = jnp.zeros((CHUNK, WIDTH), f32)
    cum_rows = jnp.zeros((CHUNK, CHUNK), f32)
    dbeta_columns = jnp.zeros((CHUNK, WIDTH), f32)
    dgain = jnp.zeros((1, WIDTH), f32)
    for head in range(heads):
        scale = scales[head]
        lanes = slice(head * WIDTH, (head + 1) * WIDTH)
        beta, start, end, keep = scale["beta"], scale["start"], scale["end"], scale["keep"]
        q_terms, q_total, q_gate = signal(0, head)
        k_terms, k_total, k_gate = signal(1, head)
        v_terms, v_total, v_gate = signal(2, head)
        q_act, k_act, value = q_total * q_gate, k_total * k_gate, v_total * v_gate
        q_norm = lax.rsqrt(jnp.sum(q_act * q_act, axis=-1, keepdims=True) + unit_eps)
        k_norm = lax.rsqrt(jnp.sum(k_act * k_act, axis=-1, keepdims=True) + unit_eps)
        q_unit, key = q_act * q_norm, k_act * k_norm
        query = q_unit * WIDTH**-0.5

        gain = gain_ref[...]
        gate_at = slice(3 * wide + head * WIDTH, 3 * wide + (head + 1) * WIDTH)
        gate = proj_ref[:, gate_at]
        gate_s = sigmoid(gate)
        gate_act = gate * gate_s
        grad = grad_ref[:, lanes].astype(f32)
        output = out_ref[:, lanes]
        inv_rms = lax.rsqrt(jnp.mean(output * output, axis=-1, keepdims=True) + norm_eps)
        unit = output * inv_rms
        grad_unit = grad * unit
        dgain = dgain + jnp.sum(grad_unit * gate_act, axis=0, keepdims=True)
        dproj_ref[:, gate_at] = (
            grad_unit * gain * (gate_s * (1.0 + gate * (1.0 - gate_s)))
        ).astype(bf16)
        dunit = grad * (gain * gate_act)
        dout = inv_rms * (dunit - unit * jnp.mean(dunit * unit, axis=-1, keepdims=True))

        both = dot(jnp.concatenate([key, query], axis=0), key, NT)
        lower_raw = both[:CHUNK] * scale["strict"]
        lower = lower_raw * beta
        scores = both[CHUNK:] * scale["within"]
        inverse = inverse_ref[:, lanes]
        pseudo = pseudo_ref[:, lanes]
        memory = state_ref[0, head]
        dmemory = dstate[head]

        dpseudo = dot(scores, dout, TN) + dot(end * key, dmemory, NN)
        start_query = start * query
        dstate[head] = keep * dmemory + dot(
            jnp.concatenate([start_query.astype(bf16), -w_ref[:, lanes]], axis=0),
            jnp.concatenate([dout.astype(bf16), dpseudo.astype(bf16)], axis=0),
            TN,
        )
        solved = dot(inverse, dpseudo, TN)
        reads = dot(jnp.concatenate([dout, solved], axis=0), memory, NT)
        dquery_start = start * reads[:CHUNK]
        dkey_start = -start * reads[CHUNK:]
        by_pseudo = dot(jnp.concatenate([dout, solved], axis=0), pseudo, NT)
        dscores = by_pseudo[:CHUNK]
        dlower = -by_pseudo[CHUNK:]
        dkey_end = end * dot(pseudo, dmemory, NT)

        dbeta = jnp.sum(
            solved * value + dkey_start * key + dlower * lower_raw, axis=-1, keepdims=True
        )
        pair = dscores * scores + dlower * lower
        end_terms = dkey_end * key
        dcum = jnp.sum(
            pair + dquery_start * query + (dkey_start * key) * beta - end_terms,
            axis=-1,
            keepdims=True,
        )
        last_total = jnp.sum(
            jnp.sum(end_terms, axis=0, keepdims=True)
            + keep * jnp.sum(memory * dmemory, axis=0, keepdims=True),
            axis=-1,
            keepdims=True,
        )
        dcum = dcum + jnp.where(row[:, :1] == CHUNK - 1, last_total, 0.0)
        cum_columns = cum_columns + jnp.where(lane == head, dcum, 0.0)
        dbeta_columns = dbeta_columns + jnp.where(lane == heads + head, dbeta, 0.0)
        cum_rows = cum_rows + jnp.where(row == head, jnp.sum(pair, axis=0, keepdims=True), 0.0)

        near = (dlower * (scale["strict"] * beta)).astype(bf16)
        far = (dscores * scale["within"]).astype(bf16)
        toward = dot(jnp.concatenate([near, far], axis=0), key, NN)
        dkey = (
            toward[:CHUNK]
            + dot(
                jnp.concatenate([near, far], axis=0),
                jnp.concatenate([key, query], axis=0),
                TN,
            )
            + beta * dkey_start
            + dkey_end
        )
        dquery = (toward[CHUNK:] + dquery_start) * WIDTH**-0.5
        dvalue = beta * solved
        dq_act = q_norm * (dquery - q_unit * jnp.sum(q_unit * dquery, axis=-1, keepdims=True))
        dk_act = k_norm * (dkey - key * jnp.sum(key * dkey, axis=-1, keepdims=True))
        signal_back(0, head, q_terms, q_total, q_gate, dq_act)
        signal_back(1, head, k_terms, k_total, k_gate, dk_act)
        signal_back(2, head, v_terms, v_total, v_gate, dvalue)

    upper_ones = jnp.where(row <= col, 1.0, 0.0).astype(f32)
    dsteps = dot_exact(upper_ones, cum_columns - cum_rows.T, NN)
    drate_ref[...] += jnp.sum(dsteps * steps, axis=0, keepdims=True)
    dgain_ref[...] += dgain
    dlogits = dsteps * neg_rate * betas + dbeta_columns * betas * (1.0 - betas)
    dproj_ref[:, 4 * wide : 4 * wide + WIDTH] = jnp.where(
        lane < 2 * heads, dlogits, 0.0
    ).astype(bf16)


def mixer_forward(proj, seg_wide, conv_rows, neg_rate, gain):
    length, width = proj.shape
    heads = (width - WIDTH) // (4 * WIDTH)
    wide = heads * WIDTH
    count = length // CHUNK
    by_chunk = lambda cols: pl.BlockSpec((CHUNK, cols), lambda i: (i, 0))
    whole = lambda rows, cols: pl.BlockSpec((rows, cols), lambda i: (0, 0))
    return pl.pallas_call(
        functools.partial(forward_kernel, heads),
        grid=(count,),
        in_specs=[
            by_chunk(width), by_chunk(WIDTH), whole(12, wide), whole(1, WIDTH), whole(1, WIDTH),
        ],
        out_specs=[
            by_chunk(wide), by_chunk(wide), by_chunk(wide), by_chunk(wide), by_chunk(wide),
            pl.BlockSpec((1, heads, WIDTH, WIDTH), lambda i: (i, 0, 0, 0)),
        ],
        out_shape=[
            jax.ShapeDtypeStruct((length, wide), bf16),
            jax.ShapeDtypeStruct((length, wide), bf16),
            jax.ShapeDtypeStruct((length, wide), bf16),
            jax.ShapeDtypeStruct((length, wide), bf16),
            jax.ShapeDtypeStruct((length, wide), f32),
            jax.ShapeDtypeStruct((count, heads, WIDTH, WIDTH), f32),
        ],
        scratch_shapes=[
            pltpu.VMEM((heads, WIDTH, WIDTH), f32),
            pltpu.VMEM((HALO, 3 * wide), f32),
            pltpu.VMEM((HALO, WIDTH), f32),
        ],
        compiler_params=pltpu.CompilerParams(vmem_limit_bytes=48 * 1024 * 1024),
        name="mixer_forward",
    )(proj, seg_wide, conv_rows, neg_rate, gain)


def mixer_backward(proj, seg_wide, conv_rows, neg_rate, gain, grad, saved):
    length, width = proj.shape
    heads = (width - WIDTH) // (4 * WIDTH)
    wide = heads * WIDTH
    count = length // CHUNK
    back = lambda i: count - 1 - i
    by_chunk = lambda cols: pl.BlockSpec((CHUNK, cols), lambda i: (back(i), 0))
    before = lambda cols: pl.BlockSpec(
        (HALO, cols), lambda i: (jnp.maximum(back(i) * (CHUNK // HALO) - 1, 0), 0)
    )
    whole = lambda rows, cols: pl.BlockSpec((rows, cols), lambda i: (0, 0))
    return pl.pallas_call(
        functools.partial(backward_kernel, heads),
        grid=(count,),
        in_specs=[
            by_chunk(width), by_chunk(WIDTH), before(WIDTH), before(3 * wide),
            whole(12, wide), whole(1, WIDTH), whole(1, WIDTH),
            by_chunk(wide), by_chunk(wide), by_chunk(wide), by_chunk(wide), by_chunk(wide),
            pl.BlockSpec((1, heads, WIDTH, WIDTH), lambda i: (back(i), 0, 0, 0)),
        ],
        out_specs=[by_chunk(width), whole(12, wide), whole(1, WIDTH), whole(1, WIDTH)],
        out_shape=[
            jax.ShapeDtypeStruct((length, width), bf16),
            jax.ShapeDtypeStruct((12, wide), f32),
            jax.ShapeDtypeStruct((1, WIDTH), f32),
            jax.ShapeDtypeStruct((1, WIDTH), f32),
        ],
        scratch_shapes=[
            pltpu.VMEM((heads, WIDTH, WIDTH), f32),
            pltpu.VMEM((HALO, 3 * wide), f32),
        ],
        compiler_params=pltpu.CompilerParams(vmem_limit_bytes=48 * 1024 * 1024),
        name="mixer_backward",
    )(proj, seg_wide, seg_wide, proj, conv_rows, neg_rate, gain, grad, *saved)


def rms_norm(values, scales):
    return values * lax.rsqrt(jnp.mean(values * values, axis=-1, keepdims=True) + norm_eps) * scales


def first_norm(values, gains):
    return rms_norm(values, gains[0])


def second_norm(values, gains):
    return rms_norm(values, gains[1])


def swish_product(gate_up):
    return jax.nn.silu(gate_up[:, 0]) * gate_up[:, 1]


def contract_last(operand, other):
    return lax.dot_general(
        operand, other, (((1,), (1,)), ((), ())), preferred_element_type=jnp.float32
    )


def contract_first(operand, other):
    return lax.dot_general(
        operand, other, (((0,), (0,)), ((), ())), preferred_element_type=jnp.float32
    )


def swap(rows):
    return lax.ppermute(rows, "tensor", [(0, 1), (1, 0)])


def local(
    tokens,
    segment_ids,
    norm_gains,
    w_mixer_in,
    w_rates,
    conv_weight,
    a_log,
    out_gain,
    w_output,
    w_gate_up,
    w_down,
    cotangent,
):
    dp_size = lax.axis_size("dp")
    tensor_size = lax.axis_size("tensor")
    tensor_rank = lax.axis_index("tensor")
    rows_here, _, heads, _ = w_mixer_in.shape
    model_width = rows_here * dp_size
    wide = heads * WIDTH
    hidden_here = w_gate_up.shape[2]
    taps_here = conv_weight.shape[3]
    conv_at = 4 * wide + 2 * heads
    out_here = w_output.shape[0]
    own_rows = tokens.shape[1]

    def gather_rows(rows):
        if tensor_size == 2:
            return jnp.concatenate([rows, swap(rows)], axis=0)
        return lax.all_gather(rows, "tensor", axis=0, tiled=True)

    def sum_rows(product):
        if tensor_size == 2:
            return product[:own_rows] + swap(product[own_rows:].astype(bf16)).astype(f32)
        return lax.psum_scatter(
            product.astype(bf16), "tensor", scatter_dimension=0, tiled=True
        ).astype(f32)

    def in_order(rows):
        if tensor_size == 2:
            turned = jnp.concatenate([rows[own_rows:], rows[:own_rows]], axis=0)
            return jnp.where(tensor_rank == 0, rows, turned)
        return rows

    conv_block = jnp.pad(
        conv_weight.transpose(3, 0, 1, 2).reshape(taps_here, 12 * heads),
        ((0, rows_here - taps_here), (0, WIDTH - 14 * heads)),
    )
    mixer_pack = jnp.concatenate(
        [w_mixer_in.reshape(rows_here, -1), w_rates.reshape(rows_here, -1), conv_block], axis=1
    )
    mix_full = lax.all_gather(mixer_pack, "dp", axis=0, tiled=True)
    rest_pack = jnp.concatenate(
        [w_gate_up.reshape(rows_here, -1), w_output.T, w_down.T], axis=1
    )
    rest_full = lax.all_gather(rest_pack, "dp", axis=0, tiled=True)
    up_full = rest_full[:, : 2 * hidden_here]
    out_full = rest_full[:, 2 * hidden_here : 2 * hidden_here + out_here]
    down_full = rest_full[:, 2 * hidden_here + out_here :]
    conv_rows = (
        mix_full[:, conv_at : conv_at + 12 * heads]
        .reshape(dp_size, rows_here, 12 * heads)[:, :taps_here]
        .reshape(dp_size * taps_here, 12 * heads)
        .T.reshape(12, wide)
        .astype(f32)
    )
    segment = jnp.broadcast_to(segment_ids[0][:, None].astype(f32), (segment_ids.shape[1], WIDTH))
    neg_rate = jnp.pad(
        -jnp.exp(lax.dynamic_slice_in_dim(a_log, tensor_rank * heads, heads)), (0, WIDTH - heads)
    )[None]
    gain_row = out_gain[None]

    grad_local = cotangent[0]
    grad_all = gather_rows(grad_local)
    inputs = tokens[0].astype(f32)
    normed, first_back = jax.vjp(first_norm, inputs, norm_gains)
    normed_all = in_order(gather_rows(normed.astype(bf16)))
    projected = jnp.dot(normed_all, mix_full, preferred_element_type=f32)
    mixed, *saved = mixer_forward(projected, segment, conv_rows, neg_rate, gain_row)
    residual = inputs + sum_rows(contract_last(in_order(mixed), out_full))
    normed_ffn, second_back = jax.vjp(second_norm, residual, norm_gains)
    ffn_all = gather_rows(normed_ffn.astype(bf16))
    gate_up = jnp.dot(ffn_all, up_full, preferred_element_type=f32).reshape(-1, 2, hidden_here)
    hidden_raw, swish_back = jax.vjp(swish_product, gate_up)
    hidden = hidden_raw.astype(bf16)
    result = residual + sum_rows(contract_last(hidden, down_full))
    out_tokens = result.astype(bf16)[None]

    hidden_grad = jnp.dot(grad_all, down_full, preferred_element_type=f32)
    down_grad = contract_first(grad_all, hidden)
    (gate_up_grad,) = swish_back(hidden_grad)
    gate_up_low = gate_up_grad.reshape(-1, 2 * hidden_here).astype(bf16)
    up_grad = contract_first(ffn_all, gate_up_low)
    rest_grads = lax.psum_scatter(
        jnp.concatenate([up_grad.astype(bf16), down_grad.astype(bf16)], axis=1),
        "dp",
        scatter_dimension=0,
        tiled=True,
    )
    ffn_input_grad = sum_rows(contract_last(gate_up_low, up_full))
    residual_part, second_gains = second_back(ffn_input_grad)
    residual_grad = grad_local.astype(f32) + residual_part
    residual_all = in_order(gather_rows(residual_grad.astype(bf16)))
    mixed_grad = jnp.dot(residual_all, out_full, preferred_element_type=f32)
    out_grad = contract_first(residual_all, mixed)
    projection_grad, conv_grad, log_grad, gain_grad = mixer_backward(
        projected, segment, conv_rows, neg_rate, gain_row, mixed_grad, saved
    )
    mix_grad = contract_first(normed_all, projection_grad)
    conv_grad = jnp.pad(
        conv_grad.reshape(12 * heads, WIDTH).T.reshape(dp_size, taps_here, 12 * heads),
        ((0, 0), (0, rows_here - taps_here), (0, 0)),
    ).reshape(model_width, 12 * heads)
    mix_grads = lax.psum_scatter(
        jnp.concatenate(
            [
                mix_grad[:, :conv_at].astype(bf16),
                conv_grad.astype(bf16),
                jnp.zeros((model_width, WIDTH - 14 * heads), bf16),
                out_grad.astype(bf16),
            ],
            axis=1,
        ),
        "dp",
        scatter_dimension=0,
        tiled=True,
    ).astype(f32)
    mixer_input_grad = sum_rows(in_order(contract_last(projection_grad, mix_full)))
    input_part, first_gains = first_back(mixer_input_grad)
    input_grad = (residual_grad + input_part).astype(bf16)[None]
    log_full = lax.dynamic_update_slice_in_dim(
        jnp.zeros(a_log.shape, f32), log_grad[0, :heads], tensor_rank * heads, 0
    )
    small = jnp.concatenate(
        [(first_gains + second_gains).reshape(-1), gain_grad.reshape(-1), log_full]
    )
    small = lax.psum(small, ("dp", "tensor"))
    gain_count = 2 * model_width
    rest_grads = rest_grads.astype(f32)
    return (
        out_tokens,
        input_grad,
        small[:gain_count].reshape(2, model_width),
        mix_grads[:, : 4 * wide].reshape(w_mixer_in.shape),
        mix_grads[:, 4 * wide : conv_at].reshape(w_rates.shape),
        mix_grads[:taps_here, conv_at : conv_at + 12 * heads]
        .reshape(taps_here, 3, 4, heads)
        .transpose(1, 2, 3, 0),
        small[gain_count + WIDTH :],
        small[gain_count : gain_count + WIDTH],
        mix_grads[:, 4 * wide + WIDTH :].T,
        rest_grads[:, : 2 * hidden_here].reshape(w_gate_up.shape),
        rest_grads[:, 2 * hidden_here :].T,
    )


def solution(mesh):
    in_specs = (
        P("dp", "tensor", None),
        P("dp", None),
        P(),
        P("dp", None, "tensor", None),
        P("dp", None, "tensor"),
        P(None, None, "tensor", "dp"),
        P(),
        P(),
        P("tensor", "dp"),
        P("dp", None, "tensor"),
        P("tensor", "dp"),
        P("dp", "tensor", None),
    )
    out_specs = (
        P("dp", "tensor", None),
        P("dp", "tensor", None),
        P(),
        P("dp", None, "tensor", None),
        P("dp", None, "tensor"),
        P(None, None, "tensor", "dp"),
        P(),
        P(),
        P("tensor", "dp"),
        P("dp", None, "tensor"),
        P("tensor", "dp"),
    )
    return jax.shard_map(local, mesh=mesh, in_specs=in_specs, out_specs=out_specs, check_vma=False)
```

```python
import functools

import jax
import jax.numpy as jnp
from jax import lax
from jax.experimental import pallas as pl
from jax.experimental.pallas import tpu as pltpu
from jax.sharding import PartitionSpec as P

CHUNK = 128
WIDTH = 128
HALO = 8
COLUMN_TILE = 256
norm_eps = 1e-05
unit_eps = 1e-06
f32 = jnp.float32
bf16 = jnp.bfloat16

NN = ((1,), (0,))
NT = ((1,), (1,))
TN = ((0,), (0,))


def dot(left, right, dims):
    return lax.dot_general(
        left.astype(bf16), right.astype(bf16), (dims, ((), ())), preferred_element_type=f32
    )


def dot_exact(left, right, dims):
    return lax.dot_general(
        left, right, (dims, ((), ())), precision=lax.Precision.HIGHEST, preferred_element_type=f32
    )


def sigmoid(value):
    return 1.0 / (1.0 + jnp.exp(-value))


def softplus(value):
    return jnp.maximum(value, 0.0) + jnp.log(1.0 + jnp.exp(-jnp.abs(value)))


def shifted(rows, offset):
    return pltpu.roll(rows, offset, 0)[HALO:] if offset else rows[HALO:]


def conv_terms(rows, keeps):
    return [rows[HALO:]] + [
        jnp.where(keeps[offset], shifted(rows, offset), 0.0) for offset in range(1, 4)
    ]


def conv_sum(terms, conv_ref, part, lanes):
    total = None
    for offset in range(4):
        weight = conv_ref[pl.ds(part * 4 + 3 - offset, 1), lanes]
        term = weight * terms[offset]
        total = term if total is None else total + term
    return total


def lane_column(values, lane):
    return jnp.broadcast_to(values[:, lane : lane + 1], values.shape)


def grids():
    row = lax.broadcasted_iota(jnp.int32, (CHUNK, CHUNK), 0)
    col = lax.broadcasted_iota(jnp.int32, (CHUNK, CHUNK), 1)
    return row, col


def level_masks(row, col):
    masks = []
    shift = 0
    while (1 << shift) < CHUNK:
        near = (row >> (shift + 1)) == (col >> (shift + 1))
        apart = (row >> shift) != (col >> shift)
        masks.append(near & apart)
        shift += 1
    return masks


def unit_lower_inverses(lowers, row, col):
    masks = level_masks(row, col)
    identity = jnp.where(row == col, 1.0, 0.0).astype(f32)
    inverses = [identity - jnp.where(masks[0], lower, 0.0) for lower in lowers]
    for mask in masks[1:]:
        blocks = [jnp.where(mask, lower, 0.0) for lower in lowers]
        firsts = [dot(inverse, block, NN) for inverse, block in zip(inverses, blocks)]
        inverses = [inverse - dot(first, inverse, NN) for first, inverse in zip(firsts, inverses)]
    return inverses


def chunk_scales(heads, rates, neg_rate, seg, last_seen, row, col):
    steps = neg_rate * softplus(rates)
    lower_ones = jnp.where(row >= col, 1.0, 0.0).astype(f32)
    cumulative = dot_exact(lower_ones, steps, NN)
    cumulative_rows = cumulative.T
    betas = sigmoid(rates)
    seg_rows = seg.T
    same = seg == seg_rows
    within = same & (row >= col)
    strict = same & (row > col)
    carry = seg == last_seen
    ends = seg == seg[CHUNK - 1 :, :]
    scales = []
    for head in range(heads):
        cum = lane_column(cumulative, head)
        cum_row = cumulative_rows[head : head + 1, :]
        gap = jnp.exp(jnp.minimum(cum - cum_row, 0.0))
        last = cum[CHUNK - 1 :, :]
        scales.append(
            dict(
                beta=lane_column(betas, heads + head),
                within=jnp.where(within, gap, 0.0),
                strict=jnp.where(strict, gap, 0.0),
                start=jnp.where(carry, jnp.exp(cum), 0.0),
                end=jnp.where(ends, jnp.exp(jnp.minimum(last - cum, 0.0)), 0.0),
                keep=jnp.where(carry[CHUNK - 1 :, :], jnp.exp(last), 0.0),
            )
        )
    return scales, steps, betas


def forward_kernel(
    heads, proj_ref, seg_ref, conv_ref, rate_ref, gain_ref,
    mixed_ref, inverse_ref, w_ref, pseudo_ref, out_ref, state_ref,
    state, halo, seg_halo,
):
    step = pl.program_id(0)

    @pl.when(step == 0)
    def _():
        state[...] = jnp.zeros_like(state)
        halo[...] = jnp.zeros_like(halo)
        seg_halo[...] = jnp.full_like(seg_halo, -1.0)

    row, col = grids()
    seg = seg_ref[...]
    seg_rows = jnp.concatenate([seg_halo[...], seg], axis=0)
    keeps = [None] + [shifted(seg_rows, offset) == seg for offset in range(1, 4)]
    last_seen = seg_halo[HALO - 1 :, :]
    wide = heads * WIDTH
    rates = proj_ref[:, 4 * wide : 4 * wide + WIDTH]
    scales, _, _ = chunk_scales(heads, rates, rate_ref[...], seg, last_seen, row, col)

    queries, keys, values = [], [], []
    for head in range(heads):
        for part, into in ((0, queries), (1, keys), (2, values)):
            at = part * wide + head * WIDTH
            lanes = slice(at, at + WIDTH)
            rows = jnp.concatenate([halo[:, lanes], proj_ref[:, lanes]], axis=0)
            terms = conv_terms(rows, keeps)
            total = conv_sum(terms, conv_ref, part, slice(head * WIDTH, (head + 1) * WIDTH))
            into.append(total * sigmoid(total))
    for head in range(heads):
        query, key = queries[head], keys[head]
        queries[head] = query * (
            lax.rsqrt(jnp.sum(query * query, axis=-1, keepdims=True) + unit_eps) * WIDTH**-0.5
        )
        keys[head] = key * lax.rsqrt(jnp.sum(key * key, axis=-1, keepdims=True) + unit_eps)
    halo[...] = proj_ref[CHUNK - HALO :, : 3 * wide]
    seg_halo[...] = seg[CHUNK - HALO :, :]

    lowers, scores = [], []
    for head in range(heads):
        scale = scales[head]
        both = dot(jnp.concatenate([keys[head], queries[head]], axis=0), keys[head], NT)
        lowers.append(both[:CHUNK] * scale["strict"] * scale["beta"])
        scores.append(both[CHUNK:] * scale["within"])
    inverses = unit_lower_inverses(lowers, row, col)
    for head in range(heads):
        scale = scales[head]
        lanes = slice(head * WIDTH, (head + 1) * WIDTH)
        inverse = inverses[head].astype(bf16)
        inverse_ref[:, lanes] = inverse
        memory = state[head]
        state_ref[0, head] = memory.astype(state_ref.dtype)
        target = jnp.concatenate(
            [scale["beta"] * values[head], scale["beta"] * scale["start"] * keys[head]], axis=1
        )
        solved = dot(inverse, target, NN)
        carried = solved[:, WIDTH:]
        w_ref[:, lanes] = carried.astype(bf16)
        read = dot(
            jnp.concatenate([carried, scale["start"] * queries[head]], axis=0), memory, NN
        )
        pseudo = solved[:, :WIDTH] - read[:CHUNK]
        pseudo_ref[:, lanes] = pseudo.astype(bf16)
        output = dot(scores[head], pseudo, NN) + read[CHUNK:]
        out_ref[:, lanes] = output
        state[head] = scale["keep"] * memory + dot(scale["end"] * keys[head], pseudo, TN)
        gate = proj_ref[:, 3 * wide + head * WIDTH : 3 * wide + (head + 1) * WIDTH]
        unit = output * lax.rsqrt(jnp.mean(output * output, axis=-1, keepdims=True) + norm_eps)
        mixed_ref[:, lanes] = (unit * gain_ref[...] * gate * sigmoid(gate)).astype(bf16)


def backward_kernel(
    heads, proj_ref, seg_ref, seg_before_ref, before_ref, conv_ref, rate_ref, gain_ref, grad_ref,
    inverse_ref, w_ref, pseudo_ref, out_ref, state_ref,
    dproj_ref, dconv_ref, drate_ref, dgain_ref,
    dstate, carry_halo,
):
    step = pl.program_id(0)
    first = step == pl.num_programs(0) - 1

    @pl.when(step == 0)
    def _():
        dstate[...] = jnp.zeros_like(dstate)
        carry_halo[...] = jnp.zeros_like(carry_halo)
        dconv_ref[...] = jnp.zeros_like(dconv_ref)
        drate_ref[...] = jnp.zeros_like(drate_ref)
        dgain_ref[...] = jnp.zeros_like(dgain_ref)

    row, col = grids()
    seg = seg_ref[...]
    seg_before = jnp.where(first, -1.0, seg_before_ref[...])
    seg_rows = jnp.concatenate([seg_before, seg], axis=0)
    keeps = [None] + [shifted(seg_rows, offset) == seg for offset in range(1, 4)]
    last_seen = seg_before[HALO - 1 :, :]
    wide = heads * WIDTH
    rates = proj_ref[:, 4 * wide : 4 * wide + WIDTH]
    neg_rate = rate_ref[...]
    scales, steps, betas = chunk_scales(heads, rates, neg_rate, seg, last_seen, row, col)

    def rows_of(part, head):
        at = part * wide + head * WIDTH
        lanes = slice(at, at + WIDTH)
        return jnp.concatenate([before_ref[:, lanes], proj_ref[:, lanes]], axis=0)

    def signal(part, head):
        terms = conv_terms(rows_of(part, head), keeps)
        total = conv_sum(terms, conv_ref, part, slice(head * WIDTH, (head + 1) * WIDTH))
        gate = sigmoid(total)
        return terms, total, gate

    def signal_back(part, head, terms, total, gate, grad):
        grad = grad * (gate * (1.0 + total * (1.0 - gate)))
        lanes = slice(head * WIDTH, (head + 1) * WIDTH)
        spread = None
        for offset in range(4):
            tap = pl.ds(part * 4 + 3 - offset, 1)
            dconv_ref[tap, lanes] += jnp.sum(grad * terms[offset], axis=0, keepdims=True)
            back = conv_ref[tap, lanes] * grad
            if offset:
                back = jnp.where(keeps[offset], back, 0.0)
            back = jnp.concatenate([jnp.zeros((HALO, WIDTH), f32), back], axis=0)
            if offset:
                back = pltpu.roll(back, CHUNK + HALO - offset, 0)
            spread = back if spread is None else spread + back
        at = part * wide + head * WIDTH
        lanes = slice(at, at + WIDTH)
        tail = jnp.concatenate(
            [jnp.zeros((CHUNK - HALO, WIDTH), f32), carry_halo[:, lanes]], axis=0
        )
        dproj_ref[:, lanes] = (spread[HALO:] + tail).astype(bf16)
        carry_halo[:, lanes] = spread[:HALO]

    lane = col
    cum_columns = jnp.zeros((CHUNK, WIDTH), f32)
    cum_rows = jnp.zeros((CHUNK, CHUNK), f32)
    dbeta_columns = jnp.zeros((CHUNK, WIDTH), f32)
    dgain = jnp.zeros((1, WIDTH), f32)
    for head in range(heads):
        scale = scales[head]
        lanes = slice(head * WIDTH, (head + 1) * WIDTH)
        beta, start, end, keep = scale["beta"], scale["start"], scale["end"], scale["keep"]
        q_terms, q_total, q_gate = signal(0, head)
        k_terms, k_total, k_gate = signal(1, head)
        v_terms, v_total, v_gate = signal(2, head)
        q_act, k_act, value = q_total * q_gate, k_total * k_gate, v_total * v_gate
        q_norm = lax.rsqrt(jnp.sum(q_act * q_act, axis=-1, keepdims=True) + unit_eps)
        k_norm = lax.rsqrt(jnp.sum(k_act * k_act, axis=-1, keepdims=True) + unit_eps)
        q_unit, key = q_act * q_norm, k_act * k_norm
        query = q_unit * WIDTH**-0.5

        gain = gain_ref[...]
        gate_at = slice(3 * wide + head * WIDTH, 3 * wide + (head + 1) * WIDTH)
        gate = proj_ref[:, gate_at]
        gate_s = sigmoid(gate)
        gate_act = gate * gate_s
        grad = grad_ref[:, lanes].astype(f32)
        output = out_ref[:, lanes]
        inv_rms = lax.rsqrt(jnp.mean(output * output, axis=-1, keepdims=True) + norm_eps)
        unit = output * inv_rms
        grad_unit = grad * unit
        dgain = dgain + jnp.sum(grad_unit * gate_act, axis=0, keepdims=True)
        dproj_ref[:, gate_at] = (
            grad_unit * gain * (gate_s * (1.0 + gate * (1.0 - gate_s)))
        ).astype(bf16)
        dunit = grad * (gain * gate_act)
        dout = inv_rms * (dunit - unit * jnp.mean(dunit * unit, axis=-1, keepdims=True))

        both = dot(jnp.concatenate([key, query], axis=0), key, NT)
        lower_raw = both[:CHUNK] * scale["strict"]
        lower = lower_raw * beta
        scores = both[CHUNK:] * scale["within"]
        inverse = inverse_ref[:, lanes]
        pseudo = pseudo_ref[:, lanes]
        memory = state_ref[0, head]
        dmemory = dstate[head]

        dpseudo = dot(scores, dout, TN) + dot(end * key, dmemory, NN)
        start_query = start * query
        dstate[head] = keep * dmemory + dot(
            jnp.concatenate([start_query.astype(bf16), -w_ref[:, lanes]], axis=0),
            jnp.concatenate([dout.astype(bf16), dpseudo.astype(bf16)], axis=0),
            TN,
        )
        solved = dot(inverse, dpseudo, TN)
        reads = dot(jnp.concatenate([dout, solved], axis=0), memory, NT)
        dquery_start = start * reads[:CHUNK]
        dkey_start = -start * reads[CHUNK:]
        by_pseudo = dot(jnp.concatenate([dout, solved], axis=0), pseudo, NT)
        dscores = by_pseudo[:CHUNK]
        dlower = -by_pseudo[CHUNK:]
        dkey_end = end * dot(pseudo, dmemory, NT)

        dbeta = jnp.sum(
            solved * value + dkey_start * key + dlower * lower_raw, axis=-1, keepdims=True
        )
        pair = dscores * scores + dlower * lower
        end_terms = dkey_end * key
        dcum = jnp.sum(
            pair + dquery_start * query + (dkey_start * key) * beta - end_terms,
            axis=-1,
            keepdims=True,
        )
        last_total = jnp.sum(
            jnp.sum(end_terms, axis=0, keepdims=True)
            + keep * jnp.sum(memory * dmemory, axis=0, keepdims=True),
            axis=-1,
            keepdims=True,
        )
        dcum = dcum + jnp.where(row[:, :1] == CHUNK - 1, last_total, 0.0)
        cum_columns = cum_columns + jnp.where(lane == head, dcum, 0.0)
        dbeta_columns = dbeta_columns + jnp.where(lane == heads + head, dbeta, 0.0)
        cum_rows = cum_rows + jnp.where(row == head, jnp.sum(pair, axis=0, keepdims=True), 0.0)

        near = (dlower * (scale["strict"] * beta)).astype(bf16)
        far = (dscores * scale["within"]).astype(bf16)
        toward = dot(jnp.concatenate([near, far], axis=0), key, NN)
        dkey = (
            toward[:CHUNK]
            + dot(
                jnp.concatenate([near, far], axis=0),
                jnp.concatenate([key, query], axis=0),
                TN,
            )
            + beta * dkey_start
            + dkey_end
        )
        dquery = (toward[CHUNK:] + dquery_start) * WIDTH**-0.5
        dvalue = beta * solved
        dq_act = q_norm * (dquery - q_unit * jnp.sum(q_unit * dquery, axis=-1, keepdims=True))
        dk_act = k_norm * (dkey - key * jnp.sum(key * dkey, axis=-1, keepdims=True))
        signal_back(0, head, q_terms, q_total, q_gate, dq_act)
        signal_back(1, head, k_terms, k_total, k_gate, dk_act)
        signal_back(2, head, v_terms, v_total, v_gate, dvalue)

    upper_ones = jnp.where(row <= col, 1.0, 0.0).astype(f32)
    dsteps = dot_exact(upper_ones, cum_columns - cum_rows.T, NN)
    drate_ref[...] += jnp.sum(dsteps * steps, axis=0, keepdims=True)
    dgain_ref[...] += dgain
    dlogits = dsteps * neg_rate * betas + dbeta_columns * betas * (1.0 - betas)
    dproj_ref[:, 4 * wide : 4 * wide + WIDTH] = jnp.where(
        lane < 2 * heads, dlogits, 0.0
    ).astype(bf16)


def mixer_forward(proj, seg_wide, conv_rows, neg_rate, gain):
    length, width = proj.shape
    heads = (width - WIDTH) // (4 * WIDTH)
    wide = heads * WIDTH
    count = length // CHUNK
    by_chunk = lambda cols: pl.BlockSpec((CHUNK, cols), lambda i: (i, 0))
    whole = lambda rows, cols: pl.BlockSpec((rows, cols), lambda i: (0, 0))
    return pl.pallas_call(
        functools.partial(forward_kernel, heads),
        grid=(count,),
        in_specs=[
            by_chunk(width), by_chunk(WIDTH), whole(12, wide), whole(1, WIDTH), whole(1, WIDTH),
        ],
        out_specs=[
            by_chunk(wide), by_chunk(wide), by_chunk(wide), by_chunk(wide), by_chunk(wide),
            pl.BlockSpec((1, heads, WIDTH, WIDTH), lambda i: (i, 0, 0, 0)),
        ],
        out_shape=[
            jax.ShapeDtypeStruct((length, wide), bf16),
            jax.ShapeDtypeStruct((length, wide), bf16),
            jax.ShapeDtypeStruct((length, wide), bf16),
            jax.ShapeDtypeStruct((length, wide), bf16),
            jax.ShapeDtypeStruct((length, wide), f32),
            jax.ShapeDtypeStruct((count, heads, WIDTH, WIDTH), f32),
        ],
        scratch_shapes=[
            pltpu.VMEM((heads, WIDTH, WIDTH), f32),
            pltpu.VMEM((HALO, 3 * wide), f32),
            pltpu.VMEM((HALO, WIDTH), f32),
        ],
        compiler_params=pltpu.CompilerParams(vmem_limit_bytes=48 * 1024 * 1024),
        name="mixer_forward",
    )(proj, seg_wide, conv_rows, neg_rate, gain)


def mixer_backward(proj, seg_wide, conv_rows, neg_rate, gain, grad, saved):
    length, width = proj.shape
    heads = (width - WIDTH) // (4 * WIDTH)
    wide = heads * WIDTH
    count = length // CHUNK
    back = lambda i: count - 1 - i
    by_chunk = lambda cols: pl.BlockSpec((CHUNK, cols), lambda i: (back(i), 0))
    before = lambda cols: pl.BlockSpec(
        (HALO, cols), lambda i: (jnp.maximum(back(i) * (CHUNK // HALO) - 1, 0), 0)
    )
    whole = lambda rows, cols: pl.BlockSpec((rows, cols), lambda i: (0, 0))
    return pl.pallas_call(
        functools.partial(backward_kernel, heads),
        grid=(count,),
        in_specs=[
            by_chunk(width), by_chunk(WIDTH), before(WIDTH), before(3 * wide),
            whole(12, wide), whole(1, WIDTH), whole(1, WIDTH),
            by_chunk(wide), by_chunk(wide), by_chunk(wide), by_chunk(wide), by_chunk(wide),
            pl.BlockSpec((1, heads, WIDTH, WIDTH), lambda i: (back(i), 0, 0, 0)),
        ],
        out_specs=[by_chunk(width), whole(12, wide), whole(1, WIDTH), whole(1, WIDTH)],
        out_shape=[
            jax.ShapeDtypeStruct((length, width), bf16),
            jax.ShapeDtypeStruct((12, wide), f32),
            jax.ShapeDtypeStruct((1, WIDTH), f32),
            jax.ShapeDtypeStruct((1, WIDTH), f32),
        ],
        scratch_shapes=[
            pltpu.VMEM((heads, WIDTH, WIDTH), f32),
            pltpu.VMEM((HALO, 3 * wide), f32),
        ],
        compiler_params=pltpu.CompilerParams(vmem_limit_bytes=48 * 1024 * 1024),
        name="mixer_backward",
    )(proj, seg_wide, seg_wide, proj, conv_rows, neg_rate, gain, grad, *saved)


def project_kernel(x_ref, w_ref, out_ref):
    out_ref[...] = dot(x_ref[...], w_ref[...], NN)


def project(x, packed, columns):
    rows, model = x.shape
    return pl.pallas_call(
        project_kernel,
        grid=(pl.cdiv(columns, COLUMN_TILE),),
        in_specs=[
            pl.BlockSpec((rows, model), lambda i: (0, 0)),
            pl.BlockSpec((model, COLUMN_TILE), lambda i: (0, i)),
        ],
        out_specs=pl.BlockSpec((rows, COLUMN_TILE), lambda i: (0, i)),
        out_shape=jax.ShapeDtypeStruct((rows, columns), f32),
        compiler_params=pltpu.CompilerParams(vmem_limit_bytes=40 * 1024 * 1024),
        cost_estimate=pl.CostEstimate(
            flops=2 * rows * model * columns,
            bytes_accessed=2 * model * (rows + columns) + 4 * rows * columns,
            transcendentals=0,
        ),
        name="project",
    )(x, packed)


def ffn_kernel(tiles, x_ref, dy_ref, w_ref, h_ref, g_ref, y_ref, dx_ref, y_sum, dx_sum):
    step = pl.program_id(0)

    @pl.when(step == 0)
    def _():
        y_sum[...] = jnp.zeros_like(y_sum)
        dx_sum[...] = jnp.zeros_like(dx_sum)

    def units(size):
        gate_up = dot(x_ref[...], w_ref[:, : 2 * size], NN)
        grad = dot(dy_ref[...], w_ref[:, 2 * size : 3 * size], NN)
        gate, up = gate_up[:, :size], gate_up[:, size:]
        gate_s = sigmoid(gate)
        act = gate * gate_s
        h_ref[:, :size] = (act * up).astype(bf16)
        g_ref[:, :size] = (grad * up * (gate_s + act * (1.0 - gate_s))).astype(bf16)
        g_ref[:, size : 2 * size] = (grad * act).astype(bf16)
        y_sum[...] += dot(h_ref[:, :size], w_ref[:, 2 * size : 3 * size], NT)
        dx_sum[...] += dot(g_ref[:, : 2 * size], w_ref[:, : 2 * size], NT)

    per_tile(tiles, step, units)

    @pl.when(step == len(tiles) - 1)
    def _():
        y_ref[...] = y_sum[...].astype(bf16)
        dx_ref[...] = dx_sum[...].astype(bf16)


def per_tile(tiles, step, units):
    if tiles[0] == tiles[-1]:
        units(tiles[0])
        return

    @pl.when(step < len(tiles) - 1)
    def _():
        units(tiles[0])

    @pl.when(step == len(tiles) - 1)
    def _():
        units(tiles[-1])


def ffn(x, dy, packed, tiles):
    rows, model = x.shape
    hidden = sum(tiles)
    whole = pl.BlockSpec((rows, model), lambda i: (0, 0))
    return pl.pallas_call(
        functools.partial(ffn_kernel, tiles),
        grid=(len(tiles),),
        in_specs=[whole, whole, pl.BlockSpec((model, 3 * tiles[0]), lambda i: (0, i))],
        out_specs=[
            pl.BlockSpec((rows, tiles[0]), lambda i: (0, i)),
            pl.BlockSpec((rows, 2 * tiles[0]), lambda i: (0, i)),
            whole,
            whole,
        ],
        out_shape=[
            jax.ShapeDtypeStruct((rows, hidden), bf16),
            jax.ShapeDtypeStruct((rows, 2 * hidden), bf16),
            jax.ShapeDtypeStruct((rows, model), bf16),
            jax.ShapeDtypeStruct((rows, model), bf16),
        ],
        scratch_shapes=[pltpu.VMEM((rows, model), f32), pltpu.VMEM((rows, model), f32)],
        compiler_params=pltpu.CompilerParams(vmem_limit_bytes=48 * 1024 * 1024),
        cost_estimate=pl.CostEstimate(
            flops=12 * rows * model * hidden,
            bytes_accessed=2 * (3 * model * hidden + rows * (4 * model + 3 * hidden)),
            transcendentals=rows * hidden,
        ),
        name="ffn",
    )(x, dy, packed)


def ffn_grads_kernel(tiles, *refs):
    *inputs, out_ref, x_turned, dy_turned = refs
    xs, dys, hs, gs = (inputs[at : at + len(inputs) // 4] for at in range(0, len(inputs), len(inputs) // 4))
    step = pl.program_id(0)
    rows = xs[0].shape[0]

    @pl.when(step == 0)
    def _():
        for at, (x_ref, dy_ref) in enumerate(zip(xs, dys)):
            x_turned[:, at * rows : (at + 1) * rows] = x_ref[...].T
            dy_turned[:, at * rows : (at + 1) * rows] = dy_ref[...].T

    def units(size):
        up_grad, down_grad = None, None
        for at, (h_ref, g_ref) in enumerate(zip(hs, gs)):
            lanes = slice(at * rows, (at + 1) * rows)
            up_term = dot(x_turned[:, lanes], g_ref[:, : 2 * size], NN)
            down_term = dot(dy_turned[:, lanes], h_ref[:, :size], NN)
            up_grad = up_term if at == 0 else up_grad + up_term
            down_grad = down_term if at == 0 else down_grad + down_term
        out_ref[:, : 2 * size] = up_grad.astype(bf16)
        out_ref[:, 2 * size : 3 * size] = down_grad.astype(bf16)

    per_tile(tiles, step, units)


def ffn_grads(xs, dys, hs, gs, tiles):
    rows, model = xs[0].shape
    hidden = sum(tiles)
    whole = pl.BlockSpec((rows, model), lambda i: (0, 0))
    total = rows * len(xs)
    return pl.pallas_call(
        functools.partial(ffn_grads_kernel, tiles),
        grid=(len(tiles),),
        in_specs=[whole] * (2 * len(xs))
        + [pl.BlockSpec((rows, tiles[0]), lambda i: (0, i))] * len(xs)
        + [pl.BlockSpec((rows, 2 * tiles[0]), lambda i: (0, i))] * len(xs),
        out_specs=pl.BlockSpec((model, 3 * tiles[0]), lambda i: (0, i)),
        out_shape=jax.ShapeDtypeStruct((model, 3 * hidden), bf16),
        scratch_shapes=[pltpu.VMEM((model, total), bf16), pltpu.VMEM((model, total), bf16)],
        compiler_params=pltpu.CompilerParams(vmem_limit_bytes=48 * 1024 * 1024),
        cost_estimate=pl.CostEstimate(
            flops=6 * total * model * hidden,
            bytes_accessed=2 * (3 * model * hidden + total * (2 * model + 3 * hidden)),
            transcendentals=0,
        ),
        name="ffn_grads",
    )(*xs, *dys, *hs, *gs)


def mixer_grads_kernel(
    tile, main_steps, normed_ref, residual_ref, dproj_ref, mixed_ref, conv_ref, out_ref, turned
):
    step = pl.program_id(0)
    last = pl.num_programs(0) - 1

    @pl.when(step == 0)
    def _():
        turned[...] = normed_ref[...].T

    @pl.when(step < main_steps)
    def _():
        out_ref[...] = dot(turned[...], dproj_ref[...], NN).astype(bf16)

    @pl.when((step >= main_steps) & (step < last))
    def _():
        out_ref[...] = dot(residual_ref[...], mixed_ref[...], TN).astype(bf16)

    @pl.when(step == last)
    def _():
        grads = dot(turned[...], dproj_ref[:, :WIDTH], NN) + conv_ref[...]
        out_ref[:, :WIDTH] = grads.astype(bf16)


def mixer_grads(normed, residual, dproj, mixed, conv_block):
    rows, model = normed.shape
    wide = mixed.shape[1]
    tile = 2 * WIDTH if wide % (2 * WIDTH) == 0 else WIDTH
    main_steps = 4 * wide // tile
    out_steps = wide // tile
    columns = 5 * wide + WIDTH
    whole = pl.BlockSpec((rows, model), lambda i: (0, 0))
    return pl.pallas_call(
        functools.partial(mixer_grads_kernel, tile, main_steps),
        grid=(main_steps + out_steps + 1,),
        in_specs=[
            whole,
            whole,
            pl.BlockSpec((rows, tile), lambda i: (0, jnp.minimum(i, main_steps))),
            pl.BlockSpec((rows, tile), lambda i: (0, jnp.clip(i - main_steps, 0, out_steps - 1))),
            pl.BlockSpec((model, WIDTH), lambda i: (0, 0)),
        ],
        out_specs=pl.BlockSpec((model, tile), lambda i: (0, i)),
        out_shape=jax.ShapeDtypeStruct((model, columns), bf16),
        scratch_shapes=[pltpu.VMEM((model, rows), bf16)],
        compiler_params=pltpu.CompilerParams(vmem_limit_bytes=40 * 1024 * 1024),
        cost_estimate=pl.CostEstimate(
            flops=2 * rows * model * columns,
            bytes_accessed=2 * (2 * rows * model + (rows + model) * columns),
            transcendentals=0,
        ),
        name="mixer_grads",
    )(normed, residual, dproj, mixed, conv_block)


def rms_norm(values, scales):
    return values * lax.rsqrt(jnp.mean(values * values, axis=-1, keepdims=True) + norm_eps) * scales


def first_norm(values, gains):
    return rms_norm(values, gains[0])


def second_norm(values, gains):
    return rms_norm(values, gains[1])


def contract_last(operand, other):
    return lax.dot_general(
        operand, other, (((1,), (1,)), ((), ())), preferred_element_type=jnp.float32
    )


def contract_first(operand, other):
    return lax.dot_general(
        operand, other, (((0,), (0,)), ((), ())), preferred_element_type=jnp.float32
    )


def swap(rows):
    return lax.ppermute(rows, "tensor", [(0, 1), (1, 0)])


def sum_over(values, axis):
    size = lax.axis_size(axis)
    if size & (size - 1):
        return lax.psum(values, axis)
    bit = 1
    while bit < size:
        values = values + lax.ppermute(values, axis, [(i, i ^ bit) for i in range(size)])
        bit *= 2
    return values


def hidden_tiles(hidden):
    if hidden % WIDTH:
        return (hidden,)
    return (2 * WIDTH,) * (hidden // (2 * WIDTH)) + (WIDTH,) * (hidden // WIDTH % 2)


def pack_tiles(gate, up, down, tiles):
    blocks = []
    at = 0
    for size in tiles:
        blocks += [part[:, at : at + size] for part in (gate, up, down)]
        at += size
    return jnp.concatenate(blocks, axis=1)


def unpack_tiles(packed, tiles):
    parts = ([], [], [])
    at = 0
    for size in tiles:
        for part in parts:
            part.append(packed[:, at : at + size])
            at += size
    return [jnp.concatenate(part, axis=1) for part in parts]


def ffn_plain(x, dy, packed, tiles):
    gate_w, up_w, down_w = unpack_tiles(packed, tiles)
    gate = jnp.dot(x, gate_w, preferred_element_type=f32)
    up = jnp.dot(x, up_w, preferred_element_type=f32)
    grad = jnp.dot(dy, down_w, preferred_element_type=f32)
    gate_s = sigmoid(gate)
    act = gate * gate_s
    hidden = (act * up).astype(bf16)
    gate_grad = (grad * up * (gate_s + act * (1.0 - gate_s))).astype(bf16)
    up_grad = (grad * act).astype(bf16)
    share = contract_last(hidden, down_w).astype(bf16)
    dx = (contract_last(gate_grad, gate_w) + contract_last(up_grad, up_w)).astype(bf16)
    return hidden, jnp.concatenate([gate_grad, up_grad], axis=1), share, dx


def ffn_grads_plain(x, dy, hidden, grads, tiles):
    size = hidden.shape[1]
    return pack_tiles(
        contract_first(x, grads[:, :size]).astype(bf16),
        contract_first(x, grads[:, size:]).astype(bf16),
        contract_first(dy, hidden).astype(bf16),
        tiles,
    )


def local(
    tokens,
    segment_ids,
    norm_gains,
    w_mixer_in,
    w_rates,
    conv_weight,
    a_log,
    out_gain,
    w_output,
    w_gate_up,
    w_down,
    cotangent,
):
    dp_size = lax.axis_size("dp")
    pair = lax.axis_size("tensor") == 2
    tensor_rank = lax.axis_index("tensor")
    rows_here, _, heads, _ = w_mixer_in.shape
    model_width = rows_here * dp_size
    wide = heads * WIDTH
    hidden_here = w_gate_up.shape[2]
    tiles = hidden_tiles(hidden_here)
    kernels = hidden_here % WIDTH == 0
    taps_here = conv_weight.shape[3]
    own_rows = tokens.shape[1]
    projected_width = 4 * wide + WIDTH

    def gather_rows(rows):
        return lax.all_gather(rows, "tensor", axis=0, tiled=True)

    def scatter_rows(product):
        return lax.psum_scatter(product.astype(bf16), "tensor", scatter_dimension=0, tiled=True)

    def in_order(own, other):
        first = tensor_rank == 0
        return jnp.concatenate([jnp.where(first, own, other), jnp.where(first, other, own)], axis=0)

    def own_and_other(rows):
        own = lax.dynamic_slice_in_dim(rows, tensor_rank * own_rows, own_rows)
        return own, lax.dynamic_slice_in_dim(rows, (1 - tensor_rank) * own_rows, own_rows)

    conv_block = jnp.pad(
        conv_weight.transpose(3, 0, 1, 2).reshape(taps_here, 12 * heads),
        ((0, rows_here - taps_here), (0, WIDTH - 14 * heads)),
    )
    mixer_pack = jnp.concatenate(
        [
            w_mixer_in.reshape(rows_here, -1),
            w_rates.reshape(rows_here, -1),
            conv_block,
            w_output.T,
        ],
        axis=1,
    )
    mix_full = lax.all_gather(mixer_pack, "dp", axis=0, tiled=True)
    ffn_pack = pack_tiles(w_gate_up[:, 0], w_gate_up[:, 1], w_down.T, tiles)
    ffn_full = lax.all_gather(ffn_pack, "dp", axis=0, tiled=True)
    out_mine = mix_full[:, projected_width:]
    conv_at = 4 * wide + 2 * heads
    conv_rows = (
        mix_full[:, conv_at : conv_at + 12 * heads]
        .reshape(dp_size, rows_here, 12 * heads)[:, :taps_here]
        .reshape(dp_size * taps_here, 12 * heads)
        .T.reshape(12, wide)
        .astype(f32)
    )
    segment = jnp.broadcast_to(segment_ids[0][:, None].astype(f32), (segment_ids.shape[1], WIDTH))
    neg_rate = jnp.pad(
        -jnp.exp(lax.dynamic_slice_in_dim(a_log, tensor_rank * heads, heads)), (0, WIDTH - heads)
    )[None]
    gain_row = out_gain[None]

    grad_own = cotangent[0]
    inputs = tokens[0].astype(f32)
    normed, first_back = jax.vjp(first_norm, inputs, norm_gains)
    normed = normed.astype(bf16)
    if pair:
        normed_all = in_order(normed, swap(normed))
        grad_other = swap(grad_own)
        out_other = swap(out_mine)
    else:
        normed_all = gather_rows(normed)
    projected = project(normed_all, mix_full, projected_width)
    mixed, *saved = mixer_forward(projected, segment, conv_rows, neg_rate, gain_row)
    if pair:
        mixed_own, mixed_theirs = own_and_other(mixed)
        share = contract_last(mixed_own, out_mine) + contract_last(swap(mixed_theirs), out_other)
    else:
        share = scatter_rows(contract_last(mixed, out_mine)).astype(f32)
    residual = inputs + share
    normed_ffn, second_back = jax.vjp(second_norm, residual, norm_gains)
    normed_ffn = normed_ffn.astype(bf16)
    if pair:
        x_both = [normed_ffn, swap(normed_ffn)]
        dy_both = [grad_own, grad_other]
    else:
        x_both = [gather_rows(normed_ffn)]
        dy_both = [gather_rows(grad_own)]
    one_ffn = ffn if kernels else ffn_plain
    done = [one_ffn(x, dy, ffn_full, tiles) for x, dy in zip(x_both, dy_both)]
    h_both, g_both, y_both, dx_both = zip(*done)
    if pair:
        dx = dx_both[0].astype(f32) + swap(dx_both[1]).astype(f32)
        y_other = swap(y_both[1])
        y = y_both[0].astype(f32) + y_other.astype(f32)
    else:
        dx = scatter_rows(dx_both[0]).astype(f32)
        y = scatter_rows(y_both[0]).astype(f32)
    out_tokens = (residual + y).astype(bf16)[None]
    if kernels:
        ffn_sums = ffn_grads(x_both, dy_both, h_both, g_both, tiles)
    else:
        ffn_sums = ffn_grads_plain(x_both[0], dy_both[0], h_both[0], g_both[0], tiles)
    residual_part, second_gains = second_back(dx)
    residual_grad = grad_own.astype(f32) + residual_part
    residual_low = residual_grad.astype(bf16)
    if pair:
        grad_theirs = jnp.dot(residual_low, out_other, preferred_element_type=f32).astype(bf16)
        grad_mine = jnp.dot(residual_low, out_mine, preferred_element_type=f32).astype(bf16)
        mixed_grad = in_order(grad_mine, swap(grad_theirs))
    else:
        residual_all = gather_rows(residual_low)
        mixed_grad = jnp.dot(residual_all, out_mine, preferred_element_type=f32).astype(bf16)
    mixed_grad, ffn_sums = lax.optimization_barrier((mixed_grad, ffn_sums))
    ffn_owned = lax.psum_scatter(ffn_sums, "dp", scatter_dimension=0, tiled=True)
    if pair:
        residual_all = in_order(residual_low, swap(residual_low))
    projection_grad, conv_grad, log_grad, gain_grad = mixer_backward(
        projected, segment, conv_rows, neg_rate, gain_row, mixed_grad, saved
    )
    conv_grad = jnp.pad(
        conv_grad.reshape(12 * heads, WIDTH).T.reshape(dp_size, taps_here, 12 * heads),
        ((0, 0), (0, rows_here - taps_here), (2 * heads, WIDTH - 14 * heads)),
    ).reshape(model_width, WIDTH)
    mix_sums = mixer_grads(normed_all, residual_all, projection_grad, mixed, conv_grad)
    mix_sums, projection_grad = lax.optimization_barrier((mix_sums, projection_grad))
    mix_owned = lax.psum_scatter(mix_sums, "dp", scatter_dimension=0, tiled=True).astype(f32)
    mix_rows = mix_full[:, :projected_width]
    if pair:
        grad_here, grad_there = own_and_other(projection_grad)
        mixer_input_grad = swap(contract_last(grad_there, mix_rows).astype(bf16)).astype(f32)
        mixer_input_grad = mixer_input_grad + contract_last(grad_here, mix_rows)
    else:
        mixer_input_grad = scatter_rows(contract_last(projection_grad, mix_rows)).astype(f32)
    input_part, first_gains = first_back(mixer_input_grad)
    input_grad = (residual_grad + input_part).astype(bf16)[None]
    log_full = lax.dynamic_update_slice_in_dim(
        jnp.zeros(a_log.shape, f32), log_grad[0, :heads], tensor_rank * heads, 0
    )
    small = jnp.concatenate(
        [
            (first_gains + second_gains).reshape(-1, WIDTH),
            gain_grad,
            jnp.pad(log_full, (0, WIDTH - log_full.shape[0]))[None],
        ]
    )
    small = sum_over(sum_over(small, "dp"), "tensor")
    gain_rows = 2 * model_width // WIDTH
    gate_grad, up_grad, down_grad = unpack_tiles(ffn_owned, tiles)
    rates = mix_owned[:, 5 * wide :]
    return (
        out_tokens,
        input_grad,
        small[:gain_rows].reshape(2, model_width),
        mix_owned[:, : 4 * wide].reshape(w_mixer_in.shape),
        rates[:, : 2 * heads].reshape(w_rates.shape),
        rates[:taps_here, 2 * heads : 14 * heads]
        .reshape(taps_here, 3, 4, heads)
        .transpose(1, 2, 3, 0),
        small[gain_rows + 1, : a_log.shape[0]],
        small[gain_rows],
        mix_owned[:, 4 * wide : 5 * wide].T,
        jnp.stack([gate_grad, up_grad], axis=1).astype(f32),
        down_grad.T.astype(f32),
    )


def solution(mesh):
    in_specs = (
        P("dp", "tensor", None),
        P("dp", None),
        P(),
        P("dp", None, "tensor", None),
        P("dp", None, "tensor"),
        P(None, None, "tensor", "dp"),
        P(),
        P(),
        P("tensor", "dp"),
        P("dp", None, "tensor"),
        P("tensor", "dp"),
        P("dp", "tensor", None),
    )
    out_specs = (
        P("dp", "tensor", None),
        P("dp", "tensor", None),
        P(),
        P("dp", None, "tensor", None),
        P("dp", None, "tensor"),
        P(None, None, "tensor", "dp"),
        P(),
        P(),
        P("tensor", "dp"),
        P("dp", None, "tensor"),
        P("tensor", "dp"),
    )
    return jax.shard_map(local, mesh=mesh, in_specs=in_specs, out_specs=out_specs, check_vma=False)
```

```python
import functools

import jax
import jax.numpy as jnp
from jax import lax
from jax.experimental import pallas as pl
from jax.experimental.pallas import tpu as pltpu
from jax.sharding import PartitionSpec as P

CHUNK = 128
WIDTH = 128
HALO = 8
COLUMN_TILE = 256
norm_eps = 1e-05
unit_eps = 1e-06
f32 = jnp.float32
bf16 = jnp.bfloat16

NN = ((1,), (0,))
NT = ((1,), (1,))
TN = ((0,), (0,))


def dot(left, right, dims):
    return lax.dot_general(
        left.astype(bf16), right.astype(bf16), (dims, ((), ())), preferred_element_type=f32
    )


def dot_exact(left, right, dims):
    return lax.dot_general(
        left, right, (dims, ((), ())), precision=lax.Precision.HIGHEST, preferred_element_type=f32
    )


def sigmoid(value):
    return 1.0 / (1.0 + jnp.exp(-value))


def softplus(value):
    return jnp.maximum(value, 0.0) + jnp.log(1.0 + jnp.exp(-jnp.abs(value)))


def shifted(rows, offset):
    return pltpu.roll(rows, offset, 0)[HALO:] if offset else rows[HALO:]


def conv_terms(rows, keeps):
    return [rows[HALO:]] + [
        jnp.where(keeps[offset], shifted(rows, offset), 0.0) for offset in range(1, 4)
    ]


def conv_sum(terms, conv_ref, part, lanes):
    total = None
    for offset in range(4):
        weight = conv_ref[pl.ds(part * 4 + 3 - offset, 1), lanes]
        term = weight * terms[offset]
        total = term if total is None else total + term
    return total


def lane_column(values, lane):
    return jnp.broadcast_to(values[:, lane : lane + 1], values.shape)


def grids():
    row = lax.broadcasted_iota(jnp.int32, (CHUNK, CHUNK), 0)
    col = lax.broadcasted_iota(jnp.int32, (CHUNK, CHUNK), 1)
    return row, col


def level_masks(row, col):
    masks = []
    shift = 0
    while (1 << shift) < CHUNK:
        near = (row >> (shift + 1)) == (col >> (shift + 1))
        apart = (row >> shift) != (col >> shift)
        masks.append(near & apart)
        shift += 1
    return masks


def unit_lower_inverses(lowers, row, col):
    masks = level_masks(row, col)
    identity = jnp.where(row == col, 1.0, 0.0).astype(f32)
    inverses = [identity - jnp.where(masks[0], lower, 0.0) for lower in lowers]
    for mask in masks[1:]:
        blocks = [jnp.where(mask, lower, 0.0) for lower in lowers]
        firsts = [dot(inverse, block, NN) for inverse, block in zip(inverses, blocks)]
        inverses = [inverse - dot(first, inverse, NN) for first, inverse in zip(firsts, inverses)]
    return inverses


def chunk_scales(heads, rates, neg_rate, seg, last_seen, row, col):
    steps = neg_rate * softplus(rates)
    lower_ones = jnp.where(row >= col, 1.0, 0.0).astype(f32)
    cumulative = dot_exact(lower_ones, steps, NN)
    cumulative_rows = cumulative.T
    betas = sigmoid(rates)
    seg_rows = seg.T
    same = seg == seg_rows
    within = same & (row >= col)
    strict = same & (row > col)
    carry = seg == last_seen
    ends = seg == seg[CHUNK - 1 :, :]
    scales = []
    for head in range(heads):
        cum = lane_column(cumulative, head)
        cum_row = cumulative_rows[head : head + 1, :]
        gap = jnp.exp(jnp.minimum(cum - cum_row, 0.0))
        last = cum[CHUNK - 1 :, :]
        scales.append(
            dict(
                beta=lane_column(betas, heads + head),
                within=jnp.where(within, gap, 0.0),
                strict=jnp.where(strict, gap, 0.0),
                start=jnp.where(carry, jnp.exp(cum), 0.0),
                end=jnp.where(ends, jnp.exp(jnp.minimum(last - cum, 0.0)), 0.0),
                keep=jnp.where(carry[CHUNK - 1 :, :], jnp.exp(last), 0.0),
            )
        )
    return scales, steps, betas


def forward_kernel(
    heads, proj_ref, seg_ref, conv_ref, rate_ref, gain_ref,
    mixed_ref, inverse_ref, w_ref, pseudo_ref, out_ref, state_ref,
    state, halo, seg_halo,
):
    step = pl.program_id(0)

    @pl.when(step == 0)
    def _():
        state[...] = jnp.zeros_like(state)
        halo[...] = jnp.zeros_like(halo)
        seg_halo[...] = jnp.full_like(seg_halo, -1.0)

    row, col = grids()
    seg = seg_ref[...]
    seg_rows = jnp.concatenate([seg_halo[...], seg], axis=0)
    keeps = [None] + [shifted(seg_rows, offset) == seg for offset in range(1, 4)]
    last_seen = seg_halo[HALO - 1 :, :]
    wide = heads * WIDTH
    rates = proj_ref[:, 4 * wide : 4 * wide + WIDTH]
    scales, _, _ = chunk_scales(heads, rates, rate_ref[...], seg, last_seen, row, col)

    queries, keys, values = [], [], []
    for head in range(heads):
        for part, into in ((0, queries), (1, keys), (2, values)):
            at = part * wide + head * WIDTH
            lanes = slice(at, at + WIDTH)
            rows = jnp.concatenate([halo[:, lanes], proj_ref[:, lanes]], axis=0)
            terms = conv_terms(rows, keeps)
            total = conv_sum(terms, conv_ref, part, slice(head * WIDTH, (head + 1) * WIDTH))
            into.append(total * sigmoid(total))
    for head in range(heads):
        query, key = queries[head], keys[head]
        queries[head] = query * (
            lax.rsqrt(jnp.sum(query * query, axis=-1, keepdims=True) + unit_eps) * WIDTH**-0.5
        )
        keys[head] = key * lax.rsqrt(jnp.sum(key * key, axis=-1, keepdims=True) + unit_eps)
    halo[...] = proj_ref[CHUNK - HALO :, : 3 * wide]
    seg_halo[...] = seg[CHUNK - HALO :, :]

    lowers, scores = [], []
    for head in range(heads):
        scale = scales[head]
        both = dot(jnp.concatenate([keys[head], queries[head]], axis=0), keys[head], NT)
        lowers.append(both[:CHUNK] * scale["strict"] * scale["beta"])
        scores.append(both[CHUNK:] * scale["within"])
    inverses = unit_lower_inverses(lowers, row, col)
    for head in range(heads):
        scale = scales[head]
        lanes = slice(head * WIDTH, (head + 1) * WIDTH)
        inverse = inverses[head].astype(bf16)
        inverse_ref[:, lanes] = inverse
        memory = state[head]
        state_ref[0, head] = memory.astype(state_ref.dtype)
        target = jnp.concatenate(
            [scale["beta"] * values[head], scale["beta"] * scale["start"] * keys[head]], axis=1
        )
        solved = dot(inverse, target, NN)
        carried = solved[:, WIDTH:]
        w_ref[:, lanes] = carried.astype(bf16)
        read = dot(
            jnp.concatenate([carried, scale["start"] * queries[head]], axis=0), memory, NN
        )
        pseudo = solved[:, :WIDTH] - read[:CHUNK]
        pseudo_ref[:, lanes] = pseudo.astype(bf16)
        output = dot(scores[head], pseudo, NN) + read[CHUNK:]
        out_ref[:, lanes] = output
        state[head] = scale["keep"] * memory + dot(scale["end"] * keys[head], pseudo, TN)
        gate = proj_ref[:, 3 * wide + head * WIDTH : 3 * wide + (head + 1) * WIDTH]
        unit = output * lax.rsqrt(jnp.mean(output * output, axis=-1, keepdims=True) + norm_eps)
        mixed_ref[:, lanes] = (unit * gain_ref[...] * gate * sigmoid(gate)).astype(bf16)


def backward_kernel(
    heads, proj_ref, seg_ref, seg_before_ref, before_ref, conv_ref, rate_ref, gain_ref, grad_ref,
    inverse_ref, w_ref, pseudo_ref, out_ref, state_ref,
    dproj_ref, dconv_ref, drate_ref, dgain_ref,
    dstate, carry_halo,
):
    step = pl.program_id(0)
    first = step == pl.num_programs(0) - 1

    @pl.when(step == 0)
    def _():
        dstate[...] = jnp.zeros_like(dstate)
        carry_halo[...] = jnp.zeros_like(carry_halo)
        dconv_ref[...] = jnp.zeros_like(dconv_ref)
        drate_ref[...] = jnp.zeros_like(drate_ref)
        dgain_ref[...] = jnp.zeros_like(dgain_ref)

    row, col = grids()
    seg = seg_ref[...]
    seg_before = jnp.where(first, -1.0, seg_before_ref[...])
    seg_rows = jnp.concatenate([seg_before, seg], axis=0)
    keeps = [None] + [shifted(seg_rows, offset) == seg for offset in range(1, 4)]
    last_seen = seg_before[HALO - 1 :, :]
    wide = heads * WIDTH
    rates = proj_ref[:, 4 * wide : 4 * wide + WIDTH]
    neg_rate = rate_ref[...]
    scales, steps, betas = chunk_scales(heads, rates, neg_rate, seg, last_seen, row, col)

    def rows_of(part, head):
        at = part * wide + head * WIDTH
        lanes = slice(at, at + WIDTH)
        return jnp.concatenate([before_ref[:, lanes], proj_ref[:, lanes]], axis=0)

    def signal(part, head):
        terms = conv_terms(rows_of(part, head), keeps)
        total = conv_sum(terms, conv_ref, part, slice(head * WIDTH, (head + 1) * WIDTH))
        gate = sigmoid(total)
        return terms, total, gate

    def signal_back(part, head, terms, total, gate, grad):
        grad = grad * (gate * (1.0 + total * (1.0 - gate)))
        lanes = slice(head * WIDTH, (head + 1) * WIDTH)
        spread = None
        for offset in range(4):
            tap = pl.ds(part * 4 + 3 - offset, 1)
            dconv_ref[tap, lanes] += jnp.sum(grad * terms[offset], axis=0, keepdims=True)
            back = conv_ref[tap, lanes] * grad
            if offset:
                back = jnp.where(keeps[offset], back, 0.0)
            back = jnp.concatenate([jnp.zeros((HALO, WIDTH), f32), back], axis=0)
            if offset:
                back = pltpu.roll(back, CHUNK + HALO - offset, 0)
            spread = back if spread is None else spread + back
        at = part * wide + head * WIDTH
        lanes = slice(at, at + WIDTH)
        tail = jnp.concatenate(
            [jnp.zeros((CHUNK - HALO, WIDTH), f32), carry_halo[:, lanes]], axis=0
        )
        dproj_ref[:, lanes] = (spread[HALO:] + tail).astype(bf16)
        carry_halo[:, lanes] = spread[:HALO]

    lane = col
    cum_columns = jnp.zeros((CHUNK, WIDTH), f32)
    cum_rows = jnp.zeros((CHUNK, CHUNK), f32)
    dbeta_columns = jnp.zeros((CHUNK, WIDTH), f32)
    dgain = jnp.zeros((1, WIDTH), f32)
    for head in range(heads):
        scale = scales[head]
        lanes = slice(head * WIDTH, (head + 1) * WIDTH)
        beta, start, end, keep = scale["beta"], scale["start"], scale["end"], scale["keep"]
        q_terms, q_total, q_gate = signal(0, head)
        k_terms, k_total, k_gate = signal(1, head)
        v_terms, v_total, v_gate = signal(2, head)
        q_act, k_act, value = q_total * q_gate, k_total * k_gate, v_total * v_gate
        q_norm = lax.rsqrt(jnp.sum(q_act * q_act, axis=-1, keepdims=True) + unit_eps)
        k_norm = lax.rsqrt(jnp.sum(k_act * k_act, axis=-1, keepdims=True) + unit_eps)
        q_unit, key = q_act * q_norm, k_act * k_norm
        query = q_unit * WIDTH**-0.5

        gain = gain_ref[...]
        gate_at = slice(3 * wide + head * WIDTH, 3 * wide + (head + 1) * WIDTH)
        gate = proj_ref[:, gate_at]
        gate_s = sigmoid(gate)
        gate_act = gate * gate_s
        grad = grad_ref[:, lanes].astype(f32)
        output = out_ref[:, lanes]
        inv_rms = lax.rsqrt(jnp.mean(output * output, axis=-1, keepdims=True) + norm_eps)
        unit = output * inv_rms
        grad_unit = grad * unit
        dgain = dgain + jnp.sum(grad_unit * gate_act, axis=0, keepdims=True)
        dproj_ref[:, gate_at] = (
            grad_unit * gain * (gate_s * (1.0 + gate * (1.0 - gate_s)))
        ).astype(bf16)
        dunit = grad * (gain * gate_act)
        dout = inv_rms * (dunit - unit * jnp.mean(dunit * unit, axis=-1, keepdims=True))

        both = dot(jnp.concatenate([key, query], axis=0), key, NT)
        lower_raw = both[:CHUNK] * scale["strict"]
        lower = lower_raw * beta
        scores = both[CHUNK:] * scale["within"]
        inverse = inverse_ref[:, lanes]
        pseudo = pseudo_ref[:, lanes]
        memory = state_ref[0, head]
        dmemory = dstate[head]

        dpseudo = dot(scores, dout, TN) + dot(end * key, dmemory, NN)
        start_query = start * query
        dstate[head] = keep * dmemory + dot(
            jnp.concatenate([start_query.astype(bf16), -w_ref[:, lanes]], axis=0),
            jnp.concatenate([dout.astype(bf16), dpseudo.astype(bf16)], axis=0),
            TN,
        )
        solved = dot(inverse, dpseudo, TN)
        reads = dot(jnp.concatenate([dout, solved], axis=0), memory, NT)
        dquery_start = start * reads[:CHUNK]
        dkey_start = -start * reads[CHUNK:]
        by_pseudo = dot(jnp.concatenate([dout, solved], axis=0), pseudo, NT)
        dscores = by_pseudo[:CHUNK]
        dlower = -by_pseudo[CHUNK:]
        dkey_end = end * dot(pseudo, dmemory, NT)

        dbeta = jnp.sum(
            solved * value + dkey_start * key + dlower * lower_raw, axis=-1, keepdims=True
        )
        pair = dscores * scores + dlower * lower
        end_terms = dkey_end * key
        dcum = jnp.sum(
            pair + dquery_start * query + (dkey_start * key) * beta - end_terms,
            axis=-1,
            keepdims=True,
        )
        last_total = jnp.sum(
            jnp.sum(end_terms, axis=0, keepdims=True)
            + keep * jnp.sum(memory * dmemory, axis=0, keepdims=True),
            axis=-1,
            keepdims=True,
        )
        dcum = dcum + jnp.where(row[:, :1] == CHUNK - 1, last_total, 0.0)
        cum_columns = cum_columns + jnp.where(lane == head, dcum, 0.0)
        dbeta_columns = dbeta_columns + jnp.where(lane == heads + head, dbeta, 0.0)
        cum_rows = cum_rows + jnp.where(row == head, jnp.sum(pair, axis=0, keepdims=True), 0.0)

        near = (dlower * (scale["strict"] * beta)).astype(bf16)
        far = (dscores * scale["within"]).astype(bf16)
        toward = dot(jnp.concatenate([near, far], axis=0), key, NN)
        dkey = (
            toward[:CHUNK]
            + dot(
                jnp.concatenate([near, far], axis=0),
                jnp.concatenate([key, query], axis=0),
                TN,
            )
            + beta * dkey_start
            + dkey_end
        )
        dquery = (toward[CHUNK:] + dquery_start) * WIDTH**-0.5
        dvalue = beta * solved
        dq_act = q_norm * (dquery - q_unit * jnp.sum(q_unit * dquery, axis=-1, keepdims=True))
        dk_act = k_norm * (dkey - key * jnp.sum(key * dkey, axis=-1, keepdims=True))
        signal_back(0, head, q_terms, q_total, q_gate, dq_act)
        signal_back(1, head, k_terms, k_total, k_gate, dk_act)
        signal_back(2, head, v_terms, v_total, v_gate, dvalue)

    upper_ones = jnp.where(row <= col, 1.0, 0.0).astype(f32)
    dsteps = dot_exact(upper_ones, cum_columns - cum_rows.T, NN)
    drate_ref[...] += jnp.sum(dsteps * steps, axis=0, keepdims=True)
    dgain_ref[...] += dgain
    dlogits = dsteps * neg_rate * betas + dbeta_columns * betas * (1.0 - betas)
    dproj_ref[:, 4 * wide : 4 * wide + WIDTH] = jnp.where(
        lane < 2 * heads, dlogits, 0.0
    ).astype(bf16)


def mixer_forward(proj, seg_wide, conv_rows, neg_rate, gain):
    length, width = proj.shape
    heads = (width - WIDTH) // (4 * WIDTH)
    wide = heads * WIDTH
    count = length // CHUNK
    by_chunk = lambda cols: pl.BlockSpec((CHUNK, cols), lambda i: (i, 0))
    whole = lambda rows, cols: pl.BlockSpec((rows, cols), lambda i: (0, 0))
    return pl.pallas_call(
        functools.partial(forward_kernel, heads),
        grid=(count,),
        in_specs=[
            by_chunk(width), by_chunk(WIDTH), whole(12, wide), whole(1, WIDTH), whole(1, WIDTH),
        ],
        out_specs=[
            by_chunk(wide), by_chunk(wide), by_chunk(wide), by_chunk(wide), by_chunk(wide),
            pl.BlockSpec((1, heads, WIDTH, WIDTH), lambda i: (i, 0, 0, 0)),
        ],
        out_shape=[
            jax.ShapeDtypeStruct((length, wide), bf16),
            jax.ShapeDtypeStruct((length, wide), bf16),
            jax.ShapeDtypeStruct((length, wide), bf16),
            jax.ShapeDtypeStruct((length, wide), bf16),
            jax.ShapeDtypeStruct((length, wide), f32),
            jax.ShapeDtypeStruct((count, heads, WIDTH, WIDTH), f32),
        ],
        scratch_shapes=[
            pltpu.VMEM((heads, WIDTH, WIDTH), f32),
            pltpu.VMEM((HALO, 3 * wide), f32),
            pltpu.VMEM((HALO, WIDTH), f32),
        ],
        compiler_params=pltpu.CompilerParams(vmem_limit_bytes=48 * 1024 * 1024),
        cost_estimate=pl.CostEstimate(
            flops=2 * 160 * length * WIDTH * wide,
            bytes_accessed=4 * length * (width + 3 * wide),
            transcendentals=8 * length * wide,
        ),
        name="mixer_forward",
    )(proj, seg_wide, conv_rows, neg_rate, gain)


def mixer_backward(proj, seg_wide, conv_rows, neg_rate, gain, grad, saved):
    length, width = proj.shape
    heads = (width - WIDTH) // (4 * WIDTH)
    wide = heads * WIDTH
    count = length // CHUNK
    back = lambda i: count - 1 - i
    by_chunk = lambda cols: pl.BlockSpec((CHUNK, cols), lambda i: (back(i), 0))
    before = lambda cols: pl.BlockSpec(
        (HALO, cols), lambda i: (jnp.maximum(back(i) * (CHUNK // HALO) - 1, 0), 0)
    )
    whole = lambda rows, cols: pl.BlockSpec((rows, cols), lambda i: (0, 0))
    return pl.pallas_call(
        functools.partial(backward_kernel, heads),
        grid=(count,),
        in_specs=[
            by_chunk(width), by_chunk(WIDTH), before(WIDTH), before(3 * wide),
            whole(12, wide), whole(1, WIDTH), whole(1, WIDTH),
            by_chunk(wide), by_chunk(wide), by_chunk(wide), by_chunk(wide), by_chunk(wide),
            pl.BlockSpec((1, heads, WIDTH, WIDTH), lambda i: (back(i), 0, 0, 0)),
        ],
        out_specs=[by_chunk(width), whole(12, wide), whole(1, WIDTH), whole(1, WIDTH)],
        out_shape=[
            jax.ShapeDtypeStruct((length, width), bf16),
            jax.ShapeDtypeStruct((12, wide), f32),
            jax.ShapeDtypeStruct((1, WIDTH), f32),
            jax.ShapeDtypeStruct((1, WIDTH), f32),
        ],
        scratch_shapes=[
            pltpu.VMEM((heads, WIDTH, WIDTH), f32),
            pltpu.VMEM((HALO, 3 * wide), f32),
        ],
        compiler_params=pltpu.CompilerParams(vmem_limit_bytes=48 * 1024 * 1024),
        cost_estimate=pl.CostEstimate(
            flops=2 * 180 * length * WIDTH * wide,
            bytes_accessed=4 * length * (2 * width + 3 * wide),
            transcendentals=8 * length * wide,
        ),
        name="mixer_backward",
    )(proj, seg_wide, seg_wide, proj, conv_rows, neg_rate, gain, grad, *saved)


def project_kernel(x_ref, w_ref, out_ref):
    out_ref[...] = dot(x_ref[...], w_ref[...], NN)


def project(x, packed, columns):
    rows, model = x.shape
    return pl.pallas_call(
        project_kernel,
        grid=(pl.cdiv(columns, COLUMN_TILE),),
        in_specs=[
            pl.BlockSpec((rows, model), lambda i: (0, 0)),
            pl.BlockSpec((model, COLUMN_TILE), lambda i: (0, i)),
        ],
        out_specs=pl.BlockSpec((rows, COLUMN_TILE), lambda i: (0, i)),
        out_shape=jax.ShapeDtypeStruct((rows, columns), f32),
        compiler_params=pltpu.CompilerParams(vmem_limit_bytes=40 * 1024 * 1024),
        cost_estimate=pl.CostEstimate(
            flops=2 * rows * model * columns,
            bytes_accessed=2 * model * (rows + columns) + 4 * rows * columns,
            transcendentals=0,
        ),
        name="project",
    )(x, packed)


def ffn_kernel(tiles, x_ref, dy_ref, w_ref, h_ref, g_ref, y_ref, dx_ref, y_sum, dx_sum):
    step = pl.program_id(0)

    @pl.when(step == 0)
    def _():
        y_sum[...] = jnp.zeros_like(y_sum)
        dx_sum[...] = jnp.zeros_like(dx_sum)

    def units(size):
        gate_up = dot(x_ref[...], w_ref[:, : 2 * size], NN)
        grad = dot(dy_ref[...], w_ref[:, 2 * size : 3 * size], NN)
        gate, up = gate_up[:, :size], gate_up[:, size:]
        gate_s = sigmoid(gate)
        act = gate * gate_s
        h_ref[:, :size] = (act * up).astype(bf16)
        g_ref[:, :size] = (grad * up * (gate_s + act * (1.0 - gate_s))).astype(bf16)
        g_ref[:, size : 2 * size] = (grad * act).astype(bf16)
        y_sum[...] += dot(h_ref[:, :size], w_ref[:, 2 * size : 3 * size], NT)
        dx_sum[...] += dot(g_ref[:, : 2 * size], w_ref[:, : 2 * size], NT)

    per_tile(tiles, step, units)

    @pl.when(step == len(tiles) - 1)
    def _():
        y_ref[...] = y_sum[...].astype(bf16)
        dx_ref[...] = dx_sum[...].astype(bf16)


def per_tile(tiles, step, units):
    if tiles[0] == tiles[-1]:
        units(tiles[0])
        return

    @pl.when(step < len(tiles) - 1)
    def _():
        units(tiles[0])

    @pl.when(step == len(tiles) - 1)
    def _():
        units(tiles[-1])


def ffn(x, dy, packed, tiles):
    rows, model = x.shape
    hidden = sum(tiles)
    whole = pl.BlockSpec((rows, model), lambda i: (0, 0))
    return pl.pallas_call(
        functools.partial(ffn_kernel, tiles),
        grid=(len(tiles),),
        in_specs=[whole, whole, pl.BlockSpec((model, 3 * tiles[0]), lambda i: (0, i))],
        out_specs=[
            pl.BlockSpec((rows, tiles[0]), lambda i: (0, i)),
            pl.BlockSpec((rows, 2 * tiles[0]), lambda i: (0, i)),
            whole,
            whole,
        ],
        out_shape=[
            jax.ShapeDtypeStruct((rows, hidden), bf16),
            jax.ShapeDtypeStruct((rows, 2 * hidden), bf16),
            jax.ShapeDtypeStruct((rows, model), bf16),
            jax.ShapeDtypeStruct((rows, model), bf16),
        ],
        scratch_shapes=[pltpu.VMEM((rows, model), f32), pltpu.VMEM((rows, model), f32)],
        compiler_params=pltpu.CompilerParams(vmem_limit_bytes=48 * 1024 * 1024),
        cost_estimate=pl.CostEstimate(
            flops=12 * rows * model * hidden,
            bytes_accessed=2 * (3 * model * hidden + rows * (4 * model + 3 * hidden)),
            transcendentals=rows * hidden,
        ),
        name="ffn",
    )(x, dy, packed)


def ffn_grads_kernel(tiles, *refs):
    *inputs, out_ref, x_turned, dy_turned = refs
    count = len(inputs) // 4
    xs, dys, hs, gs = (inputs[at * count : (at + 1) * count] for at in range(4))
    step = pl.program_id(0)
    ends = [0]
    for x_ref in xs:
        ends.append(ends[-1] + x_ref.shape[0])
    lanes = [slice(first, last) for first, last in zip(ends, ends[1:])]

    @pl.when(step == 0)
    def _():
        for at, x_ref, dy_ref in zip(lanes, xs, dys):
            x_turned[:, at] = x_ref[...].T
            dy_turned[:, at] = dy_ref[...].T

    def units(size):
        up_grad, down_grad = 0.0, 0.0
        for at, h_ref, g_ref in zip(lanes, hs, gs):
            up_grad = up_grad + dot(x_turned[:, at], g_ref[:, : 2 * size], NN)
            down_grad = down_grad + dot(dy_turned[:, at], h_ref[:, :size], NN)
        out_ref[:, : 2 * size] = up_grad.astype(bf16)
        out_ref[:, 2 * size : 3 * size] = down_grad.astype(bf16)

    per_tile(tiles, step, units)


def ffn_grads(xs, dys, hs, gs, tiles):
    model = xs[0].shape[1]
    hidden = sum(tiles)
    total = sum(x.shape[0] for x in xs)
    whole = [pl.BlockSpec(x.shape, lambda i: (0, 0)) for x in xs]
    return pl.pallas_call(
        functools.partial(ffn_grads_kernel, tiles),
        grid=(len(tiles),),
        in_specs=whole
        + whole
        + [pl.BlockSpec((x.shape[0], tiles[0]), lambda i: (0, i)) for x in xs]
        + [pl.BlockSpec((x.shape[0], 2 * tiles[0]), lambda i: (0, i)) for x in xs],
        out_specs=pl.BlockSpec((model, 3 * tiles[0]), lambda i: (0, i)),
        out_shape=jax.ShapeDtypeStruct((model, 3 * hidden), bf16),
        scratch_shapes=[pltpu.VMEM((model, total), bf16), pltpu.VMEM((model, total), bf16)],
        compiler_params=pltpu.CompilerParams(vmem_limit_bytes=48 * 1024 * 1024),
        cost_estimate=pl.CostEstimate(
            flops=6 * total * model * hidden,
            bytes_accessed=2 * (3 * model * hidden + total * (2 * model + 3 * hidden)),
            transcendentals=0,
        ),
        name="ffn_grads",
    )(*xs, *dys, *hs, *gs)


def mixer_grads_kernel(
    orders, split, main_steps, core_ref, normed_ref, residual_ref, dproj_ref, mixed_ref, conv_ref,
    first_sent_ref, first_kept_ref, second_sent_ref, second_kept_ref,
    turned, residual_turned, conv_turned,
):
    step = pl.program_id(0)
    last = pl.num_programs(0) - 1
    first_order, second_order = orders
    count = len(first_order)
    size = normed_ref.shape[1] // count

    @pl.when(step == 0)
    def _():
        normed = normed_ref[...].T
        residual = residual_ref[...].T
        for at, block in enumerate(first_order):
            away = (block % 2 + 1 + core_ref[0]) % 2
            begin = (away * (count // 2) + at % (count // 2)) * size
            rows = pl.ds(pl.multiple_of(begin, size), size)
            from_rows = slice(block * size, (block + 1) * size)
            turned[rows, :] = normed[from_rows]
            residual_turned[rows, :] = residual[from_rows]
            conv_turned[rows, :] = conv_ref[from_rows, :]

    def store(grads, lanes):
        grads = grads.astype(bf16)
        half = count // 2 * size

        @pl.when(step < split)
        def _():
            first_sent_ref[:, lanes] = grads[:half]
            first_kept_ref[:, lanes] = grads[half:]

        @pl.when(step >= split)
        def _():
            for to, block in enumerate(second_order[: count // 2]):
                at = first_order.index(block)
                to_rows = slice(to * size, (to + 1) * size)
                second_sent_ref[to_rows, lanes] = grads[at * size : (at + 1) * size]
                second_kept_ref[to_rows, lanes] = grads[half + at * size : half + (at + 1) * size]

    @pl.when(step < main_steps)
    def _():
        store(dot(turned[...], dproj_ref[...], NN), slice(None))

    @pl.when((step >= main_steps) & (step < last))
    def _():
        store(dot(residual_turned[...], mixed_ref[...], NN), slice(None))

    @pl.when(step == last)
    def _():
        store(dot(turned[...], dproj_ref[:, :WIDTH], NN) + conv_turned[...], slice(0, WIDTH))


def mixer_grads(normed, residual, dproj, mixed, conv_block, core, orders):
    rows, model = normed.shape
    wide = mixed.shape[1]
    tile = 2 * WIDTH if wide % (2 * WIDTH) == 0 else WIDTH
    main_steps = 4 * wide // tile
    out_steps = wide // tile
    columns = 5 * wide + WIDTH
    split = (main_steps + out_steps + 1) * 5 // 9
    first = split * tile
    whole = lambda cols: pl.BlockSpec((rows, cols), lambda i, core: (0, 0))
    first_block = pl.BlockSpec((model // 2, tile), lambda i, core: (0, jnp.minimum(i, split - 1)))
    second_block = pl.BlockSpec((model // 2, tile), lambda i, core: (0, jnp.maximum(i - split, 0)))
    first_shape = jax.ShapeDtypeStruct((model // 2, first), bf16)
    second_shape = jax.ShapeDtypeStruct((model // 2, columns - first), bf16)
    return pl.pallas_call(
        functools.partial(mixer_grads_kernel, orders, split, main_steps),
        grid_spec=pltpu.PrefetchScalarGridSpec(
            num_scalar_prefetch=1,
            grid=(main_steps + out_steps + 1,),
            in_specs=[
                whole(model),
                whole(model),
                pl.BlockSpec((rows, tile), lambda i, core: (0, jnp.minimum(i, main_steps))),
                pl.BlockSpec(
                    (rows, tile), lambda i, core: (0, jnp.clip(i - main_steps, 0, out_steps - 1))
                ),
                pl.BlockSpec((model, WIDTH), lambda i, core: (0, 0)),
            ],
            out_specs=[first_block, first_block, second_block, second_block],
            scratch_shapes=[
                pltpu.VMEM((model, rows), bf16),
                pltpu.VMEM((model, rows), bf16),
                pltpu.VMEM((model, WIDTH), f32),
            ],
        ),
        out_shape=[first_shape, first_shape, second_shape, second_shape],
        compiler_params=pltpu.CompilerParams(vmem_limit_bytes=40 * 1024 * 1024),
        cost_estimate=pl.CostEstimate(
            flops=2 * rows * model * columns,
            bytes_accessed=2 * (2 * rows * model + (rows + model) * columns),
            transcendentals=0,
        ),
        name="mixer_grads",
    )(core, normed, residual, dproj, mixed, conv_block)


def rms_norm(values, scales):
    return values * lax.rsqrt(jnp.mean(values * values, axis=-1, keepdims=True) + norm_eps) * scales


def first_norm(values, gains):
    return rms_norm(values, gains[0])


def second_norm(values, gains):
    return rms_norm(values, gains[1])


def contract_last(operand, other):
    return lax.dot_general(
        operand, other, (((1,), (1,)), ((), ())), preferred_element_type=jnp.float32
    )


def contract_first(operand, other):
    return lax.dot_general(
        operand, other, (((0,), (0,)), ((), ())), preferred_element_type=jnp.float32
    )


def swap(rows):
    return lax.ppermute(rows, "tensor", [(0, 1), (1, 0)])


def sum_over(values, axis):
    size = lax.axis_size(axis)
    if size & (size - 1):
        return lax.psum(values, axis)
    bit = 1
    while bit < size:
        values = values + lax.ppermute(values, axis, [(i, i ^ bit) for i in range(size)])
        bit *= 2
    return values


def hidden_tiles(hidden):
    if hidden % WIDTH:
        return (hidden,)
    return (2 * WIDTH,) * (hidden // (2 * WIDTH)) + (WIDTH,) * (hidden // WIDTH % 2)


def pack_tiles(gate, up, down, tiles):
    blocks = []
    at = 0
    for size in tiles:
        blocks += [part[:, at : at + size] for part in (gate, up, down)]
        at += size
    return jnp.concatenate(blocks, axis=1)


def unpack_tiles(packed, tiles):
    parts = ([], [], [])
    at = 0
    for size in tiles:
        for part in parts:
            part.append(packed[:, at : at + size])
            at += size
    return [jnp.concatenate(part, axis=1) for part in parts]


def ffn_plain(x, dy, packed, tiles):
    gate_w, up_w, down_w = unpack_tiles(packed, tiles)
    gate = jnp.dot(x, gate_w, preferred_element_type=f32)
    up = jnp.dot(x, up_w, preferred_element_type=f32)
    grad = jnp.dot(dy, down_w, preferred_element_type=f32)
    gate_s = sigmoid(gate)
    act = gate * gate_s
    hidden = (act * up).astype(bf16)
    gate_grad = (grad * up * (gate_s + act * (1.0 - gate_s))).astype(bf16)
    up_grad = (grad * act).astype(bf16)
    share = contract_last(hidden, down_w).astype(bf16)
    dx = (contract_last(gate_grad, gate_w) + contract_last(up_grad, up_w)).astype(bf16)
    return hidden, jnp.concatenate([gate_grad, up_grad], axis=1), share, dx


def ffn_grads_plain(x, dy, hidden, grads, tiles):
    size = hidden.shape[1]
    return pack_tiles(
        contract_first(x, grads[:, :size]).astype(bf16),
        contract_first(x, grads[:, size:]).astype(bf16),
        contract_first(dy, hidden).astype(bf16),
        tiles,
    )


def bit_orders(size):
    bits = list(range(size.bit_length() - 1))
    return bits, bits[:1] + bits[2:] + bits[1:2]


def block_order(size, bits):
    return sorted(range(size), key=lambda i: [(i >> bit) & 1 for bit in bits])


def exchange(terms, bit):
    size = lax.axis_size("dp")
    mine = lax.axis_index("dp") >> bit & 1
    half = terms[0].shape[0] // 2
    total = 0.0
    for term in terms:
        total = total + lax.dynamic_slice_in_dim(term, (1 - mine) * half, half).astype(f32)
    received = flip(total.astype(bf16), bit)
    return [lax.dynamic_slice_in_dim(term, mine * half, half) for term in terms] + [received]


def flip(values, bit):
    size = lax.axis_size("dp")
    return lax.ppermute(values, "dp", [(i, i ^ (1 << bit)) for i in range(size)])


def local(
    tokens,
    segment_ids,
    norm_gains,
    w_mixer_in,
    w_rates,
    conv_weight,
    a_log,
    out_gain,
    w_output,
    w_gate_up,
    w_down,
    cotangent,
):
    dp_size = lax.axis_size("dp")
    pair = lax.axis_size("tensor") == 2
    tensor_rank = lax.axis_index("tensor")
    rows_here, _, heads, _ = w_mixer_in.shape
    model_width = rows_here * dp_size
    wide = heads * WIDTH
    hidden_here = w_gate_up.shape[2]
    tiles = hidden_tiles(hidden_here)
    kernels = hidden_here % WIDTH == 0
    taps_here = conv_weight.shape[3]
    own_rows = tokens.shape[1]
    projected_width = 4 * wide + WIDTH

    def gather_rows(rows):
        return lax.all_gather(rows, "tensor", axis=0, tiled=True)

    def scatter_rows(product):
        return lax.psum_scatter(product.astype(bf16), "tensor", scatter_dimension=0, tiled=True)

    def in_order(own, other):
        first = tensor_rank == 0
        return jnp.concatenate([jnp.where(first, own, other), jnp.where(first, other, own)], axis=0)

    def own_and_other(rows):
        own = lax.dynamic_slice_in_dim(rows, tensor_rank * own_rows, own_rows)
        return own, lax.dynamic_slice_in_dim(rows, (1 - tensor_rank) * own_rows, own_rows)

    conv_block = jnp.pad(
        conv_weight.transpose(3, 0, 1, 2).reshape(taps_here, 12 * heads),
        ((0, rows_here - taps_here), (0, WIDTH - 14 * heads)),
    )
    mixer_pack = jnp.concatenate(
        [
            w_mixer_in.reshape(rows_here, -1),
            w_rates.reshape(rows_here, -1),
            conv_block,
            w_output.T,
        ],
        axis=1,
    )
    mix_full = lax.all_gather(mixer_pack, "dp", axis=0, tiled=True)
    ffn_pack = pack_tiles(w_gate_up[:, 0], w_gate_up[:, 1], w_down.T, tiles)
    ffn_full = lax.all_gather(ffn_pack, "dp", axis=0, tiled=True)
    out_mine = mix_full[:, projected_width:]
    conv_at = 4 * wide + 2 * heads
    conv_rows = (
        mix_full[:, conv_at : conv_at + 12 * heads]
        .reshape(dp_size, rows_here, 12 * heads)[:, :taps_here]
        .reshape(dp_size * taps_here, 12 * heads)
        .T.reshape(12, wide)
        .astype(f32)
    )
    segment = jnp.broadcast_to(segment_ids[0][:, None].astype(f32), (segment_ids.shape[1], WIDTH))
    neg_rate = jnp.pad(
        -jnp.exp(lax.dynamic_slice_in_dim(a_log, tensor_rank * heads, heads)), (0, WIDTH - heads)
    )[None]
    gain_row = out_gain[None]

    grad_own = cotangent[0]
    inputs = tokens[0].astype(f32)
    normed, first_back = jax.vjp(first_norm, inputs, norm_gains)
    normed = normed.astype(bf16)
    if pair:
        normed_other = swap(normed)
        grad_sent, normed_other = lax.optimization_barrier((grad_own, normed_other))
        grad_other = swap(grad_sent)
        normed_all, grad_other, out_sent = lax.optimization_barrier(
            (in_order(normed, normed_other), grad_other, out_mine)
        )
        out_other = swap(out_sent)
    else:
        normed_all = gather_rows(normed)
    projected = project(normed_all, mix_full, projected_width)
    mixed, *saved = mixer_forward(projected, segment, conv_rows, neg_rate, gain_row)
    if pair:
        mixed, out_other = lax.optimization_barrier((mixed, out_other))
        mixed_own, mixed_theirs = own_and_other(mixed)
        share = contract_last(mixed_own, out_mine) + contract_last(swap(mixed_theirs), out_other)
    else:
        share = scatter_rows(contract_last(mixed, out_mine)).astype(f32)
    residual = inputs + share
    normed_ffn, second_back = jax.vjp(second_norm, residual, norm_gains)
    normed_ffn = normed_ffn.astype(bf16)
    one_ffn = ffn if kernels else ffn_plain
    if pair:
        half = own_rows // 2
        x_others = [swap(normed_ffn[:half]), swap(normed_ffn[half:])]
        others = []
        for at, x_other in enumerate(x_others):
            others.append(one_ffn(x_other, grad_other[at * half : (at + 1) * half], ffn_full, tiles))
        received = [swap(other[3]) for other in others]
        done = [one_ffn(normed_ffn, grad_own, ffn_full, tiles)] + others
        x_parts = [normed_ffn] + x_others
        dy_parts = [grad_own, grad_other[:half], grad_other[half:]]
        dx = done[0][3].astype(f32) + jnp.concatenate(received, axis=0).astype(f32)
    else:
        x_parts = [gather_rows(normed_ffn)]
        dy_parts = [gather_rows(grad_own)]
        done = [one_ffn(x_parts[0], dy_parts[0], ffn_full, tiles)]
        dx = scatter_rows(done[0][3]).astype(f32)
    h_parts, g_parts, y_parts, _ = zip(*done)
    if kernels:
        ffn_sums = ffn_grads(x_parts, dy_parts, h_parts, g_parts, tiles)
    else:
        ffn_sums = ffn_grads_plain(x_parts[0], dy_parts[0], h_parts[0], g_parts[0], tiles)
    residual_part, second_gains = second_back(dx)
    residual_grad = grad_own.astype(f32) + residual_part
    residual_low = residual_grad.astype(bf16)
    if pair:
        grad_theirs = jnp.dot(residual_low, out_other, preferred_element_type=f32).astype(bf16)
        grad_mine = jnp.dot(residual_low, out_mine, preferred_element_type=f32).astype(bf16)
        mixed_grad = in_order(grad_mine, swap(grad_theirs))
        mixed_grad, ffn_sums, residual_sent, y_sent = lax.optimization_barrier(
            (mixed_grad, ffn_sums, residual_low, jnp.concatenate(y_parts[1:], axis=0))
        )
        residual_all = in_order(residual_low, swap(residual_sent))
        y = y_parts[0].astype(f32) + swap(y_sent).astype(f32)
    else:
        residual_all = gather_rows(residual_low)
        mixed_grad = jnp.dot(residual_all, out_mine, preferred_element_type=f32).astype(bf16)
        y = scatter_rows(y_parts[0]).astype(f32)
    out_tokens = (residual + y).astype(bf16)[None]
    ffn_owned = lax.psum_scatter(ffn_sums, "dp", scatter_dimension=0, tiled=True)
    projection_grad, conv_grad, log_grad, gain_grad = mixer_backward(
        projected, segment, conv_rows, neg_rate, gain_row, mixed_grad, saved
    )
    conv_grad = jnp.pad(
        conv_grad.reshape(12 * heads, WIDTH).T.reshape(dp_size, taps_here, 12 * heads),
        ((0, 0), (0, rows_here - taps_here), (2 * heads, WIDTH - 14 * heads)),
    ).reshape(model_width, WIDTH)
    core = lax.axis_index("dp") % 2
    bits = bit_orders(dp_size)
    orders = [block_order(dp_size, order) for order in bits]
    first_sent, first_kept, second_sent, second_kept = mixer_grads(
        normed_all, residual_all, projection_grad, mixed, conv_grad, core[None], orders
    )
    first_sent, second_sent, projection_grad = lax.optimization_barrier(
        (first_sent, second_sent, projection_grad)
    )
    mix_rows = mix_full[:, :projected_width]
    second = [second_kept, flip(second_sent, 0)]
    first = [first_kept, flip(first_sent, 0)]
    if pair:
        grad_here, grad_there = own_and_other(projection_grad)
        mixer_input_grad = swap(contract_last(grad_there, mix_rows).astype(bf16)).astype(f32)
        mixer_input_grad = mixer_input_grad + contract_last(grad_here, mix_rows)
    else:
        mixer_input_grad = scatter_rows(contract_last(projection_grad, mix_rows)).astype(f32)
    second = exchange(second, bits[1][1])
    first = exchange(first, bits[0][1])
    mixer_input_grad, first, second = lax.optimization_barrier((mixer_input_grad, first, second))
    for one, other in zip(bits[0][2:], bits[1][2:]):
        second = exchange(second, other)
        first = exchange(first, one)
    mix_owned = jnp.concatenate(
        [sum(term.astype(f32) for term in terms) for terms in (first, second)], axis=1
    )
    input_part, first_gains = first_back(mixer_input_grad)
    input_grad = (residual_grad + input_part).astype(bf16)[None]
    log_full = lax.dynamic_update_slice_in_dim(
        jnp.zeros(a_log.shape, f32), log_grad[0, :heads], tensor_rank * heads, 0
    )
    small = jnp.concatenate(
        [
            (first_gains + second_gains).reshape(-1, WIDTH),
            gain_grad,
            jnp.pad(log_full, (0, WIDTH - log_full.shape[0]))[None],
        ]
    )
    small = sum_over(sum_over(small, "dp"), "tensor")
    gain_rows = 2 * model_width // WIDTH
    gate_grad, up_grad, down_grad = unpack_tiles(ffn_owned, tiles)
    rates = mix_owned[:, 5 * wide :]
    return (
        out_tokens,
        input_grad,
        small[:gain_rows].reshape(2, model_width),
        mix_owned[:, : 4 * wide].reshape(w_mixer_in.shape),
        rates[:, : 2 * heads].reshape(w_rates.shape),
        rates[:taps_here, 2 * heads : 14 * heads]
        .reshape(taps_here, 3, 4, heads)
        .transpose(1, 2, 3, 0),
        small[gain_rows + 1, : a_log.shape[0]],
        small[gain_rows],
        mix_owned[:, 4 * wide : 5 * wide].T,
        jnp.stack([gate_grad, up_grad], axis=1).astype(f32),
        down_grad.T.astype(f32),
    )


def solution(mesh):
    in_specs = (
        P("dp", "tensor", None),
        P("dp", None),
        P(),
        P("dp", None, "tensor", None),
        P("dp", None, "tensor"),
        P(None, None, "tensor", "dp"),
        P(),
        P(),
        P("tensor", "dp"),
        P("dp", None, "tensor"),
        P("tensor", "dp"),
        P("dp", "tensor", None),
    )
    out_specs = (
        P("dp", "tensor", None),
        P("dp", "tensor", None),
        P(),
        P("dp", None, "tensor", None),
        P("dp", None, "tensor"),
        P(None, None, "tensor", "dp"),
        P(),
        P(),
        P("tensor", "dp"),
        P("dp", None, "tensor"),
        P("tensor", "dp"),
    )
    return jax.shard_map(local, mesh=mesh, in_specs=in_specs, out_specs=out_specs, check_vma=False)
```

```python
import functools

import jax
import jax.numpy as jnp
from jax import lax
from jax.experimental import pallas as pl
from jax.experimental.pallas import tpu as pltpu
from jax.sharding import PartitionSpec as P

CHUNK = 128
WIDTH = 128
HALO = 8
COLUMN_TILE = 256
norm_eps = 1e-05
unit_eps = 1e-06
f32 = jnp.float32
bf16 = jnp.bfloat16

NN = ((1,), (0,))
NT = ((1,), (1,))
TN = ((0,), (0,))


def in_hbm(*arrays):
    return [pltpu.with_memory_space_constraint(array, pltpu.HBM) for array in arrays]


def dot(left, right, dims):
    return lax.dot_general(
        left.astype(bf16), right.astype(bf16), (dims, ((), ())), preferred_element_type=f32
    )


def dot_exact(left, right, dims):
    return lax.dot_general(
        left, right, (dims, ((), ())), precision=lax.Precision.HIGHEST, preferred_element_type=f32
    )


def sigmoid(value):
    return 0.5 * jnp.tanh(0.5 * value) + 0.5


def softplus(value):
    return jnp.maximum(value, 0.0) + jnp.log(1.0 + jnp.exp(-jnp.abs(value)))


def shifted(rows, offset):
    return pltpu.roll(rows, offset, 0)[HALO:] if offset else rows[HALO:]


def conv_terms(rows, keeps):
    return [rows[HALO:]] + [
        jnp.where(keeps[offset], shifted(rows, offset), 0.0) for offset in range(1, 4)
    ]


def conv_sum(terms, conv_ref, part, lanes):
    total = None
    for offset in range(4):
        weight = conv_ref[pl.ds(part * 4 + 3 - offset, 1), lanes]
        term = weight * terms[offset]
        total = term if total is None else total + term
    return total


def lane_column(values, lane):
    return jnp.broadcast_to(values[:, lane : lane + 1], values.shape)


def grids():
    row = lax.broadcasted_iota(jnp.int32, (CHUNK, CHUNK), 0)
    col = lax.broadcasted_iota(jnp.int32, (CHUNK, CHUNK), 1)
    return row, col


def level_masks(row, col):
    masks = []
    shift = 0
    while (1 << shift) < CHUNK:
        near = (row >> (shift + 1)) == (col >> (shift + 1))
        apart = (row >> shift) != (col >> shift)
        masks.append(near & apart)
        shift += 1
    return masks


def unit_lower_inverses(lowers, row, col, beside):
    masks = level_masks(row, col)
    beside = list(beside)
    share = -(-len(beside) // (2 * len(masks[1:])))

    def place():
        for work in beside[:share]:
            work()
        del beside[:share]

    identity = jnp.where(row == col, 1.0, 0.0).astype(f32)
    inverses = [identity - jnp.where(masks[0], lower, 0.0) for lower in lowers]
    for mask in masks[1:]:
        blocks = [jnp.where(mask, lower, 0.0).astype(bf16) for lower in lowers]
        low = [inverse.astype(bf16) for inverse in inverses]
        firsts = [dot(inverse, block, NN) for inverse, block in zip(low, blocks)]
        place()
        firsts = [dot(first, inverse, NN) for first, inverse in zip(firsts, low)]
        place()
        inverses = [inverse - first for inverse, first in zip(inverses, firsts)]
    return inverses


def chunk_scales(heads, rates, neg_rate, seg, last_seen, row, col):
    steps = neg_rate * softplus(rates)
    lower_ones = jnp.where(row >= col, 1.0, 0.0).astype(f32)
    cumulative = dot_exact(lower_ones, steps, NN)
    cumulative_rows = cumulative.T
    betas = sigmoid(rates)
    seg_rows = seg.T
    same = seg == seg_rows
    within = same & (row >= col)
    strict = same & (row > col)
    carry = seg == last_seen
    ends = seg == seg[CHUNK - 1 :, :]
    scales = []
    for head in range(heads):
        cum = lane_column(cumulative, head)
        cum_row = cumulative_rows[head : head + 1, :]
        gap = jnp.exp(jnp.minimum(cum - cum_row, 0.0))
        last = cum[CHUNK - 1 :, :]
        scales.append(
            dict(
                beta=lane_column(betas, heads + head),
                within=jnp.where(within, gap, 0.0),
                strict=jnp.where(strict, gap, 0.0),
                start=jnp.where(carry, jnp.exp(cum), 0.0),
                end=jnp.where(ends, jnp.exp(jnp.minimum(last - cum, 0.0)), 0.0),
                keep=jnp.where(carry[CHUNK - 1 :, :], jnp.exp(last), 0.0),
            )
        )
    return scales, steps, betas


def forward_kernel(
    heads, subs, proj_ref, seg_ref, conv_ref, rate_ref, gain_ref,
    mixed_ref, inverse_ref, w_ref, pseudo_ref, out_ref, state_ref, conv_out_ref,
    state, halo, seg_halo,
):
    step = pl.program_id(0)

    @pl.when(step == 0)
    def _():
        state[...] = jnp.zeros_like(state)
        halo[...] = jnp.zeros_like(halo)
        seg_halo[...] = jnp.full_like(seg_halo, -1.0)

    row, col = grids()
    wide = heads * WIDTH
    each = range(heads)
    items = [(sub, head) for sub in range(subs) for head in each]
    head_lanes = [slice(head * WIDTH, (head + 1) * WIDTH) for head in each]
    chunk_rows = [slice(sub * CHUNK, (sub + 1) * CHUNK) for sub in range(subs)]

    def with_halo(ref, before, sub, lanes):
        if sub:
            return ref[sub * CHUNK - HALO : (sub + 1) * CHUNK, lanes]
        return jnp.concatenate([before[:, lanes], ref[:CHUNK, lanes]], axis=0)

    keeps, scales = [], {}
    for sub in range(subs):
        seg_rows = with_halo(seg_ref, seg_halo, sub, slice(None))
        seg = seg_rows[HALO:]
        keeps.append([None] + [shifted(seg_rows, offset) == seg for offset in range(1, 4)])
        rates = proj_ref[chunk_rows[sub], 4 * wide : 4 * wide + WIDTH]
        found, _, _ = chunk_scales(
            heads, rates, rate_ref[...], seg, seg_rows[HALO - 1 : HALO, :], row, col
        )
        for head in each:
            scales[sub, head] = found[head]

    def signal(part, item):
        sub, head = item
        at = part * wide + head * WIDTH
        lanes = slice(at, at + WIDTH)
        terms = conv_terms(with_halo(proj_ref, halo, sub, lanes), keeps[sub])
        total = conv_sum(terms, conv_ref, part, head_lanes[head])
        conv_out_ref[chunk_rows[sub], lanes] = total
        return total * sigmoid(total)

    def unit(rows):
        return rows * lax.rsqrt(jnp.sum(rows * rows, axis=-1, keepdims=True) + unit_eps)

    keys = {item: signal(1, item) for item in items}
    keys = {item: unit(keys[item]) for item in items}
    keys_low = {item: keys[item].astype(bf16) for item in items}
    lowers = [
        dot(keys_low[item], keys_low[item], NT) * (scales[item]["strict"] * scales[item]["beta"])
        for item in items
    ]
    queries, scores, targets, gates, ends = {}, {}, {}, {}, {}

    def query_of(item):
        queries[item] = unit(signal(0, item)) * WIDTH**-0.5

    def scores_of(item):
        scores[item] = (
            dot(queries[item], keys_low[item], NT) * scales[item]["within"]
        ).astype(bf16)
        queries[item] = (scales[item]["start"] * queries[item]).astype(bf16)

    def target_of(item):
        beta = scales[item]["beta"]
        targets[item] = jnp.concatenate(
            [
                (beta * signal(2, item)).astype(bf16),
                (beta * scales[item]["start"] * keys[item]).astype(bf16),
            ],
            axis=1,
        )

    def gate_of(item):
        sub, head = item
        gate = proj_ref[chunk_rows[sub], 3 * wide + head * WIDTH : 3 * wide + (head + 1) * WIDTH]
        gates[item] = gain_ref[...] * gate * sigmoid(gate)
        ends[item] = (scales[item]["end"] * keys[item]).astype(bf16)

    beside = [
        functools.partial(work, item)
        for work in (query_of, target_of, scores_of, gate_of)
        for item in items
    ]
    inverses = unit_lower_inverses(lowers, row, col, beside)
    inverses = {item: inverse.astype(bf16) for item, inverse in zip(items, inverses)}
    halo[...] = proj_ref[subs * CHUNK - HALO :, : 3 * wide]
    seg_halo[...] = seg_ref[subs * CHUNK - HALO :, :]
    solved = {item: dot(inverses[item], targets[item], NN) for item in items}
    carried = {item: solved[item][:, WIDTH:].astype(bf16) for item in items}
    memories = [state[head] for head in each]
    for sub in range(subs):
        rows = chunk_rows[sub]
        reads = [
            dot(
                jnp.concatenate([carried[sub, head], queries[sub, head]], axis=0),
                memories[head],
                NN,
            )
            for head in each
        ]
        pseudos = [
            (solved[sub, head][:, :WIDTH] - reads[head][:CHUNK]).astype(bf16) for head in each
        ]
        updates = [dot(ends[sub, head], pseudos[head], TN) for head in each]
        outputs = [
            dot(scores[sub, head], pseudos[head], NN) + reads[head][CHUNK:] for head in each
        ]
        for head, lanes in enumerate(head_lanes):
            state_ref[sub, head] = memories[head]
            memories[head] = scales[sub, head]["keep"] * memories[head] + updates[head]
            inverse_ref[rows, lanes] = inverses[sub, head]
            w_ref[rows, lanes] = carried[sub, head]
            pseudo_ref[rows, lanes] = pseudos[head]
            output = outputs[head]
            out_ref[rows, lanes] = output
            inv_rms = lax.rsqrt(jnp.mean(output * output, axis=-1, keepdims=True) + norm_eps)
            mixed_ref[rows, lanes] = (output * inv_rms * gates[sub, head]).astype(bf16)
    for head in each:
        state[head] = memories[head]


def backward_kernel(
    heads, proj_ref, seg_ref, seg_before_ref, before_ref, conv_ref, rate_ref, gain_ref, grad_ref,
    inverse_ref, w_ref, pseudo_ref, out_ref, state_ref, conv_out_ref,
    dproj_ref, dconv_ref, drate_ref, dgain_ref,
    dstate, carry_halo,
):
    step = pl.program_id(0)
    first = step == pl.num_programs(0) - 1

    @pl.when(step == 0)
    def _():
        dstate[...] = jnp.zeros_like(dstate)
        carry_halo[...] = jnp.zeros_like(carry_halo)
        dconv_ref[...] = jnp.zeros_like(dconv_ref)
        drate_ref[...] = jnp.zeros_like(drate_ref)
        dgain_ref[...] = jnp.zeros_like(dgain_ref)

    row, col = grids()
    seg = seg_ref[...]
    seg_before = jnp.where(first, -1.0, seg_before_ref[...])
    seg_rows = jnp.concatenate([seg_before, seg], axis=0)
    keeps = [None] + [shifted(seg_rows, offset) == seg for offset in range(1, 4)]
    last_seen = seg_before[HALO - 1 :, :]
    wide = heads * WIDTH
    rates = proj_ref[:, 4 * wide : 4 * wide + WIDTH]
    neg_rate = rate_ref[...]
    scales, steps, betas = chunk_scales(heads, rates, neg_rate, seg, last_seen, row, col)

    def signal(part, head):
        at = part * wide + head * WIDTH
        total = conv_out_ref[:, at : at + WIDTH]
        return total, sigmoid(total)

    def signal_back(part, head, total, gate, grad):
        grad = grad * (gate * (1.0 + total * (1.0 - gate)))
        at = part * wide + head * WIDTH
        lanes = slice(at, at + WIDTH)
        head_lanes = slice(head * WIDTH, (head + 1) * WIDTH)
        rows = proj_ref[:, lanes]
        rows_before = before_ref[:, lanes]
        spread, spread_before = None, None
        for offset in range(4):
            tap = pl.ds(part * 4 + 3 - offset, 1)
            weight = conv_ref[tap, head_lanes]
            if offset:
                back = jnp.where(keeps[offset], grad, 0.0)
                back = jnp.concatenate([jnp.zeros((HALO, WIDTH), f32), back], axis=0)
                back = pltpu.roll(back, CHUNK + HALO - offset, 0)
                back_before, back = back[:HALO], back[HALO:]
                product = jnp.sum(back * rows, axis=0, keepdims=True) + jnp.sum(
                    back_before * rows_before, axis=0, keepdims=True
                )
                spread = spread + weight * back
                before = weight * back_before
                spread_before = before if spread_before is None else spread_before + before
            else:
                product = jnp.sum(grad * rows, axis=0, keepdims=True)
                spread = weight * grad
            dconv_ref[tap, head_lanes] += product
        tail = spread[CHUNK - HALO :] + carry_halo[:, lanes]
        dproj_ref[:, lanes] = jnp.concatenate([spread[: CHUNK - HALO], tail], axis=0).astype(bf16)
        carry_halo[:, lanes] = spread_before

    lane = col
    cum_columns = jnp.zeros((CHUNK, WIDTH), f32)
    cum_rows = jnp.zeros((CHUNK, CHUNK), f32)
    dbeta_columns = jnp.zeros((CHUNK, WIDTH), f32)
    dgain = jnp.zeros((1, WIDTH), f32)
    each = range(heads)
    head_lanes = [slice(head * WIDTH, (head + 1) * WIDTH) for head in each]
    gain = gain_ref[...]
    beta, start, end, keep, within, strict = (
        [scale[name] for scale in scales]
        for name in ("beta", "start", "end", "keep", "within", "strict")
    )
    memory = [state_ref[0, head] for head in each]
    dmemory = [dstate[head] for head in each]
    inverse = [inverse_ref[:, lanes] for lanes in head_lanes]
    pseudo = [pseudo_ref[:, lanes] for lanes in head_lanes]

    q_total, q_gate = zip(*[signal(0, head) for head in each])
    k_total, k_gate = zip(*[signal(1, head) for head in each])
    q_act = [total * gate for total, gate in zip(q_total, q_gate)]
    k_act = [total * gate for total, gate in zip(k_total, k_gate)]
    q_norm = [lax.rsqrt(jnp.sum(act * act, axis=-1, keepdims=True) + unit_eps) for act in q_act]
    k_norm = [lax.rsqrt(jnp.sum(act * act, axis=-1, keepdims=True) + unit_eps) for act in k_act]
    q_unit = [act * norm for act, norm in zip(q_act, q_norm)]
    key = [act * norm for act, norm in zip(k_act, k_norm)]
    query = [unit * WIDTH**-0.5 for unit in q_unit]
    both = [
        dot(jnp.concatenate([key[h].astype(bf16), query[h].astype(bf16)], axis=0), key[h], NT)
        for h in each
    ]

    dout = []
    for head, lanes in enumerate(head_lanes):
        gate_at = slice(3 * wide + head * WIDTH, 3 * wide + (head + 1) * WIDTH)
        gate = proj_ref[:, gate_at]
        gate_s = sigmoid(gate)
        gate_act = gate * gate_s
        grad = grad_ref[:, lanes].astype(f32)
        output = out_ref[:, lanes]
        inv_rms = lax.rsqrt(jnp.mean(output * output, axis=-1, keepdims=True) + norm_eps)
        unit = output * inv_rms
        grad_unit = grad * unit
        dgain = dgain + jnp.sum(grad_unit * gate_act, axis=0, keepdims=True)
        dproj_ref[:, gate_at] = (
            grad_unit * gain * (gate_s * (1.0 + gate * (1.0 - gate_s)))
        ).astype(bf16)
        dunit = grad * (gain * gate_act)
        dout.append(
            inv_rms * (dunit - unit * jnp.mean(dunit * unit, axis=-1, keepdims=True))
        )

    lower_raw = [both[h][:CHUNK] * strict[h] for h in each]
    lower = [lower_raw[h] * beta[h] for h in each]
    scores = [both[h][CHUNK:] * within[h] for h in each]
    dout_low = [value.astype(bf16) for value in dout]
    from_scores = [dot(scores[h], dout_low[h], TN) for h in each]
    from_end = [dot(end[h] * key[h], dmemory[h], NN) for h in each]
    dpseudo = [(from_scores[h] + from_end[h]).astype(bf16) for h in each]
    updates = [
        dot(
            jnp.concatenate(
                [(start[h] * query[h]).astype(bf16), -w_ref[:, head_lanes[h]]], axis=0
            ),
            jnp.concatenate([dout_low[h], dpseudo[h]], axis=0),
            TN,
        )
        for h in each
    ]
    dkey_end = [end[h] * dot(pseudo[h], dmemory[h], NT) for h in each]
    for h in each:
        dstate[h] = keep[h] * dmemory[h] + updates[h]
    solved = [dot(inverse[h], dpseudo[h], TN) for h in each]
    grads = [jnp.concatenate([dout_low[h], solved[h].astype(bf16)], axis=0) for h in each]
    reads = [dot(grads[h], memory[h], NT) for h in each]
    by_pseudo = [dot(grads[h], pseudo[h], NT) for h in each]
    near = [(-by_pseudo[h][CHUNK:] * (strict[h] * beta[h])).astype(bf16) for h in each]
    far = [(by_pseudo[h][:CHUNK] * within[h]).astype(bf16) for h in each]
    nears = [jnp.concatenate([near[h], far[h]], axis=0) for h in each]
    toward = [dot(nears[h], key[h], NN) for h in each]
    turned = [
        dot(
            nears[h],
            jnp.concatenate([key[h].astype(bf16), query[h].astype(bf16)], axis=0),
            TN,
        )
        for h in each
    ]
    dquery_start = [start[h] * reads[h][:CHUNK] for h in each]
    dkey_start = [-start[h] * reads[h][CHUNK:] for h in each]
    v_total, v_gate = zip(*[signal(2, head) for head in each])
    for h in each:
        dlower = -by_pseudo[h][CHUNK:]
        start_terms = dkey_start[h] * key[h]
        dbeta = jnp.sum(
            solved[h] * (v_total[h] * v_gate[h]) + start_terms + dlower * lower_raw[h],
            axis=-1,
            keepdims=True,
        )
        pair = by_pseudo[h][:CHUNK] * scores[h] + dlower * lower[h]
        end_terms = dkey_end[h] * key[h]
        dcum = jnp.sum(
            pair + dquery_start[h] * query[h] + start_terms * beta[h] - end_terms,
            axis=-1,
            keepdims=True,
        )
        last_total = jnp.sum(
            jnp.sum(end_terms, axis=0, keepdims=True)
            + keep[h] * jnp.sum(memory[h] * dmemory[h], axis=0, keepdims=True),
            axis=-1,
            keepdims=True,
        )
        dcum = dcum + jnp.where(row[:, :1] == CHUNK - 1, last_total, 0.0)
        cum_columns = cum_columns + jnp.where(lane == h, dcum, 0.0)
        dbeta_columns = dbeta_columns + jnp.where(lane == heads + h, dbeta, 0.0)
        cum_rows = cum_rows + jnp.where(row == h, jnp.sum(pair, axis=0, keepdims=True), 0.0)
    dkey = [
        toward[h][:CHUNK] + turned[h] + beta[h] * dkey_start[h] + dkey_end[h] for h in each
    ]
    dquery = [(toward[h][CHUNK:] + dquery_start[h]) * WIDTH**-0.5 for h in each]
    dq_act = [
        q_norm[h] * (dquery[h] - q_unit[h] * jnp.sum(q_unit[h] * dquery[h], axis=-1, keepdims=True))
        for h in each
    ]
    dk_act = [
        k_norm[h] * (dkey[h] - key[h] * jnp.sum(key[h] * dkey[h], axis=-1, keepdims=True))
        for h in each
    ]
    for h in each:
        signal_back(0, h, q_total[h], q_gate[h], dq_act[h])
        signal_back(1, h, k_total[h], k_gate[h], dk_act[h])
        signal_back(2, h, v_total[h], v_gate[h], beta[h] * solved[h])

    upper_ones = jnp.where(row <= col, 1.0, 0.0).astype(f32)
    dsteps = dot_exact(upper_ones, cum_columns - cum_rows.T, NN)
    drate_ref[...] += jnp.sum(dsteps * steps, axis=0, keepdims=True)
    dgain_ref[...] += dgain
    dlogits = dsteps * neg_rate * betas + dbeta_columns * betas * (1.0 - betas)
    dproj_ref[:, 4 * wide : 4 * wide + WIDTH] = jnp.where(
        lane < 2 * heads, dlogits, 0.0
    ).astype(bf16)


def mixer_forward(proj, seg_wide, conv_rows, neg_rate, gain):
    length, width = proj.shape
    heads = (width - WIDTH) // (4 * WIDTH)
    wide = heads * WIDTH
    count = length // CHUNK
    subs = 2 if count % 2 == 0 else 1
    by_chunk = lambda cols: pl.BlockSpec((subs * CHUNK, cols), lambda i: (i, 0))
    whole = lambda rows, cols: pl.BlockSpec((rows, cols), lambda i: (0, 0))
    return pl.pallas_call(
        functools.partial(forward_kernel, heads, subs),
        grid=(count // subs,),
        in_specs=[
            by_chunk(width), by_chunk(WIDTH), whole(12, wide), whole(1, WIDTH), whole(1, WIDTH),
        ],
        out_specs=[
            by_chunk(wide), by_chunk(wide), by_chunk(wide), by_chunk(wide), by_chunk(wide),
            pl.BlockSpec((subs, heads, WIDTH, WIDTH), lambda i: (i, 0, 0, 0)),
            by_chunk(3 * wide),
        ],
        out_shape=[
            pltpu.HBM((length, wide), bf16),
            pltpu.HBM((length, wide), bf16),
            pltpu.HBM((length, wide), bf16),
            pltpu.HBM((length, wide), bf16),
            pltpu.HBM((length, wide), f32),
            pltpu.HBM((count, heads, WIDTH, WIDTH), f32),
            pltpu.HBM((length, 3 * wide), f32),
        ],
        scratch_shapes=[
            pltpu.VMEM((heads, WIDTH, WIDTH), f32),
            pltpu.VMEM((HALO, 3 * wide), f32),
            pltpu.VMEM((HALO, WIDTH), f32),
        ],
        compiler_params=pltpu.CompilerParams(vmem_limit_bytes=48 * 1024 * 1024),
        cost_estimate=pl.CostEstimate(
            flops=2 * 160 * length * WIDTH * wide,
            bytes_accessed=4 * length * (width + 3 * wide),
            transcendentals=8 * length * wide,
        ),
        name="mixer_forward",
    )(*in_hbm(proj, seg_wide, conv_rows, neg_rate, gain))


def mixer_backward(proj, seg_wide, conv_rows, neg_rate, gain, grad, saved):
    length, width = proj.shape
    heads = (width - WIDTH) // (4 * WIDTH)
    wide = heads * WIDTH
    count = length // CHUNK
    back = lambda i: count - 1 - i
    by_chunk = lambda cols: pl.BlockSpec((CHUNK, cols), lambda i: (back(i), 0))
    before = lambda cols: pl.BlockSpec(
        (HALO, cols), lambda i: (jnp.maximum(back(i) * (CHUNK // HALO) - 1, 0), 0)
    )
    whole = lambda rows, cols: pl.BlockSpec((rows, cols), lambda i: (0, 0))
    return pl.pallas_call(
        functools.partial(backward_kernel, heads),
        grid=(count,),
        in_specs=[
            by_chunk(width), by_chunk(WIDTH), before(WIDTH), before(3 * wide),
            whole(12, wide), whole(1, WIDTH), whole(1, WIDTH),
            by_chunk(wide), by_chunk(wide), by_chunk(wide), by_chunk(wide), by_chunk(wide),
            pl.BlockSpec((1, heads, WIDTH, WIDTH), lambda i: (back(i), 0, 0, 0)),
            by_chunk(3 * wide),
        ],
        out_specs=[by_chunk(width), whole(12, wide), whole(1, WIDTH), whole(1, WIDTH)],
        out_shape=[
            pltpu.HBM((length, width), bf16),
            pltpu.HBM((12, wide), f32),
            pltpu.HBM((1, WIDTH), f32),
            pltpu.HBM((1, WIDTH), f32),
        ],
        scratch_shapes=[
            pltpu.VMEM((heads, WIDTH, WIDTH), f32),
            pltpu.VMEM((HALO, 3 * wide), f32),
        ],
        compiler_params=pltpu.CompilerParams(vmem_limit_bytes=48 * 1024 * 1024),
        cost_estimate=pl.CostEstimate(
            flops=2 * 180 * length * WIDTH * wide,
            bytes_accessed=4 * length * (2 * width + 3 * wide),
            transcendentals=8 * length * wide,
        ),
        name="mixer_backward",
    )(*in_hbm(proj, seg_wide, seg_wide, proj, conv_rows, neg_rate, gain, grad, *saved))


def project_kernel(x_ref, w_ref, out_ref):
    out_ref[...] = dot(x_ref[...], w_ref[...], NN)


def project(x, packed, columns):
    rows, model = x.shape
    return pl.pallas_call(
        project_kernel,
        grid=(pl.cdiv(columns, COLUMN_TILE),),
        in_specs=[
            pl.BlockSpec((rows, model), lambda i: (0, 0)),
            pl.BlockSpec((model, COLUMN_TILE), lambda i: (0, i)),
        ],
        out_specs=pl.BlockSpec((rows, COLUMN_TILE), lambda i: (0, i)),
        out_shape=pltpu.HBM((rows, columns), f32),
        compiler_params=pltpu.CompilerParams(vmem_limit_bytes=40 * 1024 * 1024),
        cost_estimate=pl.CostEstimate(
            flops=2 * rows * model * columns,
            bytes_accessed=2 * model * (rows + columns) + 4 * rows * columns,
            transcendentals=0,
        ),
        name="project",
    )(*in_hbm(x, packed))


def ffn_kernel(tiles, x_ref, dy_ref, w_ref, h_ref, g_ref, y_ref, dx_ref, y_sum, dx_sum):
    step = pl.program_id(0)

    @pl.when(step == 0)
    def _():
        y_sum[...] = jnp.zeros_like(y_sum)
        dx_sum[...] = jnp.zeros_like(dx_sum)

    def units(size):
        gate_up = dot(x_ref[...], w_ref[:, : 2 * size], NN)
        grad = dot(dy_ref[...], w_ref[:, 2 * size : 3 * size], NN)
        gate, up = gate_up[:, :size], gate_up[:, size:]
        gate_s = sigmoid(gate)
        act = gate * gate_s
        h_ref[:, :size] = (act * up).astype(bf16)
        g_ref[:, :size] = (grad * up * (gate_s + act * (1.0 - gate_s))).astype(bf16)
        g_ref[:, size : 2 * size] = (grad * act).astype(bf16)
        y_sum[...] += dot(h_ref[:, :size], w_ref[:, 2 * size : 3 * size], NT)
        dx_sum[...] += dot(g_ref[:, : 2 * size], w_ref[:, : 2 * size], NT)

    per_tile(tiles, step, units)

    @pl.when(step == len(tiles) - 1)
    def _():
        y_ref[...] = y_sum[...].astype(bf16)
        dx_ref[...] = dx_sum[...].astype(bf16)


def per_tile(tiles, step, units):
    if tiles[0] == tiles[-1]:
        units(tiles[0])
        return

    @pl.when(step < len(tiles) - 1)
    def _():
        units(tiles[0])

    @pl.when(step == len(tiles) - 1)
    def _():
        units(tiles[-1])


def ffn(x, dy, packed, tiles):
    rows, model = x.shape
    hidden = sum(tiles)
    whole = pl.BlockSpec((rows, model), lambda i: (0, 0))
    return pl.pallas_call(
        functools.partial(ffn_kernel, tiles),
        grid=(len(tiles),),
        in_specs=[whole, whole, pl.BlockSpec((model, 3 * tiles[0]), lambda i: (0, i))],
        out_specs=[
            pl.BlockSpec((rows, tiles[0]), lambda i: (0, i)),
            pl.BlockSpec((rows, 2 * tiles[0]), lambda i: (0, i)),
            whole,
            whole,
        ],
        out_shape=[
            pltpu.HBM((rows, hidden), bf16),
            pltpu.HBM((rows, 2 * hidden), bf16),
            pltpu.HBM((rows, model), bf16),
            pltpu.HBM((rows, model), bf16),
        ],
        scratch_shapes=[pltpu.VMEM((rows, model), f32), pltpu.VMEM((rows, model), f32)],
        compiler_params=pltpu.CompilerParams(vmem_limit_bytes=48 * 1024 * 1024),
        cost_estimate=pl.CostEstimate(
            flops=12 * rows * model * hidden,
            bytes_accessed=2 * (3 * model * hidden + rows * (4 * model + 3 * hidden)),
            transcendentals=rows * hidden,
        ),
        name="ffn",
    )(*in_hbm(x, dy, packed))


def ffn_grads_kernel(tiles, *refs):
    *inputs, out_ref, x_turned, dy_turned = refs
    count = len(inputs) // 4
    xs, dys, hs, gs = (inputs[at * count : (at + 1) * count] for at in range(4))
    step = pl.program_id(0)
    ends = [0]
    for x_ref in xs:
        ends.append(ends[-1] + x_ref.shape[0])
    lanes = [slice(first, last) for first, last in zip(ends, ends[1:])]

    @pl.when(step == 0)
    def _():
        for at, x_ref, dy_ref in zip(lanes, xs, dys):
            x_turned[:, at] = x_ref[...].T
            dy_turned[:, at] = dy_ref[...].T

    def units(size):
        up_grad, down_grad = 0.0, 0.0
        for at, h_ref, g_ref in zip(lanes, hs, gs):
            up_grad = up_grad + dot(x_turned[:, at], g_ref[:, : 2 * size], NN)
            down_grad = down_grad + dot(dy_turned[:, at], h_ref[:, :size], NN)
        out_ref[:, : 2 * size] = up_grad.astype(bf16)
        out_ref[:, 2 * size : 3 * size] = down_grad.astype(bf16)

    per_tile(tiles, step, units)


def ffn_grads(xs, dys, hs, gs, tiles):
    model = xs[0].shape[1]
    hidden = sum(tiles)
    total = sum(x.shape[0] for x in xs)
    whole = [pl.BlockSpec(x.shape, lambda i: (0, 0)) for x in xs]
    return pl.pallas_call(
        functools.partial(ffn_grads_kernel, tiles),
        grid=(len(tiles),),
        in_specs=whole
        + whole
        + [pl.BlockSpec((x.shape[0], tiles[0]), lambda i: (0, i)) for x in xs]
        + [pl.BlockSpec((x.shape[0], 2 * tiles[0]), lambda i: (0, i)) for x in xs],
        out_specs=pl.BlockSpec((model, 3 * tiles[0]), lambda i: (0, i)),
        out_shape=pltpu.HBM((model, 3 * hidden), bf16),
        scratch_shapes=[pltpu.VMEM((model, total), bf16), pltpu.VMEM((model, total), bf16)],
        compiler_params=pltpu.CompilerParams(vmem_limit_bytes=48 * 1024 * 1024),
        cost_estimate=pl.CostEstimate(
            flops=6 * total * model * hidden,
            bytes_accessed=2 * (3 * model * hidden + total * (2 * model + 3 * hidden)),
            transcendentals=0,
        ),
        name="ffn_grads",
    )(*in_hbm(*xs, *dys, *hs, *gs))


def mixer_grads_kernel(
    orders, split, main_steps, core_ref, normed_ref, residual_ref, dproj_ref, mixed_ref, conv_ref,
    first_sent_ref, first_kept_ref, second_sent_ref, second_kept_ref,
    turned, residual_turned, conv_turned,
):
    step = pl.program_id(0)
    last = pl.num_programs(0) - 1
    first_order, second_order = orders
    count = len(first_order)
    size = normed_ref.shape[1] // count

    @pl.when(step == 0)
    def _():
        normed = normed_ref[...].T
        residual = residual_ref[...].T
        for at, block in enumerate(first_order):
            away = (block % 2 + 1 + core_ref[0]) % 2
            begin = (away * (count // 2) + at % (count // 2)) * size
            rows = pl.ds(pl.multiple_of(begin, size), size)
            from_rows = slice(block * size, (block + 1) * size)
            turned[rows, :] = normed[from_rows]
            residual_turned[rows, :] = residual[from_rows]
            conv_turned[rows, :] = conv_ref[from_rows, :]

    def store(grads, lanes):
        grads = grads.astype(bf16)
        half = count // 2 * size

        @pl.when(step < split)
        def _():
            first_sent_ref[:, lanes] = grads[:half]
            first_kept_ref[:, lanes] = grads[half:]

        @pl.when(step >= split)
        def _():
            for to, block in enumerate(second_order[: count // 2]):
                at = first_order.index(block)
                to_rows = slice(to * size, (to + 1) * size)
                second_sent_ref[to_rows, lanes] = grads[at * size : (at + 1) * size]
                second_kept_ref[to_rows, lanes] = grads[half + at * size : half + (at + 1) * size]

    @pl.when(step < main_steps)
    def _():
        store(dot(turned[...], dproj_ref[...], NN), slice(None))

    @pl.when((step >= main_steps) & (step < last))
    def _():
        store(dot(residual_turned[...], mixed_ref[...], NN), slice(None))

    @pl.when(step == last)
    def _():
        store(dot(turned[...], dproj_ref[:, :WIDTH], NN) + conv_turned[...], slice(0, WIDTH))


def mixer_grads(normed, residual, dproj, mixed, conv_block, core, orders):
    rows, model = normed.shape
    wide = mixed.shape[1]
    tile = 2 * WIDTH if wide % (2 * WIDTH) == 0 else WIDTH
    main_steps = 4 * wide // tile
    out_steps = wide // tile
    columns = 5 * wide + WIDTH
    split = (main_steps + out_steps + 1) * 5 // 9
    first = split * tile
    whole = lambda cols: pl.BlockSpec((rows, cols), lambda i, core: (0, 0))
    first_block = pl.BlockSpec((model // 2, tile), lambda i, core: (0, jnp.minimum(i, split - 1)))
    second_block = pl.BlockSpec((model // 2, tile), lambda i, core: (0, jnp.maximum(i - split, 0)))
    first_shape = pltpu.HBM((model // 2, first), bf16)
    second_shape = pltpu.HBM((model // 2, columns - first), bf16)
    return pl.pallas_call(
        functools.partial(mixer_grads_kernel, orders, split, main_steps),
        grid_spec=pltpu.PrefetchScalarGridSpec(
            num_scalar_prefetch=1,
            grid=(main_steps + out_steps + 1,),
            in_specs=[
                whole(model),
                whole(model),
                pl.BlockSpec((rows, tile), lambda i, core: (0, jnp.minimum(i, main_steps))),
                pl.BlockSpec(
                    (rows, tile), lambda i, core: (0, jnp.clip(i - main_steps, 0, out_steps - 1))
                ),
                pl.BlockSpec((model, WIDTH), lambda i, core: (0, 0)),
            ],
            out_specs=[first_block, first_block, second_block, second_block],
            scratch_shapes=[
                pltpu.VMEM((model, rows), bf16),
                pltpu.VMEM((model, rows), bf16),
                pltpu.VMEM((model, WIDTH), f32),
            ],
        ),
        out_shape=[first_shape, first_shape, second_shape, second_shape],
        compiler_params=pltpu.CompilerParams(vmem_limit_bytes=40 * 1024 * 1024),
        cost_estimate=pl.CostEstimate(
            flops=2 * rows * model * columns,
            bytes_accessed=2 * (2 * rows * model + (rows + model) * columns),
            transcendentals=0,
        ),
        name="mixer_grads",
    )(core, *in_hbm(normed, residual, dproj, mixed, conv_block))


def rms_norm(values, scales):
    return values * lax.rsqrt(jnp.mean(values * values, axis=-1, keepdims=True) + norm_eps) * scales


def first_norm(values, gains):
    return rms_norm(values, gains[0])


def second_norm(values, gains):
    return rms_norm(values, gains[1])


def contract_last(operand, other):
    return lax.dot_general(
        operand, other, (((1,), (1,)), ((), ())), preferred_element_type=jnp.float32
    )


def contract_first(operand, other):
    return lax.dot_general(
        operand, other, (((0,), (0,)), ((), ())), preferred_element_type=jnp.float32
    )


def swap(rows):
    return lax.ppermute(rows, "tensor", [(0, 1), (1, 0)])


def sum_over(values, axis):
    size = lax.axis_size(axis)
    if size & (size - 1):
        return lax.psum(values, axis)
    bit = 1
    while bit < size:
        values = values + lax.ppermute(values, axis, [(i, i ^ bit) for i in range(size)])
        bit *= 2
    return values


def hidden_tiles(hidden):
    if hidden % WIDTH:
        return (hidden,)
    return (2 * WIDTH,) * (hidden // (2 * WIDTH)) + (WIDTH,) * (hidden // WIDTH % 2)


def pack_tiles(gate, up, down, tiles):
    blocks = []
    at = 0
    for size in tiles:
        blocks += [part[:, at : at + size] for part in (gate, up, down)]
        at += size
    return jnp.concatenate(blocks, axis=1)


def unpack_tiles(packed, tiles):
    parts = ([], [], [])
    at = 0
    for size in tiles:
        for part in parts:
            part.append(packed[:, at : at + size])
            at += size
    return [jnp.concatenate(part, axis=1) for part in parts]


def ffn_plain(x, dy, packed, tiles):
    gate_w, up_w, down_w = unpack_tiles(packed, tiles)
    gate = jnp.dot(x, gate_w, preferred_element_type=f32)
    up = jnp.dot(x, up_w, preferred_element_type=f32)
    grad = jnp.dot(dy, down_w, preferred_element_type=f32)
    gate_s = sigmoid(gate)
    act = gate * gate_s
    hidden = (act * up).astype(bf16)
    gate_grad = (grad * up * (gate_s + act * (1.0 - gate_s))).astype(bf16)
    up_grad = (grad * act).astype(bf16)
    share = contract_last(hidden, down_w).astype(bf16)
    dx = (contract_last(gate_grad, gate_w) + contract_last(up_grad, up_w)).astype(bf16)
    return hidden, jnp.concatenate([gate_grad, up_grad], axis=1), share, dx


def ffn_grads_plain(x, dy, hidden, grads, tiles):
    size = hidden.shape[1]
    return pack_tiles(
        contract_first(x, grads[:, :size]).astype(bf16),
        contract_first(x, grads[:, size:]).astype(bf16),
        contract_first(dy, hidden).astype(bf16),
        tiles,
    )


def bit_orders(size):
    bits = list(range(size.bit_length() - 1))
    return bits, bits[:1] + bits[2:] + bits[1:2]


def block_order(size, bits):
    return sorted(range(size), key=lambda i: [(i >> bit) & 1 for bit in bits])


def outgoing(terms, bit):
    mine = lax.axis_index("dp") >> bit & 1
    half = terms[0].shape[0] // 2
    total = 0.0
    for term in terms:
        total = total + lax.dynamic_slice_in_dim(term, (1 - mine) * half, half).astype(f32)
    return total.astype(bf16)


def settle(terms, bit, sent):
    mine = lax.axis_index("dp") >> bit & 1
    half = terms[0].shape[0] // 2
    own = [lax.dynamic_slice_in_dim(term, mine * half, half) for term in terms]
    return own + [flip(sent, bit)]


def flip(values, bit):
    size = lax.axis_size("dp")
    return lax.ppermute(values, "dp", [(i, i ^ (1 << bit)) for i in range(size)])


def local(
    tokens,
    segment_ids,
    norm_gains,
    w_mixer_in,
    w_rates,
    conv_weight,
    a_log,
    out_gain,
    w_output,
    w_gate_up,
    w_down,
    cotangent,
):
    dp_size = lax.axis_size("dp")
    pair = lax.axis_size("tensor") == 2
    tensor_rank = lax.axis_index("tensor")
    rows_here, _, heads, _ = w_mixer_in.shape
    model_width = rows_here * dp_size
    wide = heads * WIDTH
    hidden_here = w_gate_up.shape[2]
    tiles = hidden_tiles(hidden_here)
    kernels = hidden_here % WIDTH == 0
    taps_here = conv_weight.shape[3]
    own_rows = tokens.shape[1]
    projected_width = 4 * wide + WIDTH

    def gather_rows(rows):
        return lax.all_gather(rows, "tensor", axis=0, tiled=True)

    def scatter_rows(product):
        return lax.psum_scatter(product.astype(bf16), "tensor", scatter_dimension=0, tiled=True)

    def in_order(own, other):
        first = tensor_rank == 0
        return jnp.concatenate([jnp.where(first, own, other), jnp.where(first, other, own)], axis=0)

    def own_and_other(rows):
        own = lax.dynamic_slice_in_dim(rows, tensor_rank * own_rows, own_rows)
        return own, lax.dynamic_slice_in_dim(rows, (1 - tensor_rank) * own_rows, own_rows)

    conv_block = jnp.pad(
        conv_weight.transpose(3, 0, 1, 2).reshape(taps_here, 12 * heads),
        ((0, rows_here - taps_here), (0, WIDTH - 14 * heads)),
    )
    mixer_pack = jnp.concatenate(
        [
            w_mixer_in.reshape(rows_here, -1),
            w_rates.reshape(rows_here, -1),
            conv_block,
            w_output.T,
        ],
        axis=1,
    )
    mix_full = lax.all_gather(mixer_pack, "dp", axis=0, tiled=True)
    ffn_pack = pack_tiles(w_gate_up[:, 0], w_gate_up[:, 1], w_down.T, tiles)
    ffn_full = lax.all_gather(ffn_pack, "dp", axis=0, tiled=True)
    out_mine = mix_full[:, projected_width:]
    conv_at = 4 * wide + 2 * heads
    conv_rows = (
        mix_full[:, conv_at : conv_at + 12 * heads]
        .reshape(dp_size, rows_here, 12 * heads)[:, :taps_here]
        .reshape(dp_size * taps_here, 12 * heads)
        .T.reshape(12, wide)
        .astype(f32)
    )
    segment = jnp.broadcast_to(segment_ids[0][:, None].astype(f32), (segment_ids.shape[1], WIDTH))
    neg_rate = jnp.pad(
        -jnp.exp(lax.dynamic_slice_in_dim(a_log, tensor_rank * heads, heads)), (0, WIDTH - heads)
    )[None]
    gain_row = out_gain[None]

    grad_own = cotangent[0]
    inputs = tokens[0].astype(f32)
    normed, first_back = jax.vjp(first_norm, inputs, norm_gains)
    normed = normed.astype(bf16)
    if pair:
        normed_other = swap(normed)
        grad_sent, normed_other = lax.optimization_barrier((grad_own, normed_other))
        grad_other = swap(grad_sent)
        normed_all, grad_other, out_sent = lax.optimization_barrier(
            (in_order(normed, normed_other), grad_other, out_mine)
        )
        out_other = swap(out_sent)
    else:
        normed_all = gather_rows(normed)
    projected = project(normed_all, mix_full, projected_width)
    mixed, *saved = mixer_forward(projected, segment, conv_rows, neg_rate, gain_row)
    if pair:
        mixed, out_other = lax.optimization_barrier((mixed, out_other))
        mixed_own, mixed_theirs = own_and_other(mixed)
        share = contract_last(mixed_own, out_mine) + contract_last(swap(mixed_theirs), out_other)
    else:
        share = scatter_rows(contract_last(mixed, out_mine)).astype(f32)
    residual = inputs + share
    normed_ffn, second_back = jax.vjp(second_norm, residual, norm_gains)
    normed_ffn = normed_ffn.astype(bf16)
    one_ffn = ffn if kernels else ffn_plain
    if pair:
        half = own_rows // 2
        x_others = [swap(normed_ffn[:half]), swap(normed_ffn[half:])]
        others = []
        for at, x_other in enumerate(x_others):
            others.append(one_ffn(x_other, grad_other[at * half : (at + 1) * half], ffn_full, tiles))
        received = [swap(other[3]) for other in others]
        done = [one_ffn(normed_ffn, grad_own, ffn_full, tiles)] + others
        x_parts = [normed_ffn] + x_others
        dy_parts = [grad_own, grad_other[:half], grad_other[half:]]
        dx = done[0][3].astype(f32) + jnp.concatenate(received, axis=0).astype(f32)
    else:
        x_parts = [gather_rows(normed_ffn)]
        dy_parts = [gather_rows(grad_own)]
        done = [one_ffn(x_parts[0], dy_parts[0], ffn_full, tiles)]
        dx = scatter_rows(done[0][3]).astype(f32)
    h_parts, g_parts, y_parts, _ = zip(*done)
    if kernels:
        ffn_sums = ffn_grads(x_parts, dy_parts, h_parts, g_parts, tiles)
    else:
        ffn_sums = ffn_grads_plain(x_parts[0], dy_parts[0], h_parts[0], g_parts[0], tiles)
    residual_part, second_gains = second_back(dx)
    residual_grad = grad_own.astype(f32) + residual_part
    residual_low = residual_grad.astype(bf16)
    if pair:
        grad_theirs = jnp.dot(residual_low, out_other, preferred_element_type=f32).astype(bf16)
        grad_mine = jnp.dot(residual_low, out_mine, preferred_element_type=f32).astype(bf16)
        mixed_grad = in_order(grad_mine, swap(grad_theirs))
        mixed_grad, ffn_sums, residual_sent, y_sent = lax.optimization_barrier(
            (mixed_grad, ffn_sums, residual_low, jnp.concatenate(y_parts[1:], axis=0))
        )
        residual_all = in_order(residual_low, swap(residual_sent))
    else:
        residual_all = gather_rows(residual_low)
        mixed_grad = jnp.dot(residual_all, out_mine, preferred_element_type=f32).astype(bf16)
    ffn_owned = lax.psum_scatter(ffn_sums, "dp", scatter_dimension=0, tiled=True)
    projection_grad, conv_grad, log_grad, gain_grad = mixer_backward(
        projected, segment, conv_rows, neg_rate, gain_row, mixed_grad, saved
    )
    conv_grad = jnp.pad(
        conv_grad.reshape(12 * heads, WIDTH).T.reshape(dp_size, taps_here, 12 * heads),
        ((0, 0), (0, rows_here - taps_here), (2 * heads, WIDTH - 14 * heads)),
    ).reshape(model_width, WIDTH)
    core = lax.axis_index("dp") % 2
    bits = bit_orders(dp_size)
    orders = [block_order(dp_size, order) for order in bits]
    mix_rows = mix_full[:, :projected_width]
    if pair:
        grad_here, grad_there = own_and_other(projection_grad)
        sent = contract_last(grad_there, mix_rows).astype(bf16)
        sent, projection_grad = lax.optimization_barrier((sent, projection_grad))
        half = own_rows // 2
        received, received_late = swap(sent[:half]), swap(sent[half:])
    else:
        received = scatter_rows(contract_last(projection_grad, mix_rows))
    first_sent, first_kept, second_sent, second_kept = mixer_grads(
        normed_all, residual_all, projection_grad, mixed, conv_grad, core[None], orders
    )
    if pair:
        first_sent, second_sent, received = lax.optimization_barrier(
            (first_sent, second_sent, received)
        )
    second = [second_kept, flip(second_sent, 0)]
    first = [first_kept, flip(first_sent, 0)]
    second_out = outgoing(second, bits[1][1])
    first_out = outgoing(first, bits[0][1])
    if pair:
        received_late, y_sent, _, _ = lax.optimization_barrier(
            (received_late, y_sent, first_out, second_out)
        )
        received = jnp.concatenate([received, received_late], axis=0)
        y_other = swap(y_sent)
    else:
        y_other = scatter_rows(y_parts[0])
    second = settle(second, bits[1][1], second_out)
    first = settle(first, bits[0][1], first_out)
    mixer_input_grad = received.astype(f32)
    y = y_other.astype(f32)
    if pair:
        mixer_input_grad = mixer_input_grad + contract_last(grad_here, mix_rows)
        y = y + y_parts[0].astype(f32)
    out_tokens = (residual + y).astype(bf16)[None]
    input_part, first_gains = first_back(mixer_input_grad)
    input_grad = (residual_grad + input_part).astype(bf16)[None]
    log_full = lax.dynamic_update_slice_in_dim(
        jnp.zeros(a_log.shape, f32), log_grad[0, :heads], tensor_rank * heads, 0
    )
    small = jnp.concatenate(
        [
            (first_gains + second_gains).reshape(-1, WIDTH),
            gain_grad,
            jnp.pad(log_full, (0, WIDTH - log_full.shape[0]))[None],
        ]
    )
    for one, other in zip(bits[0][2:], bits[1][2:]):
        second_out = outgoing(second, other)
        first_out = outgoing(first, one)
        if one == bits[0][2]:
            small, _ = lax.optimization_barrier((small, first_out))
        second = settle(second, other, second_out)
        first = settle(first, one, first_out)
    mix_owned = jnp.concatenate(
        [sum(term.astype(f32) for term in terms) for terms in (first, second)], axis=1
    )
    small = sum_over(sum_over(small, "dp"), "tensor")
    gain_rows = 2 * model_width // WIDTH
    gate_grad, up_grad, down_grad = unpack_tiles(ffn_owned, tiles)
    rates = mix_owned[:, 5 * wide :]
    return (
        out_tokens,
        input_grad,
        small[:gain_rows].reshape(2, model_width),
        mix_owned[:, : 4 * wide].reshape(w_mixer_in.shape),
        rates[:, : 2 * heads].reshape(w_rates.shape),
        rates[:taps_here, 2 * heads : 14 * heads]
        .reshape(taps_here, 3, 4, heads)
        .transpose(1, 2, 3, 0),
        small[gain_rows + 1, : a_log.shape[0]],
        small[gain_rows],
        mix_owned[:, 4 * wide : 5 * wide].T,
        jnp.stack([gate_grad, up_grad], axis=1).astype(f32),
        down_grad.T.astype(f32),
    )


def solution(mesh):
    in_specs = (
        P("dp", "tensor", None),
        P("dp", None),
        P(),
        P("dp", None, "tensor", None),
        P("dp", None, "tensor"),
        P(None, None, "tensor", "dp"),
        P(),
        P(),
        P("tensor", "dp"),
        P("dp", None, "tensor"),
        P("tensor", "dp"),
        P("dp", "tensor", None),
    )
    out_specs = (
        P("dp", "tensor", None),
        P("dp", "tensor", None),
        P(),
        P("dp", None, "tensor", None),
        P("dp", None, "tensor"),
        P(None, None, "tensor", "dp"),
        P(),
        P(),
        P("tensor", "dp"),
        P("dp", None, "tensor"),
        P("tensor", "dp"),
    )
    return jax.shard_map(local, mesh=mesh, in_specs=in_specs, out_specs=out_specs, check_vma=False)
```

```python
import functools

import jax
import jax.numpy as jnp
from jax import lax
from jax.experimental import pallas as pl
from jax.experimental.pallas import tpu as pltpu
from jax.sharding import PartitionSpec as P

CHUNK = 128
WIDTH = 128
HALO = 8
COLUMN_TILE = 256
norm_eps = 1e-05
unit_eps = 1e-06
f32 = jnp.float32
bf16 = jnp.bfloat16

NN = ((1,), (0,))
NT = ((1,), (1,))
TN = ((0,), (0,))


def in_hbm(*arrays):
    return [pltpu.with_memory_space_constraint(array, pltpu.HBM) for array in arrays]


def dot(left, right, dims):
    return lax.dot_general(
        left.astype(bf16), right.astype(bf16), (dims, ((), ())), preferred_element_type=f32
    )


def dot_exact(left, right, dims):
    return lax.dot_general(
        left, right, (dims, ((), ())), precision=lax.Precision.HIGHEST, preferred_element_type=f32
    )


def sigmoid(value):
    return 0.5 * jnp.tanh(0.5 * value) + 0.5


def softplus(value):
    return jnp.maximum(value, 0.0) + jnp.log(1.0 + jnp.exp(-jnp.abs(value)))


def shifted(rows, offset):
    return pltpu.roll(rows, offset, 0)[HALO:] if offset else rows[HALO:]


def conv_terms(rows, keeps):
    return [rows[HALO:]] + [
        jnp.where(keeps[offset], shifted(rows, offset), 0.0) for offset in range(1, 4)
    ]


def conv_sum(terms, conv_ref, part, lanes):
    total = None
    for offset in range(4):
        weight = conv_ref[pl.ds(part * 4 + 3 - offset, 1), lanes]
        term = weight * terms[offset]
        total = term if total is None else total + term
    return total


def lane_column(values, lane):
    return jnp.broadcast_to(values[:, lane : lane + 1], values.shape)


def grids():
    row = lax.broadcasted_iota(jnp.int32, (CHUNK, CHUNK), 0)
    col = lax.broadcasted_iota(jnp.int32, (CHUNK, CHUNK), 1)
    return row, col


def level_masks(row, col):
    masks = []
    shift = 0
    while (1 << shift) < CHUNK:
        near = (row >> (shift + 1)) == (col >> (shift + 1))
        apart = (row >> shift) != (col >> shift)
        masks.append(near & apart)
        shift += 1
    return masks


def unit_lower_inverses(lowers, row, col, beside):
    masks = level_masks(row, col)
    beside = list(beside)
    share = -(-len(beside) // (2 * len(masks[1:])))

    def place():
        for work in beside[:share]:
            work()
        del beside[:share]

    identity = jnp.where(row == col, 1.0, 0.0).astype(f32)
    inverses = [identity - jnp.where(masks[0], lower, 0.0) for lower in lowers]
    for mask in masks[1:]:
        blocks = [jnp.where(mask, lower, 0.0).astype(bf16) for lower in lowers]
        low = [inverse.astype(bf16) for inverse in inverses]
        firsts = [dot(inverse, block, NN) for inverse, block in zip(low, blocks)]
        place()
        firsts = [dot(first, inverse, NN) for first, inverse in zip(firsts, low)]
        place()
        inverses = [inverse - first for inverse, first in zip(inverses, firsts)]
    return inverses


def chunk_scales(heads, rates, neg_rate, seg, last_seen, row, col):
    steps = neg_rate * softplus(rates)
    lower_ones = jnp.where(row >= col, 1.0, 0.0).astype(f32)
    cumulative = dot_exact(lower_ones, steps, NN)
    cumulative_rows = cumulative.T
    betas = sigmoid(rates)
    seg_rows = seg.T
    same = seg == seg_rows
    within = same & (row >= col)
    strict = same & (row > col)
    carry = seg == last_seen
    ends = seg == seg[CHUNK - 1 :, :]
    scales = []
    for head in range(heads):
        cum = lane_column(cumulative, head)
        cum_row = cumulative_rows[head : head + 1, :]
        gap = jnp.exp(jnp.minimum(cum - cum_row, 0.0))
        last = cum[CHUNK - 1 :, :]
        scales.append(
            dict(
                beta=lane_column(betas, heads + head),
                within=jnp.where(within, gap, 0.0),
                strict=jnp.where(strict, gap, 0.0),
                start=jnp.where(carry, jnp.exp(cum), 0.0),
                end=jnp.where(ends, jnp.exp(jnp.minimum(last - cum, 0.0)), 0.0),
                keep=jnp.where(carry[CHUNK - 1 :, :], jnp.exp(last), 0.0),
            )
        )
    return scales, steps, betas


def forward_kernel(
    heads, subs, x_ref, weight_ref, seg_ref, conv_ref, rate_ref, gain_ref,
    proj_ref, mixed_ref, inverse_ref, w_ref, pseudo_ref, out_ref, state_ref, conv_out_ref,
    state, halo, seg_halo, ahead,
):
    step = pl.program_id(0)
    block_rows = subs * CHUNK
    width = proj_ref.shape[1]

    def project(block, lanes):
        rows = x_ref[pl.ds(pl.multiple_of(block * block_rows, block_rows), block_rows), :]
        ahead[:, lanes] = dot(rows, weight_ref[:, lanes], NN)

    column_tiles = [
        slice(at, min(at + COLUMN_TILE, width)) for at in range(0, width, COLUMN_TILE)
    ]

    @pl.when(step == 0)
    def _():
        state[...] = jnp.zeros_like(state)
        halo[...] = jnp.zeros_like(halo)
        seg_halo[...] = jnp.full_like(seg_halo, -1.0)
        for lanes in column_tiles:
            project(0, lanes)

    proj_ref[...] = ahead[...]
    following = jnp.minimum(step + 1, pl.num_programs(0) - 1)
    row, col = grids()
    wide = heads * WIDTH
    each = range(heads)
    items = [(sub, head) for sub in range(subs) for head in each]
    head_lanes = [slice(head * WIDTH, (head + 1) * WIDTH) for head in each]
    chunk_rows = [slice(sub * CHUNK, (sub + 1) * CHUNK) for sub in range(subs)]

    def with_halo(ref, before, sub, lanes):
        if sub:
            return ref[sub * CHUNK - HALO : (sub + 1) * CHUNK, lanes]
        return jnp.concatenate([before[:, lanes], ref[:CHUNK, lanes]], axis=0)

    keeps, scales = [], {}
    for sub in range(subs):
        seg_rows = with_halo(seg_ref, seg_halo, sub, slice(None))
        seg = seg_rows[HALO:]
        keeps.append([None] + [shifted(seg_rows, offset) == seg for offset in range(1, 4)])
        rates = proj_ref[chunk_rows[sub], 4 * wide : 4 * wide + WIDTH]
        found, _, _ = chunk_scales(
            heads, rates, rate_ref[...], seg, seg_rows[HALO - 1 : HALO, :], row, col
        )
        for head in each:
            scales[sub, head] = found[head]

    def signal(part, item):
        sub, head = item
        at = part * wide + head * WIDTH
        lanes = slice(at, at + WIDTH)
        terms = conv_terms(with_halo(proj_ref, halo, sub, lanes), keeps[sub])
        total = conv_sum(terms, conv_ref, part, head_lanes[head])
        conv_out_ref[chunk_rows[sub], lanes] = total
        return total * sigmoid(total)

    def unit(rows):
        return rows * lax.rsqrt(jnp.sum(rows * rows, axis=-1, keepdims=True) + unit_eps)

    keys = {item: signal(1, item) for item in items}
    keys = {item: unit(keys[item]) for item in items}
    keys_low = {item: keys[item].astype(bf16) for item in items}
    lowers = [
        dot(keys_low[item], keys_low[item], NT) * (scales[item]["strict"] * scales[item]["beta"])
        for item in items
    ]
    queries, scores, targets, gates, ends = {}, {}, {}, {}, {}

    def query_of(item):
        queries[item] = unit(signal(0, item)) * WIDTH**-0.5

    def scores_of(item):
        scores[item] = (
            dot(queries[item], keys_low[item], NT) * scales[item]["within"]
        ).astype(bf16)
        queries[item] = (scales[item]["start"] * queries[item]).astype(bf16)

    def target_of(item):
        beta = scales[item]["beta"]
        targets[item] = jnp.concatenate(
            [
                (beta * signal(2, item)).astype(bf16),
                (beta * scales[item]["start"] * keys[item]).astype(bf16),
            ],
            axis=1,
        )

    def gate_of(item):
        sub, head = item
        gate = proj_ref[chunk_rows[sub], 3 * wide + head * WIDTH : 3 * wide + (head + 1) * WIDTH]
        gates[item] = gain_ref[...] * gate * sigmoid(gate)
        ends[item] = (scales[item]["end"] * keys[item]).astype(bf16)

    beside = [
        functools.partial(work, item)
        for work in (query_of, target_of, scores_of, gate_of)
        for item in items
    ]
    for at, lanes in enumerate(column_tiles):
        place = at * (len(beside) // len(column_tiles) + 1)
        beside.insert(place, functools.partial(project, following, lanes))
    inverses = unit_lower_inverses(lowers, row, col, beside)
    inverses = {item: inverse.astype(bf16) for item, inverse in zip(items, inverses)}
    halo[...] = proj_ref[subs * CHUNK - HALO :, : 3 * wide]
    seg_halo[...] = seg_ref[subs * CHUNK - HALO :, :]
    solved = {item: dot(inverses[item], targets[item], NN) for item in items}
    carried = {item: solved[item][:, WIDTH:].astype(bf16) for item in items}
    memories = [state[head] for head in each]
    for sub in range(subs):
        rows = chunk_rows[sub]
        reads = [
            dot(
                jnp.concatenate([carried[sub, head], queries[sub, head]], axis=0),
                memories[head],
                NN,
            )
            for head in each
        ]
        pseudos = [
            (solved[sub, head][:, :WIDTH] - reads[head][:CHUNK]).astype(bf16) for head in each
        ]
        updates = [dot(ends[sub, head], pseudos[head], TN) for head in each]
        outputs = [
            dot(scores[sub, head], pseudos[head], NN) + reads[head][CHUNK:] for head in each
        ]
        for head, lanes in enumerate(head_lanes):
            state_ref[sub, head] = memories[head]
            memories[head] = scales[sub, head]["keep"] * memories[head] + updates[head]
            inverse_ref[rows, lanes] = inverses[sub, head]
            w_ref[rows, lanes] = carried[sub, head]
            pseudo_ref[rows, lanes] = pseudos[head]
            output = outputs[head]
            out_ref[rows, lanes] = output
            inv_rms = lax.rsqrt(jnp.mean(output * output, axis=-1, keepdims=True) + norm_eps)
            mixed_ref[rows, lanes] = (output * inv_rms * gates[sub, head]).astype(bf16)
    for head in each:
        state[head] = memories[head]


def backward_kernel(
    heads, parts, rank_ref, proj_ref, seg_ref, seg_before_ref, before_ref, conv_ref, rate_ref,
    gain_ref, *refs
):
    grad_refs, refs = refs[:parts], refs[parts:]
    backward_steps(
        heads, rank_ref, proj_ref, seg_ref, seg_before_ref, before_ref, conv_ref, rate_ref,
        gain_ref, grad_refs, *refs
    )


def backward_steps(
    heads, rank_ref, proj_ref, seg_ref, seg_before_ref, before_ref, conv_ref, rate_ref, gain_ref,
    grad_refs, inverse_ref, w_ref, pseudo_ref, out_ref, state_ref, conv_out_ref,
    dproj_ref, dconv_ref, drate_ref, dgain_ref,
    dstate, carry_halo,
):
    step = pl.program_id(0)
    first = step == pl.num_programs(0) - 1

    @pl.when(step == 0)
    def _():
        dstate[...] = jnp.zeros_like(dstate)
        carry_halo[...] = jnp.zeros_like(carry_halo)
        dconv_ref[...] = jnp.zeros_like(dconv_ref)
        drate_ref[...] = jnp.zeros_like(drate_ref)
        dgain_ref[...] = jnp.zeros_like(dgain_ref)

    row, col = grids()
    seg = seg_ref[...]
    seg_before = jnp.where(first, -1.0, seg_before_ref[...])
    seg_rows = jnp.concatenate([seg_before, seg], axis=0)
    keeps = [None] + [shifted(seg_rows, offset) == seg for offset in range(1, 4)]
    last_seen = seg_before[HALO - 1 :, :]
    wide = heads * WIDTH
    rates = proj_ref[:, 4 * wide : 4 * wide + WIDTH]
    neg_rate = rate_ref[...]
    scales, steps, betas = chunk_scales(heads, rates, neg_rate, seg, last_seen, row, col)

    def signal(part, head):
        at = part * wide + head * WIDTH
        total = conv_out_ref[:, at : at + WIDTH]
        return total, sigmoid(total)

    def signal_back(part, head, total, gate, grad):
        grad = grad * (gate * (1.0 + total * (1.0 - gate)))
        at = part * wide + head * WIDTH
        lanes = slice(at, at + WIDTH)
        head_lanes = slice(head * WIDTH, (head + 1) * WIDTH)
        rows = proj_ref[:, lanes]
        rows_before = before_ref[:, lanes]
        spread, spread_before = None, None
        for offset in range(4):
            tap = pl.ds(part * 4 + 3 - offset, 1)
            weight = conv_ref[tap, head_lanes]
            if offset:
                back = jnp.where(keeps[offset], grad, 0.0)
                back = jnp.concatenate([jnp.zeros((HALO, WIDTH), f32), back], axis=0)
                back = pltpu.roll(back, CHUNK + HALO - offset, 0)
                back_before, back = back[:HALO], back[HALO:]
                product = jnp.sum(back * rows, axis=0, keepdims=True) + jnp.sum(
                    back_before * rows_before, axis=0, keepdims=True
                )
                spread = spread + weight * back
                before = weight * back_before
                spread_before = before if spread_before is None else spread_before + before
            else:
                product = jnp.sum(grad * rows, axis=0, keepdims=True)
                spread = weight * grad
            dconv_ref[tap, head_lanes] += product
        tail = spread[CHUNK - HALO :] + carry_halo[:, lanes]
        dproj_ref[:, lanes] = jnp.concatenate([spread[: CHUNK - HALO], tail], axis=0).astype(bf16)
        carry_halo[:, lanes] = spread_before

    lane = col
    cum_columns = jnp.zeros((CHUNK, WIDTH), f32)
    cum_rows = jnp.zeros((CHUNK, CHUNK), f32)
    dbeta_columns = jnp.zeros((CHUNK, WIDTH), f32)
    dgain = jnp.zeros((1, WIDTH), f32)
    each = range(heads)
    head_lanes = [slice(head * WIDTH, (head + 1) * WIDTH) for head in each]
    gain = gain_ref[...]
    beta, start, end, keep, within, strict = (
        [scale[name] for scale in scales]
        for name in ("beta", "start", "end", "keep", "within", "strict")
    )
    memory = [state_ref[0, head] for head in each]
    dmemory = [dstate[head] for head in each]
    inverse = [inverse_ref[:, lanes] for lanes in head_lanes]
    pseudo = [pseudo_ref[:, lanes] for lanes in head_lanes]

    q_total, q_gate = zip(*[signal(0, head) for head in each])
    k_total, k_gate = zip(*[signal(1, head) for head in each])
    q_act = [total * gate for total, gate in zip(q_total, q_gate)]
    k_act = [total * gate for total, gate in zip(k_total, k_gate)]
    q_norm = [lax.rsqrt(jnp.sum(act * act, axis=-1, keepdims=True) + unit_eps) for act in q_act]
    k_norm = [lax.rsqrt(jnp.sum(act * act, axis=-1, keepdims=True) + unit_eps) for act in k_act]
    q_unit = [act * norm for act, norm in zip(q_act, q_norm)]
    key = [act * norm for act, norm in zip(k_act, k_norm)]
    query = [unit * WIDTH**-0.5 for unit in q_unit]
    both = [
        dot(jnp.concatenate([key[h].astype(bf16), query[h].astype(bf16)], axis=0), key[h], NT)
        for h in each
    ]

    half = pl.num_programs(0) // 2
    from_own = (pl.num_programs(0) - 1 - step) // half == rank_ref[0]
    dout = []
    for head, lanes in enumerate(head_lanes):
        gate_at = slice(3 * wide + head * WIDTH, 3 * wide + (head + 1) * WIDTH)
        gate = proj_ref[:, gate_at]
        gate_s = sigmoid(gate)
        gate_act = gate * gate_s
        grad = grad_refs[0][:, lanes].astype(f32)
        if len(grad_refs) == 2:
            grad = jnp.where(from_own, grad, grad_refs[1][:, lanes].astype(f32))
        output = out_ref[:, lanes]
        inv_rms = lax.rsqrt(jnp.mean(output * output, axis=-1, keepdims=True) + norm_eps)
        unit = output * inv_rms
        grad_unit = grad * unit
        dgain = dgain + jnp.sum(grad_unit * gate_act, axis=0, keepdims=True)
        dproj_ref[:, gate_at] = (
            grad_unit * gain * (gate_s * (1.0 + gate * (1.0 - gate_s)))
        ).astype(bf16)
        dunit = grad * (gain * gate_act)
        dout.append(
            inv_rms * (dunit - unit * jnp.mean(dunit * unit, axis=-1, keepdims=True))
        )

    lower_raw = [both[h][:CHUNK] * strict[h] for h in each]
    lower = [lower_raw[h] * beta[h] for h in each]
    scores = [both[h][CHUNK:] * within[h] for h in each]
    dout_low = [value.astype(bf16) for value in dout]
    from_scores = [dot(scores[h], dout_low[h], TN) for h in each]
    from_end = [dot(end[h] * key[h], dmemory[h], NN) for h in each]
    dpseudo = [(from_scores[h] + from_end[h]).astype(bf16) for h in each]
    updates = [
        dot(
            jnp.concatenate(
                [(start[h] * query[h]).astype(bf16), -w_ref[:, head_lanes[h]]], axis=0
            ),
            jnp.concatenate([dout_low[h], dpseudo[h]], axis=0),
            TN,
        )
        for h in each
    ]
    dkey_end = [end[h] * dot(pseudo[h], dmemory[h], NT) for h in each]
    for h in each:
        dstate[h] = keep[h] * dmemory[h] + updates[h]
    solved = [dot(inverse[h], dpseudo[h], TN) for h in each]
    grads = [jnp.concatenate([dout_low[h], solved[h].astype(bf16)], axis=0) for h in each]
    reads = [dot(grads[h], memory[h], NT) for h in each]
    by_pseudo = [dot(grads[h], pseudo[h], NT) for h in each]
    near = [(-by_pseudo[h][CHUNK:] * (strict[h] * beta[h])).astype(bf16) for h in each]
    far = [(by_pseudo[h][:CHUNK] * within[h]).astype(bf16) for h in each]
    nears = [jnp.concatenate([near[h], far[h]], axis=0) for h in each]
    toward = [dot(nears[h], key[h], NN) for h in each]
    turned = [
        dot(
            nears[h],
            jnp.concatenate([key[h].astype(bf16), query[h].astype(bf16)], axis=0),
            TN,
        )
        for h in each
    ]
    dquery_start = [start[h] * reads[h][:CHUNK] for h in each]
    dkey_start = [-start[h] * reads[h][CHUNK:] for h in each]
    v_total, v_gate = zip(*[signal(2, head) for head in each])
    for h in each:
        dlower = -by_pseudo[h][CHUNK:]
        start_terms = dkey_start[h] * key[h]
        dbeta = jnp.sum(
            solved[h] * (v_total[h] * v_gate[h]) + start_terms + dlower * lower_raw[h],
            axis=-1,
            keepdims=True,
        )
        pair = by_pseudo[h][:CHUNK] * scores[h] + dlower * lower[h]
        end_terms = dkey_end[h] * key[h]
        dcum = jnp.sum(
            pair + dquery_start[h] * query[h] + start_terms * beta[h] - end_terms,
            axis=-1,
            keepdims=True,
        )
        last_total = jnp.sum(
            jnp.sum(end_terms, axis=0, keepdims=True)
            + keep[h] * jnp.sum(memory[h] * dmemory[h], axis=0, keepdims=True),
            axis=-1,
            keepdims=True,
        )
        dcum = dcum + jnp.where(row[:, :1] == CHUNK - 1, last_total, 0.0)
        cum_columns = cum_columns + jnp.where(lane == h, dcum, 0.0)
        dbeta_columns = dbeta_columns + jnp.where(lane == heads + h, dbeta, 0.0)
        cum_rows = cum_rows + jnp.where(row == h, jnp.sum(pair, axis=0, keepdims=True), 0.0)
    dkey = [
        toward[h][:CHUNK] + turned[h] + beta[h] * dkey_start[h] + dkey_end[h] for h in each
    ]
    dquery = [(toward[h][CHUNK:] + dquery_start[h]) * WIDTH**-0.5 for h in each]
    dq_act = [
        q_norm[h] * (dquery[h] - q_unit[h] * jnp.sum(q_unit[h] * dquery[h], axis=-1, keepdims=True))
        for h in each
    ]
    dk_act = [
        k_norm[h] * (dkey[h] - key[h] * jnp.sum(key[h] * dkey[h], axis=-1, keepdims=True))
        for h in each
    ]
    for h in each:
        signal_back(0, h, q_total[h], q_gate[h], dq_act[h])
        signal_back(1, h, k_total[h], k_gate[h], dk_act[h])
        signal_back(2, h, v_total[h], v_gate[h], beta[h] * solved[h])

    upper_ones = jnp.where(row <= col, 1.0, 0.0).astype(f32)
    dsteps = dot_exact(upper_ones, cum_columns - cum_rows.T, NN)
    drate_ref[...] += jnp.sum(dsteps * steps, axis=0, keepdims=True)
    dgain_ref[...] += dgain
    dlogits = dsteps * neg_rate * betas + dbeta_columns * betas * (1.0 - betas)
    dproj_ref[:, 4 * wide : 4 * wide + WIDTH] = jnp.where(
        lane < 2 * heads, dlogits, 0.0
    ).astype(bf16)


def mixer_forward(x, weights, heads, seg_wide, conv_rows, neg_rate, gain):
    length, model = x.shape
    wide = heads * WIDTH
    width = 4 * wide + WIDTH
    count = length // CHUNK
    subs = 2 if count % 2 == 0 else 1
    by_chunk = lambda cols: pl.BlockSpec((subs * CHUNK, cols), lambda i: (i, 0))
    whole = lambda rows, cols: pl.BlockSpec((rows, cols), lambda i: (0, 0))
    return pl.pallas_call(
        functools.partial(forward_kernel, heads, subs),
        grid=(count // subs,),
        in_specs=[
            whole(length, model), whole(model, width), by_chunk(WIDTH), whole(12, wide), whole(1, WIDTH), whole(1, WIDTH),
        ],
        out_specs=[
            by_chunk(width), by_chunk(wide), by_chunk(wide), by_chunk(wide), by_chunk(wide), by_chunk(wide),
            pl.BlockSpec((subs, heads, WIDTH, WIDTH), lambda i: (i, 0, 0, 0)),
            by_chunk(3 * wide),
        ],
        out_shape=[
            pltpu.HBM((length, width), f32),
            pltpu.HBM((length, wide), bf16),
            pltpu.HBM((length, wide), bf16),
            pltpu.HBM((length, wide), bf16),
            pltpu.HBM((length, wide), bf16),
            pltpu.HBM((length, wide), f32),
            pltpu.HBM((count, heads, WIDTH, WIDTH), f32),
            pltpu.HBM((length, 3 * wide), f32),
        ],
        scratch_shapes=[
            pltpu.VMEM((heads, WIDTH, WIDTH), f32),
            pltpu.VMEM((HALO, 3 * wide), f32),
            pltpu.VMEM((HALO, WIDTH), f32),
            pltpu.VMEM((subs * CHUNK, width), f32),
        ],
        compiler_params=pltpu.CompilerParams(vmem_limit_bytes=48 * 1024 * 1024),
        cost_estimate=pl.CostEstimate(
            flops=2 * 160 * length * WIDTH * wide + 2 * length * model * width,
            bytes_accessed=2 * model * (length + width) + 4 * length * (width + 6 * wide),
            transcendentals=8 * length * wide,
        ),
        name="mixer_forward",
    )(*in_hbm(x, weights, seg_wide, conv_rows, neg_rate, gain))


def mixer_backward(proj, seg_wide, conv_rows, neg_rate, gain, rank, grads, saved):
    length, width = proj.shape
    heads = (width - WIDTH) // (4 * WIDTH)
    wide = heads * WIDTH
    count = length // CHUNK
    back = lambda i: count - 1 - i
    by_chunk = lambda cols: pl.BlockSpec((CHUNK, cols), lambda i, rank: (back(i), 0))
    before = lambda cols: pl.BlockSpec(
        (HALO, cols), lambda i, rank: (jnp.maximum(back(i) * (CHUNK // HALO) - 1, 0), 0)
    )
    whole = lambda rows, cols: pl.BlockSpec((rows, cols), lambda i, rank: (0, 0))
    part_count = grads[0].shape[0] // CHUNK

    def grad_block(other):
        def index(i, rank):
            first = (1 - rank[0] if other else rank[0]) * part_count
            return jnp.clip(back(i) - first, 0, part_count - 1), 0

        return pl.BlockSpec((CHUNK, wide), index)

    grad_blocks = [grad_block(False), grad_block(True)] if len(grads) == 2 else [by_chunk(wide)]
    grid_spec = pltpu.PrefetchScalarGridSpec(
        num_scalar_prefetch=1,
        grid=(count,),
        in_specs=[
            by_chunk(width), by_chunk(WIDTH), before(WIDTH), before(3 * wide),
            whole(12, wide), whole(1, WIDTH), whole(1, WIDTH),
            *grad_blocks,
            by_chunk(wide), by_chunk(wide), by_chunk(wide), by_chunk(wide),
            pl.BlockSpec((1, heads, WIDTH, WIDTH), lambda i, rank: (back(i), 0, 0, 0)),
            by_chunk(3 * wide),
        ],
        out_specs=[by_chunk(width), whole(12, wide), whole(1, WIDTH), whole(1, WIDTH)],
        scratch_shapes=[
            pltpu.VMEM((heads, WIDTH, WIDTH), f32),
            pltpu.VMEM((HALO, 3 * wide), f32),
        ],
    )
    return pl.pallas_call(
        functools.partial(backward_kernel, heads, len(grads)),
        grid_spec=grid_spec,
        out_shape=[
            pltpu.HBM((length, width), bf16),
            pltpu.HBM((12, wide), f32),
            pltpu.HBM((1, WIDTH), f32),
            pltpu.HBM((1, WIDTH), f32),
        ],
        compiler_params=pltpu.CompilerParams(vmem_limit_bytes=48 * 1024 * 1024),
        cost_estimate=pl.CostEstimate(
            flops=2 * 180 * length * WIDTH * wide,
            bytes_accessed=4 * length * (2 * width + 3 * wide),
            transcendentals=8 * length * wide,
        ),
        name="mixer_backward",
    )(rank, *in_hbm(proj, seg_wide, seg_wide, proj, conv_rows, neg_rate, gain, *grads, *saved))


def ffn_kernel(tiles, x_ref, dy_ref, w_ref, h_ref, g_ref, y_ref, dx_ref, y_sum, dx_sum):
    step = pl.program_id(0)

    @pl.when(step == 0)
    def _():
        y_sum[...] = jnp.zeros_like(y_sum)
        dx_sum[...] = jnp.zeros_like(dx_sum)

    def units(size):
        gate_up = dot(x_ref[...], w_ref[:, : 2 * size], NN)
        grad = dot(dy_ref[...], w_ref[:, 2 * size : 3 * size], NN)
        gate, up = gate_up[:, :size], gate_up[:, size:]
        gate_s = sigmoid(gate)
        act = gate * gate_s
        h_ref[:, :size] = (act * up).astype(bf16)
        g_ref[:, :size] = (grad * up * (gate_s + act * (1.0 - gate_s))).astype(bf16)
        g_ref[:, size : 2 * size] = (grad * act).astype(bf16)
        y_sum[...] += dot(h_ref[:, :size], w_ref[:, 2 * size : 3 * size], NT)
        dx_sum[...] += dot(g_ref[:, : 2 * size], w_ref[:, : 2 * size], NT)

    per_tile(tiles, step, units)

    @pl.when(step == len(tiles) - 1)
    def _():
        y_ref[...] = y_sum[...].astype(bf16)
        dx_ref[...] = dx_sum[...].astype(bf16)


def per_tile(tiles, step, units):
    if tiles[0] == tiles[-1]:
        units(tiles[0])
        return

    @pl.when(step < len(tiles) - 1)
    def _():
        units(tiles[0])

    @pl.when(step == len(tiles) - 1)
    def _():
        units(tiles[-1])


def ffn(x, dy, packed, tiles):
    rows, model = x.shape
    hidden = sum(tiles)
    whole = pl.BlockSpec((rows, model), lambda i: (0, 0))
    return pl.pallas_call(
        functools.partial(ffn_kernel, tiles),
        grid=(len(tiles),),
        in_specs=[whole, whole, pl.BlockSpec((model, 3 * tiles[0]), lambda i: (0, i))],
        out_specs=[
            pl.BlockSpec((rows, tiles[0]), lambda i: (0, i)),
            pl.BlockSpec((rows, 2 * tiles[0]), lambda i: (0, i)),
            whole,
            whole,
        ],
        out_shape=[
            pltpu.HBM((rows, hidden), bf16),
            pltpu.HBM((rows, 2 * hidden), bf16),
            pltpu.HBM((rows, model), bf16),
            pltpu.HBM((rows, model), bf16),
        ],
        scratch_shapes=[pltpu.VMEM((rows, model), f32), pltpu.VMEM((rows, model), f32)],
        compiler_params=pltpu.CompilerParams(vmem_limit_bytes=48 * 1024 * 1024),
        cost_estimate=pl.CostEstimate(
            flops=12 * rows * model * hidden,
            bytes_accessed=2 * (3 * model * hidden + rows * (4 * model + 3 * hidden)),
            transcendentals=rows * hidden,
        ),
        name="ffn",
    )(*in_hbm(x, dy, packed))


def turn_rows(core_ref, order, turned, source):
    half = len(order) // 2
    size = source.shape[0] // len(order)
    for at, block in enumerate(order):
        away = (block % 2 + 1 + core_ref[0]) % 2
        begin = (away * half + at % half) * size
        rows = pl.ds(pl.multiple_of(begin, size), size)
        turned[rows, :] = source[block * size : (block + 1) * size, :]


def ffn_grads_kernel(tiles, *refs):
    *inputs, out_ref, x_turned, dy_turned = refs
    count = len(inputs) // 4
    xs, dys, hs, gs = (inputs[at * count : (at + 1) * count] for at in range(4))
    step = pl.program_id(0)
    ends = [0]
    for x_ref in xs:
        ends.append(ends[-1] + x_ref.shape[0])
    lanes = [slice(first, last) for first, last in zip(ends, ends[1:])]

    @pl.when(step == 0)
    def _():
        for at, x_ref, dy_ref in zip(lanes, xs, dys):
            x_turned[:, at] = x_ref[...].T
            dy_turned[:, at] = dy_ref[...].T

    def units(size):
        up_grad, down_grad = 0.0, 0.0
        for at, h_ref, g_ref in zip(lanes, hs, gs):
            up_grad = up_grad + dot(x_turned[:, at], g_ref[:, : 2 * size], NN)
            down_grad = down_grad + dot(dy_turned[:, at], h_ref[:, :size], NN)
        out_ref[:, : 2 * size] = up_grad.astype(bf16)
        out_ref[:, 2 * size : 3 * size] = down_grad.astype(bf16)

    per_tile(tiles, step, units)


def ffn_grads(xs, dys, hs, gs, tiles):
    model = xs[0].shape[1]
    hidden = sum(tiles)
    total = sum(x.shape[0] for x in xs)
    whole = [pl.BlockSpec(x.shape, lambda i: (0, 0)) for x in xs]
    return pl.pallas_call(
        functools.partial(ffn_grads_kernel, tiles),
        grid=(len(tiles),),
        in_specs=whole
        + whole
        + [pl.BlockSpec((x.shape[0], tiles[0]), lambda i: (0, i)) for x in xs]
        + [pl.BlockSpec((x.shape[0], 2 * tiles[0]), lambda i: (0, i)) for x in xs],
        out_specs=pl.BlockSpec((model, 3 * tiles[0]), lambda i: (0, i)),
        out_shape=pltpu.HBM((model, 3 * hidden), bf16),
        scratch_shapes=[pltpu.VMEM((model, total), bf16), pltpu.VMEM((model, total), bf16)],
        compiler_params=pltpu.CompilerParams(vmem_limit_bytes=48 * 1024 * 1024),
        cost_estimate=pl.CostEstimate(
            flops=6 * total * model * hidden,
            bytes_accessed=2 * (3 * model * hidden + total * (2 * model + 3 * hidden)),
            transcendentals=0,
        ),
        name="ffn_grads",
    )(*in_hbm(*xs, *dys, *hs, *gs))


def turn_rows(core_ref, order, turned, source):
    half = len(order) // 2
    size = source.shape[0] // len(order)
    for at, block in enumerate(order):
        away = (block % 2 + 1 + core_ref[0]) % 2
        begin = (away * half + at % half) * size
        rows = pl.ds(pl.multiple_of(begin, size), size)
        turned[rows, :] = source[block * size : (block + 1) * size, :]


def mixer_grads_kernel(
    orders, split, main_steps, parts, core_ref, normed_ref, dproj_ref, conv_ref, *refs
):
    residual_refs, mixed_refs, refs = refs[:parts], refs[parts : 2 * parts], refs[2 * parts :]
    first_sent_ref, first_kept_ref, second_sent_ref, second_kept_ref, *refs = refs
    turned, conv_turned, *residuals_turned = refs
    step = pl.program_id(0)
    last = pl.num_programs(0) - 1
    first_order, second_order = orders
    count = len(first_order)
    size = normed_ref.shape[1] // count

    @pl.when(step == 0)
    def _():
        turn_rows(core_ref, first_order, turned, normed_ref[...].T)
        for residual_turned, residual_ref in zip(residuals_turned, residual_refs):
            turn_rows(core_ref, first_order, residual_turned, residual_ref[...].T)
        turn_rows(core_ref, first_order, conv_turned, conv_ref[...])

    def store(grads, lanes):
        grads = grads.astype(bf16)
        half = count // 2 * size

        @pl.when(step < split)
        def _():
            first_sent_ref[:, lanes] = grads[:half]
            first_kept_ref[:, lanes] = grads[half:]

        @pl.when(step >= split)
        def _():
            for to, block in enumerate(second_order[: count // 2]):
                at = first_order.index(block)
                to_rows = slice(to * size, (to + 1) * size)
                second_sent_ref[to_rows, lanes] = grads[at * size : (at + 1) * size]
                second_kept_ref[to_rows, lanes] = grads[half + at * size : half + (at + 1) * size]

    @pl.when(step < main_steps)
    def _():
        store(dot(turned[...], dproj_ref[...], NN), slice(None))

    @pl.when((step >= main_steps) & (step < last))
    def _():
        grads = 0.0
        for residual_turned, mixed_ref in zip(residuals_turned, mixed_refs):
            grads = grads + dot(residual_turned[...], mixed_ref[...], NN)
        store(grads, slice(None))

    @pl.when(step == last)
    def _():
        store(dot(turned[...], dproj_ref[:, :WIDTH], NN) + conv_turned[...], slice(0, WIDTH))


def mixer_grads(normed, residuals, dproj, mixed_parts, conv_block, core, orders):
    rows, model = normed.shape
    wide = mixed_parts[0].shape[1]
    parts = len(residuals)
    part_rows = residuals[0].shape[0]
    tile = 2 * WIDTH if wide % (2 * WIDTH) == 0 else WIDTH
    main_steps = 4 * wide // tile
    out_steps = wide // tile
    columns = 5 * wide + WIDTH
    split = (main_steps + out_steps + 1) * 5 // 11
    first = split * tile
    whole = lambda rows, cols: pl.BlockSpec((rows, cols), lambda i, core: (0, 0))
    mixed_block = pl.BlockSpec(
        (part_rows, tile), lambda i, core: (0, jnp.clip(i - main_steps, 0, out_steps - 1))
    )
    first_block = pl.BlockSpec((model // 2, tile), lambda i, core: (0, jnp.minimum(i, split - 1)))
    second_block = pl.BlockSpec((model // 2, tile), lambda i, core: (0, jnp.maximum(i - split, 0)))
    first_shape = pltpu.HBM((model // 2, first), bf16)
    second_shape = pltpu.HBM((model // 2, columns - first), bf16)
    return pl.pallas_call(
        functools.partial(mixer_grads_kernel, orders, split, main_steps, parts),
        grid_spec=pltpu.PrefetchScalarGridSpec(
            num_scalar_prefetch=1,
            grid=(main_steps + out_steps + 1,),
            in_specs=[
                whole(rows, model),
                pl.BlockSpec((rows, tile), lambda i, core: (0, jnp.minimum(i, main_steps))),
                whole(model, WIDTH),
            ]
            + [whole(part_rows, model)] * parts
            + [mixed_block] * parts,
            out_specs=[first_block, first_block, second_block, second_block],
            scratch_shapes=[
                pltpu.VMEM((model, rows), bf16),
                pltpu.VMEM((model, WIDTH), f32),
            ]
            + [pltpu.VMEM((model, part_rows), bf16)] * parts,
        ),
        out_shape=[first_shape, first_shape, second_shape, second_shape],
        compiler_params=pltpu.CompilerParams(vmem_limit_bytes=40 * 1024 * 1024),
        cost_estimate=pl.CostEstimate(
            flops=2 * rows * model * columns,
            bytes_accessed=2 * (2 * rows * model + (rows + model) * columns),
            transcendentals=0,
        ),
        name="mixer_grads",
    )(core, *in_hbm(normed, dproj, conv_block, *residuals, *mixed_parts))


def rms_norm(values, scales):
    return values * lax.rsqrt(jnp.mean(values * values, axis=-1, keepdims=True) + norm_eps) * scales


def first_norm(values, gains):
    return rms_norm(values, gains[0])


def second_norm(values, gains):
    return rms_norm(values, gains[1])


def contract_last(operand, other):
    return lax.dot_general(
        operand, other, (((1,), (1,)), ((), ())), preferred_element_type=jnp.float32
    )


def contract_first(operand, other):
    return lax.dot_general(
        operand, other, (((0,), (0,)), ((), ())), preferred_element_type=jnp.float32
    )


def swap(rows):
    return lax.ppermute(rows, "tensor", [(0, 1), (1, 0)])


def sum_steps(axis):
    size = lax.axis_size(axis)
    if size & (size - 1):
        return [lambda values: lax.psum(values, axis)]

    def step(bit, values):
        def across(mask):
            return lax.ppermute(values, axis, [(i, i ^ mask) for i in range(size)])

        if 2 * bit < size:
            return (values + across(bit)) + (across(2 * bit) + across(3 * bit))
        return values + across(bit)

    return [functools.partial(step, 1 << at) for at in range(0, size.bit_length() - 1, 2)]


def hidden_tiles(hidden):
    if hidden % WIDTH:
        return (hidden,)
    size = min(4 * WIDTH, hidden)
    return (size,) * (hidden // size) + ((hidden % size,) if hidden % size else ())


def pack_tiles(parts, tiles):
    blocks = []
    at = 0
    for size in tiles:
        blocks += [part[:, at : at + size] for part in parts]
        at += size
    return jnp.concatenate(blocks, axis=1)


def unpack_tiles(packed, tiles, count):
    parts = [[] for _ in range(count)]
    at = 0
    for size in tiles:
        for part in parts:
            part.append(packed[:, at : at + size])
            at += size
    return [jnp.concatenate(part, axis=1) for part in parts]


def ffn_plain(x, dy, packed, tiles):
    gate_w, up_w, down_w = unpack_tiles(packed, tiles, 3)
    gate = jnp.dot(x, gate_w, preferred_element_type=f32)
    up = jnp.dot(x, up_w, preferred_element_type=f32)
    grad = jnp.dot(dy, down_w, preferred_element_type=f32)
    gate_s = sigmoid(gate)
    act = gate * gate_s
    hidden = (act * up).astype(bf16)
    gate_grad = (grad * up * (gate_s + act * (1.0 - gate_s))).astype(bf16)
    up_grad = (grad * act).astype(bf16)
    share = contract_last(hidden, down_w).astype(bf16)
    dx = (contract_last(gate_grad, gate_w) + contract_last(up_grad, up_w)).astype(bf16)
    return hidden, jnp.concatenate([gate_grad, up_grad], axis=1), share, dx


def ffn_grads_plain(x, dy, hidden, grads, tiles):
    size = hidden.shape[1]
    parts = [
        contract_first(x, grads[:, :size]),
        contract_first(x, grads[:, size:]),
        contract_first(dy, hidden),
    ]
    return pack_tiles([part.astype(bf16) for part in parts], tiles)


def bit_orders(size):
    bits = list(range(size.bit_length() - 1))
    return bits, bits[:1] + bits[2:] + bits[1:2]


def block_order(size, bits):
    return sorted(range(size), key=lambda i: [(i >> bit) & 1 for bit in bits])


def outgoing(terms, bit):
    mine = lax.axis_index("dp") >> bit & 1
    half = terms[0].shape[0] // 2
    total = 0.0
    for term in terms:
        total = total + lax.dynamic_slice_in_dim(term, (1 - mine) * half, half).astype(f32)
    return total.astype(bf16)


def settle(terms, bit, sent):
    mine = lax.axis_index("dp") >> bit & 1
    half = terms[0].shape[0] // 2
    own = [lax.dynamic_slice_in_dim(term, mine * half, half) for term in terms]
    return own + [flip(sent, bit)]


def flip(values, bit):
    size = lax.axis_size("dp")
    return lax.ppermute(values, "dp", [(i, i ^ (1 << bit)) for i in range(size)])


def local(
    tokens,
    segment_ids,
    norm_gains,
    w_mixer_in,
    w_rates,
    conv_weight,
    a_log,
    out_gain,
    w_output,
    w_gate_up,
    w_down,
    cotangent,
):
    dp_size = lax.axis_size("dp")
    pair = lax.axis_size("tensor") == 2
    tensor_rank = lax.axis_index("tensor")
    rows_here, _, heads, _ = w_mixer_in.shape
    model_width = rows_here * dp_size
    wide = heads * WIDTH
    hidden_here = w_gate_up.shape[2]
    tiles = hidden_tiles(hidden_here)
    kernels = hidden_here % WIDTH == 0
    taps_here = conv_weight.shape[3]
    own_rows = tokens.shape[1]
    projected_width = 4 * wide + WIDTH

    def gather_rows(rows):
        return lax.all_gather(rows, "tensor", axis=0, tiled=True)

    def scatter_rows(product):
        return lax.psum_scatter(product.astype(bf16), "tensor", scatter_dimension=0, tiled=True)

    def in_order(own, other):
        first = tensor_rank == 0
        return jnp.concatenate([jnp.where(first, own, other), jnp.where(first, other, own)], axis=0)

    def own_and_other(rows):
        own = lax.dynamic_slice_in_dim(rows, tensor_rank * own_rows, own_rows)
        return own, lax.dynamic_slice_in_dim(rows, (1 - tensor_rank) * own_rows, own_rows)

    conv_block = jnp.pad(
        conv_weight.transpose(3, 0, 1, 2).reshape(taps_here, 12 * heads),
        ((0, rows_here - taps_here), (0, WIDTH - 14 * heads)),
    )
    mixer_pack = jnp.concatenate(
        [
            w_mixer_in.reshape(rows_here, -1),
            w_rates.reshape(rows_here, -1),
            conv_block,
            w_output.T,
        ],
        axis=1,
    )
    mix_full = lax.all_gather(mixer_pack, "dp", axis=0, tiled=True)
    ffn_pack = pack_tiles([w_gate_up[:, 0], w_gate_up[:, 1], w_down.T], tiles)
    ffn_full = lax.all_gather(ffn_pack, "dp", axis=0, tiled=True)
    out_mine = mix_full[:, projected_width:]
    conv_at = 4 * wide + 2 * heads
    conv_rows = (
        mix_full[:, conv_at : conv_at + 12 * heads]
        .reshape(dp_size, rows_here, 12 * heads)[:, :taps_here]
        .reshape(dp_size * taps_here, 12 * heads)
        .T.reshape(12, wide)
        .astype(f32)
    )
    segment = jnp.broadcast_to(segment_ids[0][:, None].astype(f32), (segment_ids.shape[1], WIDTH))
    neg_rate = jnp.pad(
        -jnp.exp(lax.dynamic_slice_in_dim(a_log, tensor_rank * heads, heads)), (0, WIDTH - heads)
    )[None]
    gain_row = out_gain[None]

    grad_own = cotangent[0]
    inputs = tokens[0].astype(f32)
    normed, first_back = jax.vjp(first_norm, inputs, norm_gains)
    normed = normed.astype(bf16)
    if pair:
        normed_other = swap(normed)
        grad_sent, normed_other, segment, neg_rate = lax.optimization_barrier(
            (grad_own, normed_other, segment, neg_rate)
        )
        grad_other = swap(grad_sent)
        normed_all, grad_other, out_sent = lax.optimization_barrier(
            (in_order(normed, normed_other), grad_other, out_mine)
        )
        out_other = swap(out_sent)
    else:
        normed_all = gather_rows(normed)
    projected, mixed, *saved = mixer_forward(
        normed_all, mix_full, heads, segment, conv_rows, neg_rate, gain_row
    )
    if pair:
        mixed, out_other = lax.optimization_barrier((mixed, out_other))
        mixed_own, mixed_theirs = own_and_other(mixed)
        share = contract_last(mixed_own, out_mine) + contract_last(swap(mixed_theirs), out_other)
    else:
        share = scatter_rows(contract_last(mixed, out_mine)).astype(f32)
    residual = inputs + share
    normed_ffn, second_back = jax.vjp(second_norm, residual, norm_gains)
    normed_ffn = normed_ffn.astype(bf16)
    one_ffn = ffn if kernels else ffn_plain
    if pair:
        half = own_rows // 2
        x_others = [swap(normed_ffn[:half]), swap(normed_ffn[half:])]
        others = []
        for at, x_other in enumerate(x_others):
            others.append(one_ffn(x_other, grad_other[at * half : (at + 1) * half], ffn_full, tiles))
        received = [swap(other[3]) for other in others]
        done = [one_ffn(normed_ffn, grad_own, ffn_full, tiles)] + others
        x_parts = [normed_ffn] + x_others
        dy_parts = [grad_own, grad_other[:half], grad_other[half:]]
        dx = done[0][3].astype(f32) + jnp.concatenate(received, axis=0).astype(f32)
    else:
        x_parts = [gather_rows(normed_ffn)]
        dy_parts = [gather_rows(grad_own)]
        done = [one_ffn(x_parts[0], dy_parts[0], ffn_full, tiles)]
        dx = scatter_rows(done[0][3]).astype(f32)
    h_parts, g_parts, y_parts, _ = zip(*done)
    core = lax.axis_index("dp") % 2
    bits = bit_orders(dp_size)
    orders = [block_order(dp_size, order) for order in bits]
    if kernels:
        ffn_sums = ffn_grads(x_parts, dy_parts, h_parts, g_parts, tiles)
    else:
        ffn_sums = ffn_grads_plain(x_parts[0], dy_parts[0], h_parts[0], g_parts[0], tiles)
    residual_part, second_gains = second_back(dx)
    residual_grad = grad_own.astype(f32) + residual_part
    residual_low = residual_grad.astype(bf16)
    if pair:
        grad_theirs = jnp.dot(residual_low, out_other, preferred_element_type=f32).astype(bf16)
        grad_mine = jnp.dot(residual_low, out_mine, preferred_element_type=f32).astype(bf16)
        grad_mine, mixed_grad, ffn_sums, residual_sent, y_first, y_last = lax.optimization_barrier(
            (
                grad_mine,
                swap(grad_theirs),
                ffn_sums,
                residual_low,
                y_parts[1],
                y_parts[2],
            )
        )
        mixed_grads = [grad_mine, mixed_grad]
        residuals = [residual_low, swap(residual_sent)]
        mixed_parts = [mixed_own, mixed_theirs]
    else:
        residuals = [gather_rows(residual_low)]
        mixed_grads = [jnp.dot(residuals[0], out_mine, preferred_element_type=f32).astype(bf16)]
        mixed_parts = [mixed]
    ffn_owned = lax.psum_scatter(ffn_sums, "dp", scatter_dimension=0, tiled=True)
    projection_grad, conv_grad, log_grad, gain_grad = mixer_backward(
        projected, segment, conv_rows, neg_rate, gain_row, tensor_rank[None], mixed_grads, saved
    )
    conv_grad = jnp.pad(
        conv_grad.reshape(12 * heads, WIDTH).T.reshape(dp_size, taps_here, 12 * heads),
        ((0, 0), (0, rows_here - taps_here), (2 * heads, WIDTH - 14 * heads)),
    ).reshape(model_width, WIDTH)
    mix_rows = mix_full[:, :projected_width]
    first_sent, first_kept, second_sent, second_kept = mixer_grads(
        normed_all, residuals, projection_grad, mixed_parts, conv_grad, core[None], orders
    )
    projection_grad, _, _ = lax.optimization_barrier((projection_grad, first_sent, second_sent))
    second = [second_kept, flip(second_sent, 0)]
    first = [first_kept, flip(first_sent, 0)]
    second_out = outgoing(second, bits[1][1])
    first_out = outgoing(first, bits[0][1])
    if pair:
        grad_here, grad_there = own_and_other(projection_grad)
        sent = contract_last(grad_there, mix_rows).astype(bf16)
        first_out, second_out, sent = lax.optimization_barrier((first_out, second_out, sent))
        received = swap(sent)
    else:
        received = scatter_rows(contract_last(projection_grad, mix_rows))
    first = settle(first, bits[0][1], first_out)
    second = settle(second, bits[1][1], second_out)
    first_out = outgoing(first, bits[0][2])
    second_out = outgoing(second, bits[1][2])
    if pair:
        y_first, y_last, _ = lax.optimization_barrier((y_first, y_last, second_out))
        received, grad_here, _ = lax.optimization_barrier((received, grad_here, first_out))
        y_other = jnp.concatenate([swap(y_first), swap(y_last)], axis=0)
        mixer_input_grad = received.astype(f32) + contract_last(grad_here, mix_rows)
    else:
        y_other = scatter_rows(y_parts[0])
        mixer_input_grad = received.astype(f32)
    first = settle(first, bits[0][2], first_out)
    second = settle(second, bits[1][2], second_out)
    input_part, first_gains = first_back(mixer_input_grad)
    input_grad = (residual_grad + input_part).astype(bf16)[None]
    log_full = lax.dynamic_update_slice_in_dim(
        jnp.zeros(a_log.shape, f32), log_grad[0, :heads], tensor_rank * heads, 0
    )
    last_row = jnp.concatenate([gain_grad[0], log_full])
    last_row = jnp.pad(last_row, (0, model_width - last_row.shape[0]))[None]
    small = jnp.concatenate([first_gains + second_gains, last_row], axis=0)
    for one, other in zip(bits[0][3:], bits[1][3:]):
        last_out = first_out
        first_out = outgoing(first, one)
        second_out = outgoing(second, other)
        second_out, _ = lax.optimization_barrier((second_out, last_out))
        small, _ = lax.optimization_barrier((small, first_out))
        first = settle(first, one, first_out)
        second = settle(second, other, second_out)
    y = y_other.astype(f32)
    if pair:
        y = y + y_parts[0].astype(f32)
    out_tokens = (residual + y).astype(bf16)[None]
    *steps, last_step = sum_steps("tensor") + sum_steps("dp")
    for step in steps:
        small = step(small)
    gate_grad, up_grad, down_grad = unpack_tiles(ffn_owned, tiles, 3)
    up_owned = jnp.stack([gate_grad, up_grad], axis=1).astype(f32)
    down_owned = down_grad.T.astype(f32)
    small = last_step(small)
    first[-1], out_tokens, up_owned, down_owned = lax.optimization_barrier(
        (first[-1], out_tokens, up_owned, down_owned)
    )
    mix_owned = jnp.concatenate(
        [sum(term.astype(f32) for term in terms) for terms in (first, second)], axis=1
    )
    rates = mix_owned[:, 5 * wide :]
    return (
        out_tokens,
        input_grad,
        small[:2],
        mix_owned[:, : 4 * wide].reshape(w_mixer_in.shape),
        rates[:, : 2 * heads].reshape(w_rates.shape),
        rates[:taps_here, 2 * heads : 14 * heads]
        .reshape(taps_here, 3, 4, heads)
        .transpose(1, 2, 3, 0),
        small[2, WIDTH : WIDTH + a_log.shape[0]],
        small[2, :WIDTH],
        mix_owned[:, 4 * wide : 5 * wide].T,
        up_owned,
        down_owned,
    )


def solution(mesh):
    in_specs = (
        P("dp", "tensor", None),
        P("dp", None),
        P(),
        P("dp", None, "tensor", None),
        P("dp", None, "tensor"),
        P(None, None, "tensor", "dp"),
        P(),
        P(),
        P("tensor", "dp"),
        P("dp", None, "tensor"),
        P("tensor", "dp"),
        P("dp", "tensor", None),
    )
    out_specs = (
        P("dp", "tensor", None),
        P("dp", "tensor", None),
        P(),
        P("dp", None, "tensor", None),
        P("dp", None, "tensor"),
        P(None, None, "tensor", "dp"),
        P(),
        P(),
        P("tensor", "dp"),
        P("dp", None, "tensor"),
        P("tensor", "dp"),
    )
    return jax.shard_map(local, mesh=mesh, in_specs=in_specs, out_specs=out_specs, check_vma=False)
```

```python
import functools

import jax
import jax.numpy as jnp
from jax import lax
from jax.experimental import pallas as pl
from jax.experimental.pallas import tpu as pltpu
from jax.sharding import PartitionSpec as P

CHUNK = 128
WIDTH = 128
HALO = 8
COLUMN_TILE = 256
norm_eps = 1e-05
unit_eps = 1e-06
f32 = jnp.float32
bf16 = jnp.bfloat16

NN = ((1,), (0,))
NT = ((1,), (1,))
TN = ((0,), (0,))


def in_hbm(*arrays):
    return [pltpu.with_memory_space_constraint(array, pltpu.HBM) for array in arrays]


def dot(left, right, dims):
    return lax.dot_general(
        left.astype(bf16), right.astype(bf16), (dims, ((), ())), preferred_element_type=f32
    )


def dot_exact(left, right, dims):
    return lax.dot_general(
        left, right, (dims, ((), ())), precision=lax.Precision.HIGHEST, preferred_element_type=f32
    )


def sigmoid(value):
    return 0.5 * jnp.tanh(0.5 * value) + 0.5


def softplus(value):
    return jnp.maximum(value, 0.0) + jnp.log(1.0 + jnp.exp(-jnp.abs(value)))


def shifted(rows, offset):
    return pltpu.roll(rows, offset, 0)[HALO:] if offset else rows[HALO:]


def conv_terms(rows, keeps):
    return [rows[HALO:]] + [
        jnp.where(keeps[offset], shifted(rows, offset), 0.0) for offset in range(1, 4)
    ]


def conv_sum(terms, conv_ref, part, lanes):
    total = None
    for offset in range(4):
        weight = conv_ref[pl.ds(part * 4 + 3 - offset, 1), lanes]
        term = weight * terms[offset]
        total = term if total is None else total + term
    return total


def lane_column(values, lane):
    return jnp.broadcast_to(values[:, lane : lane + 1], values.shape)


def grids():
    row = lax.broadcasted_iota(jnp.int32, (CHUNK, CHUNK), 0)
    col = lax.broadcasted_iota(jnp.int32, (CHUNK, CHUNK), 1)
    return row, col


def level_masks(row, col):
    masks = []
    shift = 0
    while (1 << shift) < CHUNK:
        near = (row >> (shift + 1)) == (col >> (shift + 1))
        apart = (row >> shift) != (col >> shift)
        masks.append(near & apart)
        shift += 1
    return masks


def unit_lower_inverses(lowers, row, col, beside):
    masks = level_masks(row, col)
    beside = list(beside)
    share = -(-len(beside) // (2 * len(masks[1:])))

    def place():
        for work in beside[:share]:
            work()
        del beside[:share]

    identity = jnp.where(row == col, 1.0, 0.0).astype(f32)
    inverses = [identity - jnp.where(masks[0], lower, 0.0) for lower in lowers]
    for mask in masks[1:]:
        blocks = [jnp.where(mask, lower, 0.0).astype(bf16) for lower in lowers]
        low = [inverse.astype(bf16) for inverse in inverses]
        firsts = [dot(inverse, block, NN) for inverse, block in zip(low, blocks)]
        place()
        firsts = [dot(first, inverse, NN) for first, inverse in zip(firsts, low)]
        place()
        inverses = [inverse - first for inverse, first in zip(inverses, firsts)]
    return inverses


def chunk_scales(heads, rates, neg_rate, seg, last_seen, row, col):
    steps = neg_rate * softplus(rates)
    lower_ones = jnp.where(row >= col, 1.0, 0.0).astype(f32)
    cumulative = dot_exact(lower_ones, steps, NN)
    cumulative_rows = cumulative.T
    betas = sigmoid(rates)
    seg_rows = seg.T
    same = seg == seg_rows
    within = same & (row >= col)
    strict = same & (row > col)
    carry = seg == last_seen
    ends = seg == seg[CHUNK - 1 :, :]
    scales = []
    for head in range(heads):
        cum = lane_column(cumulative, head)
        cum_row = cumulative_rows[head : head + 1, :]
        gap = jnp.exp(jnp.minimum(cum - cum_row, 0.0))
        last = cum[CHUNK - 1 :, :]
        scales.append(
            dict(
                beta=lane_column(betas, heads + head),
                within=jnp.where(within, gap, 0.0),
                strict=jnp.where(strict, gap, 0.0),
                start=jnp.where(carry, jnp.exp(cum), 0.0),
                end=jnp.where(ends, jnp.exp(jnp.minimum(last - cum, 0.0)), 0.0),
                keep=jnp.where(carry[CHUNK - 1 :, :], jnp.exp(last), 0.0),
            )
        )
    return scales, steps, betas


def forward_kernel(
    heads, subs, x_ref, weight_ref, seg_ref, conv_ref, rate_ref, gain_ref,
    proj_ref, mixed_ref, inverse_ref, w_ref, pseudo_ref, out_ref, state_ref, conv_out_ref,
    state, halo, seg_halo, ahead,
):
    step = pl.program_id(0)
    block_rows = subs * CHUNK
    width = proj_ref.shape[1]

    def project(block, lanes):
        rows = x_ref[pl.ds(pl.multiple_of(block * block_rows, block_rows), block_rows), :]
        ahead[:, lanes] = dot(rows, weight_ref[:, lanes], NN)

    column_tiles = [
        slice(at, min(at + COLUMN_TILE, width)) for at in range(0, width, COLUMN_TILE)
    ]

    @pl.when(step == 0)
    def _():
        state[...] = jnp.zeros_like(state)
        halo[...] = jnp.zeros_like(halo)
        seg_halo[...] = jnp.full_like(seg_halo, -1.0)
        for lanes in column_tiles:
            project(0, lanes)

    proj_ref[...] = ahead[...]
    following = jnp.minimum(step + 1, pl.num_programs(0) - 1)
    row, col = grids()
    wide = heads * WIDTH
    each = range(heads)
    items = [(sub, head) for sub in range(subs) for head in each]
    head_lanes = [slice(head * WIDTH, (head + 1) * WIDTH) for head in each]
    chunk_rows = [slice(sub * CHUNK, (sub + 1) * CHUNK) for sub in range(subs)]

    def with_halo(ref, before, sub, lanes):
        if sub:
            return ref[sub * CHUNK - HALO : (sub + 1) * CHUNK, lanes]
        return jnp.concatenate([before[:, lanes], ref[:CHUNK, lanes]], axis=0)

    keeps, scales = [], {}
    for sub in range(subs):
        seg_rows = with_halo(seg_ref, seg_halo, sub, slice(None))
        seg = seg_rows[HALO:]
        keeps.append([None] + [shifted(seg_rows, offset) == seg for offset in range(1, 4)])
        rates = proj_ref[chunk_rows[sub], 4 * wide : 4 * wide + WIDTH]
        found, _, _ = chunk_scales(
            heads, rates, rate_ref[...], seg, seg_rows[HALO - 1 : HALO, :], row, col
        )
        for head in each:
            scales[sub, head] = found[head]

    def signal(part, item):
        sub, head = item
        at = part * wide + head * WIDTH
        lanes = slice(at, at + WIDTH)
        terms = conv_terms(with_halo(proj_ref, halo, sub, lanes), keeps[sub])
        total = conv_sum(terms, conv_ref, part, head_lanes[head])
        conv_out_ref[chunk_rows[sub], lanes] = total
        return total * sigmoid(total)

    def unit(rows):
        return rows * lax.rsqrt(jnp.sum(rows * rows, axis=-1, keepdims=True) + unit_eps)

    keys = {item: signal(1, item) for item in items}
    keys = {item: unit(keys[item]) for item in items}
    keys_low = {item: keys[item].astype(bf16) for item in items}
    lowers = [
        dot(keys_low[item], keys_low[item], NT) * (scales[item]["strict"] * scales[item]["beta"])
        for item in items
    ]
    queries, scores, targets, gates, ends = {}, {}, {}, {}, {}

    def query_of(item):
        queries[item] = unit(signal(0, item)) * WIDTH**-0.5

    def scores_of(item):
        scores[item] = (
            dot(queries[item], keys_low[item], NT) * scales[item]["within"]
        ).astype(bf16)
        queries[item] = (scales[item]["start"] * queries[item]).astype(bf16)

    def target_of(item):
        beta = scales[item]["beta"]
        targets[item] = jnp.concatenate(
            [
                (beta * signal(2, item)).astype(bf16),
                (beta * scales[item]["start"] * keys[item]).astype(bf16),
            ],
            axis=1,
        )

    def gate_of(item):
        sub, head = item
        gate = proj_ref[chunk_rows[sub], 3 * wide + head * WIDTH : 3 * wide + (head + 1) * WIDTH]
        gates[item] = gain_ref[...] * gate * sigmoid(gate)
        ends[item] = (scales[item]["end"] * keys[item]).astype(bf16)

    beside = [
        functools.partial(work, item)
        for work in (query_of, target_of, scores_of, gate_of)
        for item in items
    ]
    for at, lanes in enumerate(column_tiles):
        place = at * (len(beside) // len(column_tiles) + 1)
        beside.insert(place, functools.partial(project, following, lanes))
    inverses = unit_lower_inverses(lowers, row, col, beside)
    inverses = {item: inverse.astype(bf16) for item, inverse in zip(items, inverses)}
    halo[...] = proj_ref[subs * CHUNK - HALO :, : 3 * wide]
    seg_halo[...] = seg_ref[subs * CHUNK - HALO :, :]
    solved = {item: dot(inverses[item], targets[item], NN) for item in items}
    carried = {item: solved[item][:, WIDTH:].astype(bf16) for item in items}
    memories = [state[head] for head in each]
    for sub in range(subs):
        rows = chunk_rows[sub]
        reads = [
            dot(
                jnp.concatenate([carried[sub, head], queries[sub, head]], axis=0),
                memories[head],
                NN,
            )
            for head in each
        ]
        pseudos = [
            (solved[sub, head][:, :WIDTH] - reads[head][:CHUNK]).astype(bf16) for head in each
        ]
        updates = [dot(ends[sub, head], pseudos[head], TN) for head in each]
        outputs = [
            dot(scores[sub, head], pseudos[head], NN) + reads[head][CHUNK:] for head in each
        ]
        for head, lanes in enumerate(head_lanes):
            state_ref[sub, head] = memories[head]
            memories[head] = scales[sub, head]["keep"] * memories[head] + updates[head]
            inverse_ref[rows, lanes] = inverses[sub, head]
            w_ref[rows, lanes] = carried[sub, head]
            pseudo_ref[rows, lanes] = pseudos[head]
            output = outputs[head]
            out_ref[rows, lanes] = output
            inv_rms = lax.rsqrt(jnp.mean(output * output, axis=-1, keepdims=True) + norm_eps)
            mixed_ref[rows, lanes] = (output * inv_rms * gates[sub, head]).astype(bf16)
    for head in each:
        state[head] = memories[head]


def backward_kernel(
    heads, parts, rank_ref, proj_ref, seg_ref, seg_before_ref, before_ref, conv_ref, rate_ref,
    gain_ref, *refs
):
    grad_refs, refs = refs[:parts], refs[parts:]
    backward_steps(
        heads, rank_ref, proj_ref, seg_ref, seg_before_ref, before_ref, conv_ref, rate_ref,
        gain_ref, grad_refs, *refs
    )


def backward_steps(
    heads, rank_ref, proj_ref, seg_ref, seg_before_ref, before_ref, conv_ref, rate_ref, gain_ref,
    grad_refs, inverse_ref, w_ref, pseudo_ref, out_ref, state_ref, conv_out_ref,
    dproj_ref, dconv_ref, drate_ref, dgain_ref,
    dstate, carry_halo,
):
    step = pl.program_id(0)
    first = step == pl.num_programs(0) - 1

    @pl.when(step == 0)
    def _():
        dstate[...] = jnp.zeros_like(dstate)
        carry_halo[...] = jnp.zeros_like(carry_halo)
        dconv_ref[...] = jnp.zeros_like(dconv_ref)
        drate_ref[...] = jnp.zeros_like(drate_ref)
        dgain_ref[...] = jnp.zeros_like(dgain_ref)

    row, col = grids()
    seg = seg_ref[...]
    seg_before = jnp.where(first, -1.0, seg_before_ref[...])
    seg_rows = jnp.concatenate([seg_before, seg], axis=0)
    keeps = [None] + [shifted(seg_rows, offset) == seg for offset in range(1, 4)]
    last_seen = seg_before[HALO - 1 :, :]
    wide = heads * WIDTH
    rates = proj_ref[:, 4 * wide : 4 * wide + WIDTH]
    neg_rate = rate_ref[...]
    scales, steps, betas = chunk_scales(heads, rates, neg_rate, seg, last_seen, row, col)

    def signal(part, head):
        at = part * wide + head * WIDTH
        total = conv_out_ref[:, at : at + WIDTH]
        return total, sigmoid(total)

    def signal_back(part, head, total, gate, grad):
        grad = grad * (gate * (1.0 + total * (1.0 - gate)))
        at = part * wide + head * WIDTH
        lanes = slice(at, at + WIDTH)
        head_lanes = slice(head * WIDTH, (head + 1) * WIDTH)
        rows = proj_ref[:, lanes]
        rows_before = before_ref[:, lanes]
        spread, spread_before = None, None
        for offset in range(4):
            tap = pl.ds(part * 4 + 3 - offset, 1)
            weight = conv_ref[tap, head_lanes]
            if offset:
                back = jnp.where(keeps[offset], grad, 0.0)
                back = jnp.concatenate([jnp.zeros((HALO, WIDTH), f32), back], axis=0)
                back = pltpu.roll(back, CHUNK + HALO - offset, 0)
                back_before, back = back[:HALO], back[HALO:]
                product = jnp.sum(back * rows, axis=0, keepdims=True) + jnp.sum(
                    back_before * rows_before, axis=0, keepdims=True
                )
                spread = spread + weight * back
                before = weight * back_before
                spread_before = before if spread_before is None else spread_before + before
            else:
                product = jnp.sum(grad * rows, axis=0, keepdims=True)
                spread = weight * grad
            dconv_ref[tap, head_lanes] += product
        tail = spread[CHUNK - HALO :] + carry_halo[:, lanes]
        dproj_ref[:, lanes] = jnp.concatenate([spread[: CHUNK - HALO], tail], axis=0).astype(bf16)
        carry_halo[:, lanes] = spread_before

    lane = col
    cum_columns = jnp.zeros((CHUNK, WIDTH), f32)
    cum_rows = jnp.zeros((CHUNK, CHUNK), f32)
    dbeta_columns = jnp.zeros((CHUNK, WIDTH), f32)
    dgain = jnp.zeros((1, WIDTH), f32)
    each = range(heads)
    head_lanes = [slice(head * WIDTH, (head + 1) * WIDTH) for head in each]
    gain = gain_ref[...]
    beta, start, end, keep, within, strict = (
        [scale[name] for scale in scales]
        for name in ("beta", "start", "end", "keep", "within", "strict")
    )
    memory = [state_ref[0, head] for head in each]
    dmemory = [dstate[head] for head in each]
    inverse = [inverse_ref[:, lanes] for lanes in head_lanes]
    pseudo = [pseudo_ref[:, lanes] for lanes in head_lanes]

    q_total, q_gate = zip(*[signal(0, head) for head in each])
    k_total, k_gate = zip(*[signal(1, head) for head in each])
    q_act = [total * gate for total, gate in zip(q_total, q_gate)]
    k_act = [total * gate for total, gate in zip(k_total, k_gate)]
    q_norm = [lax.rsqrt(jnp.sum(act * act, axis=-1, keepdims=True) + unit_eps) for act in q_act]
    k_norm = [lax.rsqrt(jnp.sum(act * act, axis=-1, keepdims=True) + unit_eps) for act in k_act]
    q_unit = [act * norm for act, norm in zip(q_act, q_norm)]
    key = [act * norm for act, norm in zip(k_act, k_norm)]
    query = [unit * WIDTH**-0.5 for unit in q_unit]
    both = [
        dot(jnp.concatenate([key[h].astype(bf16), query[h].astype(bf16)], axis=0), key[h], NT)
        for h in each
    ]

    half = pl.num_programs(0) // 2
    from_own = (pl.num_programs(0) - 1 - step) // half == rank_ref[0]
    dout = []
    for head, lanes in enumerate(head_lanes):
        gate_at = slice(3 * wide + head * WIDTH, 3 * wide + (head + 1) * WIDTH)
        gate = proj_ref[:, gate_at]
        gate_s = sigmoid(gate)
        gate_act = gate * gate_s
        grad = grad_refs[0][:, lanes].astype(f32)
        if len(grad_refs) == 2:
            grad = jnp.where(from_own, grad, grad_refs[1][:, lanes].astype(f32))
        output = out_ref[:, lanes]
        inv_rms = lax.rsqrt(jnp.mean(output * output, axis=-1, keepdims=True) + norm_eps)
        unit = output * inv_rms
        grad_unit = grad * unit
        dgain = dgain + jnp.sum(grad_unit * gate_act, axis=0, keepdims=True)
        dproj_ref[:, gate_at] = (
            grad_unit * gain * (gate_s * (1.0 + gate * (1.0 - gate_s)))
        ).astype(bf16)
        dunit = grad * (gain * gate_act)
        dout.append(
            inv_rms * (dunit - unit * jnp.mean(dunit * unit, axis=-1, keepdims=True))
        )

    lower_raw = [both[h][:CHUNK] * strict[h] for h in each]
    lower = [lower_raw[h] * beta[h] for h in each]
    scores = [both[h][CHUNK:] * within[h] for h in each]
    dout_low = [value.astype(bf16) for value in dout]
    from_scores = [dot(scores[h], dout_low[h], TN) for h in each]
    from_end = [dot(end[h] * key[h], dmemory[h], NN) for h in each]
    dpseudo = [(from_scores[h] + from_end[h]).astype(bf16) for h in each]
    updates = [
        dot(
            jnp.concatenate(
                [(start[h] * query[h]).astype(bf16), -w_ref[:, head_lanes[h]]], axis=0
            ),
            jnp.concatenate([dout_low[h], dpseudo[h]], axis=0),
            TN,
        )
        for h in each
    ]
    dkey_end = [end[h] * dot(pseudo[h], dmemory[h], NT) for h in each]
    for h in each:
        dstate[h] = keep[h] * dmemory[h] + updates[h]
    solved = [dot(inverse[h], dpseudo[h], TN) for h in each]
    grads = [jnp.concatenate([dout_low[h], solved[h].astype(bf16)], axis=0) for h in each]
    reads = [dot(grads[h], memory[h], NT) for h in each]
    by_pseudo = [dot(grads[h], pseudo[h], NT) for h in each]
    near = [(-by_pseudo[h][CHUNK:] * (strict[h] * beta[h])).astype(bf16) for h in each]
    far = [(by_pseudo[h][:CHUNK] * within[h]).astype(bf16) for h in each]
    nears = [jnp.concatenate([near[h], far[h]], axis=0) for h in each]
    toward = [dot(nears[h], key[h], NN) for h in each]
    turned = [
        dot(
            nears[h],
            jnp.concatenate([key[h].astype(bf16), query[h].astype(bf16)], axis=0),
            TN,
        )
        for h in each
    ]
    dquery_start = [start[h] * reads[h][:CHUNK] for h in each]
    dkey_start = [-start[h] * reads[h][CHUNK:] for h in each]
    v_total, v_gate = zip(*[signal(2, head) for head in each])
    for h in each:
        dlower = -by_pseudo[h][CHUNK:]
        start_terms = dkey_start[h] * key[h]
        dbeta = jnp.sum(
            solved[h] * (v_total[h] * v_gate[h]) + start_terms + dlower * lower_raw[h],
            axis=-1,
            keepdims=True,
        )
        pair = by_pseudo[h][:CHUNK] * scores[h] + dlower * lower[h]
        end_terms = dkey_end[h] * key[h]
        dcum = jnp.sum(
            pair + dquery_start[h] * query[h] + start_terms * beta[h] - end_terms,
            axis=-1,
            keepdims=True,
        )
        last_total = jnp.sum(
            jnp.sum(end_terms, axis=0, keepdims=True)
            + keep[h] * jnp.sum(memory[h] * dmemory[h], axis=0, keepdims=True),
            axis=-1,
            keepdims=True,
        )
        dcum = dcum + jnp.where(row[:, :1] == CHUNK - 1, last_total, 0.0)
        cum_columns = cum_columns + jnp.where(lane == h, dcum, 0.0)
        dbeta_columns = dbeta_columns + jnp.where(lane == heads + h, dbeta, 0.0)
        cum_rows = cum_rows + jnp.where(row == h, jnp.sum(pair, axis=0, keepdims=True), 0.0)
    dkey = [
        toward[h][:CHUNK] + turned[h] + beta[h] * dkey_start[h] + dkey_end[h] for h in each
    ]
    dquery = [(toward[h][CHUNK:] + dquery_start[h]) * WIDTH**-0.5 for h in each]
    dq_act = [
        q_norm[h] * (dquery[h] - q_unit[h] * jnp.sum(q_unit[h] * dquery[h], axis=-1, keepdims=True))
        for h in each
    ]
    dk_act = [
        k_norm[h] * (dkey[h] - key[h] * jnp.sum(key[h] * dkey[h], axis=-1, keepdims=True))
        for h in each
    ]
    for h in each:
        signal_back(0, h, q_total[h], q_gate[h], dq_act[h])
        signal_back(1, h, k_total[h], k_gate[h], dk_act[h])
        signal_back(2, h, v_total[h], v_gate[h], beta[h] * solved[h])

    upper_ones = jnp.where(row <= col, 1.0, 0.0).astype(f32)
    dsteps = dot_exact(upper_ones, cum_columns - cum_rows.T, NN)
    drate_ref[...] += jnp.sum(dsteps * steps, axis=0, keepdims=True)
    dgain_ref[...] += dgain
    dlogits = dsteps * neg_rate * betas + dbeta_columns * betas * (1.0 - betas)
    dproj_ref[:, 4 * wide : 4 * wide + WIDTH] = jnp.where(
        lane < 2 * heads, dlogits, 0.0
    ).astype(bf16)


def mixer_forward(x, weights, heads, seg_wide, conv_rows, neg_rate, gain):
    length, model = x.shape
    wide = heads * WIDTH
    width = 4 * wide + WIDTH
    count = length // CHUNK
    subs = 2 if count % 2 == 0 else 1
    by_chunk = lambda cols: pl.BlockSpec((subs * CHUNK, cols), lambda i: (i, 0))
    whole = lambda rows, cols: pl.BlockSpec((rows, cols), lambda i: (0, 0))
    return pl.pallas_call(
        functools.partial(forward_kernel, heads, subs),
        grid=(count // subs,),
        in_specs=[
            whole(length, model), whole(model, width), by_chunk(WIDTH), whole(12, wide), whole(1, WIDTH), whole(1, WIDTH),
        ],
        out_specs=[
            by_chunk(width), by_chunk(wide), by_chunk(wide), by_chunk(wide), by_chunk(wide), by_chunk(wide),
            pl.BlockSpec((subs, heads, WIDTH, WIDTH), lambda i: (i, 0, 0, 0)),
            by_chunk(3 * wide),
        ],
        out_shape=[
            pltpu.HBM((length, width), f32),
            pltpu.HBM((length, wide), bf16),
            pltpu.HBM((length, wide), bf16),
            pltpu.HBM((length, wide), bf16),
            pltpu.HBM((length, wide), bf16),
            pltpu.HBM((length, wide), f32),
            pltpu.HBM((count, heads, WIDTH, WIDTH), f32),
            pltpu.HBM((length, 3 * wide), f32),
        ],
        scratch_shapes=[
            pltpu.VMEM((heads, WIDTH, WIDTH), f32),
            pltpu.VMEM((HALO, 3 * wide), f32),
            pltpu.VMEM((HALO, WIDTH), f32),
            pltpu.VMEM((subs * CHUNK, width), f32),
        ],
        compiler_params=pltpu.CompilerParams(vmem_limit_bytes=48 * 1024 * 1024),
        cost_estimate=pl.CostEstimate(
            flops=2 * 160 * length * WIDTH * wide + 2 * length * model * width,
            bytes_accessed=2 * model * (length + width) + 4 * length * (width + 6 * wide),
            transcendentals=8 * length * wide,
        ),
        name="mixer_forward",
    )(*in_hbm(x, weights, seg_wide, conv_rows, neg_rate, gain))


def mixer_backward(proj, seg_wide, conv_rows, neg_rate, gain, rank, grads, saved):
    length, width = proj.shape
    heads = (width - WIDTH) // (4 * WIDTH)
    wide = heads * WIDTH
    count = length // CHUNK
    back = lambda i: count - 1 - i
    by_chunk = lambda cols: pl.BlockSpec((CHUNK, cols), lambda i, rank: (back(i), 0))
    before = lambda cols: pl.BlockSpec(
        (HALO, cols), lambda i, rank: (jnp.maximum(back(i) * (CHUNK // HALO) - 1, 0), 0)
    )
    whole = lambda rows, cols: pl.BlockSpec((rows, cols), lambda i, rank: (0, 0))
    part_count = grads[0].shape[0] // CHUNK

    def grad_block(other):
        def index(i, rank):
            first = (1 - rank[0] if other else rank[0]) * part_count
            return jnp.clip(back(i) - first, 0, part_count - 1), 0

        return pl.BlockSpec((CHUNK, wide), index)

    grad_blocks = [grad_block(False), grad_block(True)] if len(grads) == 2 else [by_chunk(wide)]
    grid_spec = pltpu.PrefetchScalarGridSpec(
        num_scalar_prefetch=1,
        grid=(count,),
        in_specs=[
            by_chunk(width), by_chunk(WIDTH), before(WIDTH), before(3 * wide),
            whole(12, wide), whole(1, WIDTH), whole(1, WIDTH),
            *grad_blocks,
            by_chunk(wide), by_chunk(wide), by_chunk(wide), by_chunk(wide),
            pl.BlockSpec((1, heads, WIDTH, WIDTH), lambda i, rank: (back(i), 0, 0, 0)),
            by_chunk(3 * wide),
        ],
        out_specs=[by_chunk(width), whole(12, wide), whole(1, WIDTH), whole(1, WIDTH)],
        scratch_shapes=[
            pltpu.VMEM((heads, WIDTH, WIDTH), f32),
            pltpu.VMEM((HALO, 3 * wide), f32),
        ],
    )
    return pl.pallas_call(
        functools.partial(backward_kernel, heads, len(grads)),
        grid_spec=grid_spec,
        out_shape=[
            pltpu.HBM((length, width), bf16),
            pltpu.HBM((12, wide), f32),
            pltpu.HBM((1, WIDTH), f32),
            pltpu.HBM((1, WIDTH), f32),
        ],
        compiler_params=pltpu.CompilerParams(vmem_limit_bytes=48 * 1024 * 1024),
        cost_estimate=pl.CostEstimate(
            flops=2 * 180 * length * WIDTH * wide,
            bytes_accessed=4 * length * (2 * width + 3 * wide),
            transcendentals=8 * length * wide,
        ),
        name="mixer_backward",
    )(rank, *in_hbm(proj, seg_wide, seg_wide, proj, conv_rows, neg_rate, gain, *grads, *saved))


def ffn_kernel(tiles, x_ref, dy_ref, w_ref, h_ref, g_ref, y_ref, dx_ref, y_sum, dx_sum):
    step = pl.program_id(0)

    @pl.when(step == 0)
    def _():
        y_sum[...] = jnp.zeros_like(y_sum)
        dx_sum[...] = jnp.zeros_like(dx_sum)

    def units(size):
        gate_up = dot(x_ref[...], w_ref[:, : 2 * size], NN)
        grad = dot(dy_ref[...], w_ref[:, 2 * size : 3 * size], NN)
        gate, up = gate_up[:, :size], gate_up[:, size:]
        gate_s = sigmoid(gate)
        act = gate * gate_s
        h_ref[:, :size] = (act * up).astype(bf16)
        g_ref[:, :size] = (grad * up * (gate_s + act * (1.0 - gate_s))).astype(bf16)
        g_ref[:, size : 2 * size] = (grad * act).astype(bf16)
        y_sum[...] += dot(h_ref[:, :size], w_ref[:, 2 * size : 3 * size], NT)
        dx_sum[...] += dot(g_ref[:, : 2 * size], w_ref[:, : 2 * size], NT)

    per_tile(tiles, step, units)

    @pl.when(step == len(tiles) - 1)
    def _():
        y_ref[...] = y_sum[...].astype(bf16)
        dx_ref[...] = dx_sum[...].astype(bf16)


def per_tile(tiles, step, units):
    if tiles[0] == tiles[-1]:
        units(tiles[0])
        return

    @pl.when(step < len(tiles) - 1)
    def _():
        units(tiles[0])

    @pl.when(step == len(tiles) - 1)
    def _():
        units(tiles[-1])


def ffn(x, dy, packed, tiles):
    rows, model = x.shape
    hidden = sum(tiles)
    whole = pl.BlockSpec((rows, model), lambda i: (0, 0))
    return pl.pallas_call(
        functools.partial(ffn_kernel, tiles),
        grid=(len(tiles),),
        in_specs=[whole, whole, pl.BlockSpec((model, 3 * tiles[0]), lambda i: (0, i))],
        out_specs=[
            pl.BlockSpec((rows, tiles[0]), lambda i: (0, i)),
            pl.BlockSpec((rows, 2 * tiles[0]), lambda i: (0, i)),
            whole,
            whole,
        ],
        out_shape=[
            pltpu.HBM((rows, hidden), bf16),
            pltpu.HBM((rows, 2 * hidden), bf16),
            pltpu.HBM((rows, model), bf16),
            pltpu.HBM((rows, model), bf16),
        ],
        scratch_shapes=[pltpu.VMEM((rows, model), f32), pltpu.VMEM((rows, model), f32)],
        compiler_params=pltpu.CompilerParams(vmem_limit_bytes=48 * 1024 * 1024),
        cost_estimate=pl.CostEstimate(
            flops=12 * rows * model * hidden,
            bytes_accessed=2 * (3 * model * hidden + rows * (4 * model + 3 * hidden)),
            transcendentals=rows * hidden,
        ),
        name="ffn",
    )(*in_hbm(x, dy, packed))


def turn_rows(core_ref, order, turned, source):
    half = len(order) // 2
    size = source.shape[0] // len(order)
    for at, block in enumerate(order):
        away = (block % 2 + 1 + core_ref[0]) % 2
        begin = (away * half + at % half) * size
        rows = pl.ds(pl.multiple_of(begin, size), size)
        turned[rows, :] = source[block * size : (block + 1) * size, :]


def ffn_grads_kernel(tiles, *refs):
    *inputs, out_ref, x_turned, dy_turned = refs
    count = len(inputs) // 4
    xs, dys, hs, gs = (inputs[at * count : (at + 1) * count] for at in range(4))
    step = pl.program_id(0)
    ends = [0]
    for x_ref in xs:
        ends.append(ends[-1] + x_ref.shape[0])
    lanes = [slice(first, last) for first, last in zip(ends, ends[1:])]

    @pl.when(step == 0)
    def _():
        for at, x_ref, dy_ref in zip(lanes, xs, dys):
            x_turned[:, at] = x_ref[...].T
            dy_turned[:, at] = dy_ref[...].T

    def units(size):
        up_grad, down_grad = 0.0, 0.0
        for at, h_ref, g_ref in zip(lanes, hs, gs):
            up_grad = up_grad + dot(x_turned[:, at], g_ref[:, : 2 * size], NN)
            down_grad = down_grad + dot(dy_turned[:, at], h_ref[:, :size], NN)
        out_ref[:, : 2 * size] = up_grad.astype(bf16)
        out_ref[:, 2 * size : 3 * size] = down_grad.astype(bf16)

    per_tile(tiles, step, units)


def ffn_grads(xs, dys, hs, gs, tiles):
    model = xs[0].shape[1]
    hidden = sum(tiles)
    total = sum(x.shape[0] for x in xs)
    whole = [pl.BlockSpec(x.shape, lambda i: (0, 0)) for x in xs]
    return pl.pallas_call(
        functools.partial(ffn_grads_kernel, tiles),
        grid=(len(tiles),),
        in_specs=whole
        + whole
        + [pl.BlockSpec((x.shape[0], tiles[0]), lambda i: (0, i)) for x in xs]
        + [pl.BlockSpec((x.shape[0], 2 * tiles[0]), lambda i: (0, i)) for x in xs],
        out_specs=pl.BlockSpec((model, 3 * tiles[0]), lambda i: (0, i)),
        out_shape=pltpu.HBM((model, 3 * hidden), bf16),
        scratch_shapes=[pltpu.VMEM((model, total), bf16), pltpu.VMEM((model, total), bf16)],
        compiler_params=pltpu.CompilerParams(vmem_limit_bytes=48 * 1024 * 1024),
        cost_estimate=pl.CostEstimate(
            flops=6 * total * model * hidden,
            bytes_accessed=2 * (3 * model * hidden + total * (2 * model + 3 * hidden)),
            transcendentals=0,
        ),
        name="ffn_grads",
    )(*in_hbm(*xs, *dys, *hs, *gs))


def turn_rows(core_ref, order, turned, source):
    half = len(order) // 2
    size = source.shape[0] // len(order)
    for at, block in enumerate(order):
        away = (block % 2 + 1 + core_ref[0]) % 2
        begin = (away * half + at % half) * size
        rows = pl.ds(pl.multiple_of(begin, size), size)
        turned[rows, :] = source[block * size : (block + 1) * size, :]


def mixer_grads_kernel(
    orders, split, main_steps, parts, core_ref, normed_ref, dproj_ref, conv_ref, *refs
):
    residual_refs, mixed_refs, refs = refs[:parts], refs[parts : 2 * parts], refs[2 * parts :]
    first_sent_ref, first_kept_ref, second_sent_ref, second_kept_ref, *refs = refs
    turned, conv_turned, *residuals_turned = refs
    step = pl.program_id(0)
    last = pl.num_programs(0) - 1
    first_order, second_order = orders
    count = len(first_order)
    size = normed_ref.shape[1] // count

    @pl.when(step == 0)
    def _():
        turn_rows(core_ref, first_order, turned, normed_ref[...].T)
        for residual_turned, residual_ref in zip(residuals_turned, residual_refs):
            turn_rows(core_ref, first_order, residual_turned, residual_ref[...].T)
        turn_rows(core_ref, first_order, conv_turned, conv_ref[...])

    def store(grads, lanes):
        grads = grads.astype(bf16)
        half = count // 2 * size

        @pl.when(step < split)
        def _():
            first_sent_ref[:, lanes] = grads[:half]
            first_kept_ref[:, lanes] = grads[half:]

        @pl.when(step >= split)
        def _():
            for to, block in enumerate(second_order[: count // 2]):
                at = first_order.index(block)
                to_rows = slice(to * size, (to + 1) * size)
                second_sent_ref[to_rows, lanes] = grads[at * size : (at + 1) * size]
                second_kept_ref[to_rows, lanes] = grads[half + at * size : half + (at + 1) * size]

    @pl.when(step < main_steps)
    def _():
        store(dot(turned[...], dproj_ref[...], NN), slice(None))

    @pl.when((step >= main_steps) & (step < last))
    def _():
        grads = 0.0
        for residual_turned, mixed_ref in zip(residuals_turned, mixed_refs):
            grads = grads + dot(residual_turned[...], mixed_ref[...], NN)
        store(grads, slice(None))

    @pl.when(step == last)
    def _():
        store(dot(turned[...], dproj_ref[:, :WIDTH], NN) + conv_turned[...], slice(0, WIDTH))


def mixer_grads(normed, residuals, dproj, mixed_parts, conv_block, core, orders):
    rows, model = normed.shape
    wide = mixed_parts[0].shape[1]
    parts = len(residuals)
    part_rows = residuals[0].shape[0]
    tile = 2 * WIDTH if wide % (2 * WIDTH) == 0 else WIDTH
    main_steps = 4 * wide // tile
    out_steps = wide // tile
    columns = 5 * wide + WIDTH
    split = (main_steps + out_steps + 1) * 5 // 11
    first = split * tile
    whole = lambda rows, cols: pl.BlockSpec((rows, cols), lambda i, core: (0, 0))
    mixed_block = pl.BlockSpec(
        (part_rows, tile), lambda i, core: (0, jnp.clip(i - main_steps, 0, out_steps - 1))
    )
    first_block = pl.BlockSpec((model // 2, tile), lambda i, core: (0, jnp.minimum(i, split - 1)))
    second_block = pl.BlockSpec((model // 2, tile), lambda i, core: (0, jnp.maximum(i - split, 0)))
    first_shape = pltpu.HBM((model // 2, first), bf16)
    second_shape = pltpu.HBM((model // 2, columns - first), bf16)
    return pl.pallas_call(
        functools.partial(mixer_grads_kernel, orders, split, main_steps, parts),
        grid_spec=pltpu.PrefetchScalarGridSpec(
            num_scalar_prefetch=1,
            grid=(main_steps + out_steps + 1,),
            in_specs=[
                whole(rows, model),
                pl.BlockSpec((rows, tile), lambda i, core: (0, jnp.minimum(i, main_steps))),
                whole(model, WIDTH),
            ]
            + [whole(part_rows, model)] * parts
            + [mixed_block] * parts,
            out_specs=[first_block, first_block, second_block, second_block],
            scratch_shapes=[
                pltpu.VMEM((model, rows), bf16),
                pltpu.VMEM((model, WIDTH), f32),
            ]
            + [pltpu.VMEM((model, part_rows), bf16)] * parts,
        ),
        out_shape=[first_shape, first_shape, second_shape, second_shape],
        compiler_params=pltpu.CompilerParams(vmem_limit_bytes=40 * 1024 * 1024),
        cost_estimate=pl.CostEstimate(
            flops=2 * rows * model * columns,
            bytes_accessed=2 * (2 * rows * model + (rows + model) * columns),
            transcendentals=0,
        ),
        name="mixer_grads",
    )(core, *in_hbm(normed, dproj, conv_block, *residuals, *mixed_parts))


def rms_norm(values, scales):
    return values * lax.rsqrt(jnp.mean(values * values, axis=-1, keepdims=True) + norm_eps) * scales


def first_norm(values, gains):
    return rms_norm(values, gains[0])


def second_norm(values, gains):
    return rms_norm(values, gains[1])


def contract_last(operand, other):
    return lax.dot_general(
        operand, other, (((1,), (1,)), ((), ())), preferred_element_type=jnp.float32
    )


def contract_first(operand, other):
    return lax.dot_general(
        operand, other, (((0,), (0,)), ((), ())), preferred_element_type=jnp.float32
    )


def swap(rows):
    return lax.ppermute(rows, "tensor", [(0, 1), (1, 0)])


def sum_steps(axis):
    size = lax.axis_size(axis)
    if size & (size - 1):
        return [lambda values: lax.psum(values, axis)]

    def step(bit, values):
        def across(mask):
            return lax.ppermute(values, axis, [(i, i ^ mask) for i in range(size)])

        if 2 * bit < size:
            return (values + across(bit)) + (across(2 * bit) + across(3 * bit))
        return values + across(bit)

    return [functools.partial(step, 1 << at) for at in range(0, size.bit_length() - 1, 2)]


def hidden_tiles(hidden):
    if hidden % WIDTH:
        return (hidden,)
    size = min(4 * WIDTH, hidden)
    return (size,) * (hidden // size) + ((hidden % size,) if hidden % size else ())


def pack_tiles(parts, tiles):
    blocks = []
    at = 0
    for size in tiles:
        blocks += [part[:, at : at + size] for part in parts]
        at += size
    return jnp.concatenate(blocks, axis=1)


def unpack_tiles(packed, tiles, count):
    parts = [[] for _ in range(count)]
    at = 0
    for size in tiles:
        for part in parts:
            part.append(packed[:, at : at + size])
            at += size
    return [jnp.concatenate(part, axis=1) for part in parts]


def ffn_plain(x, dy, packed, tiles):
    gate_w, up_w, down_w = unpack_tiles(packed, tiles, 3)
    gate = jnp.dot(x, gate_w, preferred_element_type=f32)
    up = jnp.dot(x, up_w, preferred_element_type=f32)
    grad = jnp.dot(dy, down_w, preferred_element_type=f32)
    gate_s = sigmoid(gate)
    act = gate * gate_s
    hidden = (act * up).astype(bf16)
    gate_grad = (grad * up * (gate_s + act * (1.0 - gate_s))).astype(bf16)
    up_grad = (grad * act).astype(bf16)
    share = contract_last(hidden, down_w).astype(bf16)
    dx = (contract_last(gate_grad, gate_w) + contract_last(up_grad, up_w)).astype(bf16)
    return hidden, jnp.concatenate([gate_grad, up_grad], axis=1), share, dx


def ffn_grads_plain(x, dy, hidden, grads, tiles):
    size = hidden.shape[1]
    parts = [
        contract_first(x, grads[:, :size]),
        contract_first(x, grads[:, size:]),
        contract_first(dy, hidden),
    ]
    return pack_tiles([part.astype(bf16) for part in parts], tiles)


def bit_orders(size):
    bits = list(range(size.bit_length() - 1))
    return bits, bits[:1] + bits[2:] + bits[1:2]


def block_order(size, bits):
    return sorted(range(size), key=lambda i: [(i >> bit) & 1 for bit in bits])


def outgoing(terms, bit):
    mine = lax.axis_index("dp") >> bit & 1
    half = terms[0].shape[0] // 2
    total = 0.0
    for term in terms:
        total = total + lax.dynamic_slice_in_dim(term, (1 - mine) * half, half).astype(f32)
    return total.astype(bf16)


def settle(terms, bit, sent):
    mine = lax.axis_index("dp") >> bit & 1
    half = terms[0].shape[0] // 2
    own = [lax.dynamic_slice_in_dim(term, mine * half, half) for term in terms]
    return own + [flip(sent, bit)]


def flip(values, bit):
    size = lax.axis_size("dp")
    return lax.ppermute(values, "dp", [(i, i ^ (1 << bit)) for i in range(size)])


def local(
    tokens,
    segment_ids,
    norm_gains,
    w_mixer_in,
    w_rates,
    conv_weight,
    a_log,
    out_gain,
    w_output,
    w_gate_up,
    w_down,
    cotangent,
):
    dp_size = lax.axis_size("dp")
    pair = lax.axis_size("tensor") == 2
    tensor_rank = lax.axis_index("tensor")
    rows_here, _, heads, _ = w_mixer_in.shape
    model_width = rows_here * dp_size
    wide = heads * WIDTH
    hidden_here = w_gate_up.shape[2]
    tiles = hidden_tiles(hidden_here)
    kernels = hidden_here % WIDTH == 0
    taps_here = conv_weight.shape[3]
    own_rows = tokens.shape[1]
    projected_width = 4 * wide + WIDTH

    def gather_rows(rows):
        return lax.all_gather(rows, "tensor", axis=0, tiled=True)

    def scatter_rows(product):
        return lax.psum_scatter(product.astype(bf16), "tensor", scatter_dimension=0, tiled=True)

    def in_order(own, other):
        first = tensor_rank == 0
        return jnp.concatenate([jnp.where(first, own, other), jnp.where(first, other, own)], axis=0)

    def own_and_other(rows):
        own = lax.dynamic_slice_in_dim(rows, tensor_rank * own_rows, own_rows)
        return own, lax.dynamic_slice_in_dim(rows, (1 - tensor_rank) * own_rows, own_rows)

    conv_block = jnp.pad(
        conv_weight.transpose(3, 0, 1, 2).reshape(taps_here, 12 * heads),
        ((0, rows_here - taps_here), (0, WIDTH - 14 * heads)),
    )
    mixer_pack = jnp.concatenate(
        [
            w_mixer_in.reshape(rows_here, -1),
            w_rates.reshape(rows_here, -1),
            conv_block,
            w_output.T,
        ],
        axis=1,
    )
    mix_full = lax.all_gather(mixer_pack, "dp", axis=0, tiled=True)
    ffn_pack = pack_tiles([w_gate_up[:, 0], w_gate_up[:, 1], w_down.T], tiles)
    ffn_full = lax.all_gather(ffn_pack, "dp", axis=0, tiled=True)
    out_mine = mix_full[:, projected_width:]
    conv_at = 4 * wide + 2 * heads
    conv_rows = (
        mix_full[:, conv_at : conv_at + 12 * heads]
        .reshape(dp_size, rows_here, 12 * heads)[:, :taps_here]
        .reshape(dp_size * taps_here, 12 * heads)
        .T.reshape(12, wide)
        .astype(f32)
    )
    segment = jnp.broadcast_to(segment_ids[0][:, None].astype(f32), (segment_ids.shape[1], WIDTH))
    neg_rate = jnp.pad(
        -jnp.exp(lax.dynamic_slice_in_dim(a_log, tensor_rank * heads, heads)), (0, WIDTH - heads)
    )[None]
    gain_row = out_gain[None]

    grad_own = cotangent[0]
    inputs = tokens[0].astype(f32)
    normed, first_back = jax.vjp(first_norm, inputs, norm_gains)
    normed = normed.astype(bf16)
    if pair:
        normed_other = swap(normed)
        grad_sent, normed_other, segment, neg_rate = lax.optimization_barrier(
            (grad_own, normed_other, segment, neg_rate)
        )
        grad_other = swap(grad_sent)
        normed_all, grad_other, out_sent = lax.optimization_barrier(
            (in_order(normed, normed_other), grad_other, out_mine)
        )
        out_other = swap(out_sent)
    else:
        normed_all = gather_rows(normed)
    projected, mixed, *saved = mixer_forward(
        normed_all, mix_full, heads, segment, conv_rows, neg_rate, gain_row
    )
    if pair:
        mixed, out_other = lax.optimization_barrier((mixed, out_other))
        mixed_own, mixed_theirs = own_and_other(mixed)
        share = contract_last(mixed_own, out_mine) + contract_last(swap(mixed_theirs), out_other)
    else:
        share = scatter_rows(contract_last(mixed, out_mine)).astype(f32)
    residual = inputs + share
    normed_ffn, second_back = jax.vjp(second_norm, residual, norm_gains)
    normed_ffn = normed_ffn.astype(bf16)
    one_ffn = ffn if kernels else ffn_plain
    if pair:
        half = own_rows // 2
        x_others = [swap(normed_ffn[:half]), swap(normed_ffn[half:])]
        others = []
        for at, x_other in enumerate(x_others):
            others.append(one_ffn(x_other, grad_other[at * half : (at + 1) * half], ffn_full, tiles))
        received = [swap(other[3]) for other in others]
        done = [one_ffn(normed_ffn, grad_own, ffn_full, tiles)] + others
        x_parts = [normed_ffn] + x_others
        dy_parts = [grad_own, grad_other[:half], grad_other[half:]]
        dx = done[0][3].astype(f32) + jnp.concatenate(received, axis=0).astype(f32)
    else:
        x_parts = [gather_rows(normed_ffn)]
        dy_parts = [gather_rows(grad_own)]
        done = [one_ffn(x_parts[0], dy_parts[0], ffn_full, tiles)]
        dx = scatter_rows(done[0][3]).astype(f32)
    h_parts, g_parts, y_parts, _ = zip(*done)
    core = lax.axis_index("dp") % 2
    bits = bit_orders(dp_size)
    orders = [block_order(dp_size, order) for order in bits]
    if kernels:
        ffn_sums = ffn_grads(x_parts, dy_parts, h_parts, g_parts, tiles)
    else:
        ffn_sums = ffn_grads_plain(x_parts[0], dy_parts[0], h_parts[0], g_parts[0], tiles)
    residual_part, second_gains = second_back(dx)
    residual_grad = grad_own.astype(f32) + residual_part
    residual_low = residual_grad.astype(bf16)
    if pair:
        grad_theirs = jnp.dot(residual_low, out_other, preferred_element_type=f32).astype(bf16)
        grad_mine = jnp.dot(residual_low, out_mine, preferred_element_type=f32).astype(bf16)
        grad_mine, mixed_grad, ffn_sums, residual_sent, y_first, y_last = lax.optimization_barrier(
            (
                grad_mine,
                swap(grad_theirs),
                ffn_sums,
                residual_low,
                y_parts[1],
                y_parts[2],
            )
        )
        mixed_grads = [grad_mine, mixed_grad]
        residuals = [residual_low, swap(residual_sent)]
        mixed_parts = [mixed_own, mixed_theirs]
    else:
        residuals = [gather_rows(residual_low)]
        mixed_grads = [jnp.dot(residuals[0], out_mine, preferred_element_type=f32).astype(bf16)]
        mixed_parts = [mixed]
    ffn_owned = lax.psum_scatter(ffn_sums, "dp", scatter_dimension=0, tiled=True)
    projection_grad, conv_grad, log_grad, gain_grad = mixer_backward(
        projected, segment, conv_rows, neg_rate, gain_row, tensor_rank[None], mixed_grads, saved
    )
    conv_grad = jnp.pad(
        conv_grad.reshape(12 * heads, WIDTH).T.reshape(dp_size, taps_here, 12 * heads),
        ((0, 0), (0, rows_here - taps_here), (2 * heads, WIDTH - 14 * heads)),
    ).reshape(model_width, WIDTH)
    mix_rows = mix_full[:, :projected_width]
    first_sent, first_kept, second_sent, second_kept = mixer_grads(
        normed_all, residuals, projection_grad, mixed_parts, conv_grad, core[None], orders
    )
    projection_grad, _, _ = lax.optimization_barrier((projection_grad, first_sent, second_sent))
    second = [second_kept, flip(second_sent, 0)]
    first = [first_kept, flip(first_sent, 0)]
    second_out = outgoing(second, bits[1][1])
    first_out = outgoing(first, bits[0][1])
    if pair:
        grad_here, grad_there = own_and_other(projection_grad)
        first_out, second_out, grad_there = lax.optimization_barrier(
            (first_out, second_out, grad_there)
        )
        received = swap(contract_last(grad_there, mix_rows).astype(bf16))
    else:
        received = scatter_rows(contract_last(projection_grad, mix_rows))
    first = settle(first, bits[0][1], first_out)
    second = settle(second, bits[1][1], second_out)
    first_out = outgoing(first, bits[0][2])
    second_out = outgoing(second, bits[1][2])
    if pair:
        y_first, y_last, _ = lax.optimization_barrier((y_first, y_last, second_out))
        received, grad_here, _ = lax.optimization_barrier((received, grad_here, first_out))
        y_other = jnp.concatenate([swap(y_first), swap(y_last)], axis=0)
        mixer_input_grad = received.astype(f32) + contract_last(grad_here, mix_rows)
    else:
        y_other = scatter_rows(y_parts[0])
        mixer_input_grad = received.astype(f32)
    first = settle(first, bits[0][2], first_out)
    second = settle(second, bits[1][2], second_out)
    input_part, first_gains = first_back(mixer_input_grad)
    input_grad = (residual_grad + input_part).astype(bf16)[None]
    log_full = lax.dynamic_update_slice_in_dim(
        jnp.zeros(a_log.shape, f32), log_grad[0, :heads], tensor_rank * heads, 0
    )
    last_row = jnp.concatenate([gain_grad[0], log_full])
    last_row = jnp.pad(last_row, (0, model_width - last_row.shape[0]))[None]
    small = jnp.concatenate([first_gains + second_gains, last_row], axis=0)
    for one, other in zip(bits[0][3:], bits[1][3:]):
        last_out = first_out
        first_out = outgoing(first, one)
        second_out = outgoing(second, other)
        second_out, _ = lax.optimization_barrier((second_out, last_out))
        small, _ = lax.optimization_barrier((small, first_out))
        first = settle(first, one, first_out)
        second = settle(second, other, second_out)
    y = y_other.astype(f32)
    if pair:
        y = y + y_parts[0].astype(f32)
    out_tokens = (residual + y).astype(bf16)[None]
    *steps, last_step = sum_steps("tensor") + sum_steps("dp")
    for step in steps:
        small = step(small)
    gate_grad, up_grad, down_grad = unpack_tiles(ffn_owned, tiles, 3)
    up_owned = jnp.stack([gate_grad, up_grad], axis=1).astype(f32)
    down_owned = down_grad.T.astype(f32)
    small = last_step(small)
    first[-1], out_tokens, up_owned, down_owned = lax.optimization_barrier(
        (first[-1], out_tokens, up_owned, down_owned)
    )
    mix_owned = jnp.concatenate(
        [sum(term.astype(f32) for term in terms) for terms in (first, second)], axis=1
    )
    rates = mix_owned[:, 5 * wide :]
    return (
        out_tokens,
        input_grad,
        small[:2],
        mix_owned[:, : 4 * wide].reshape(w_mixer_in.shape),
        rates[:, : 2 * heads].reshape(w_rates.shape),
        rates[:taps_here, 2 * heads : 14 * heads]
        .reshape(taps_here, 3, 4, heads)
        .transpose(1, 2, 3, 0),
        small[2, WIDTH : WIDTH + a_log.shape[0]],
        small[2, :WIDTH],
        mix_owned[:, 4 * wide : 5 * wide].T,
        up_owned,
        down_owned,
    )


def solution(mesh):
    in_specs = (
        P("dp", "tensor", None),
        P("dp", None),
        P(),
        P("dp", None, "tensor", None),
        P("dp", None, "tensor"),
        P(None, None, "tensor", "dp"),
        P(),
        P(),
        P("tensor", "dp"),
        P("dp", None, "tensor"),
        P("tensor", "dp"),
        P("dp", "tensor", None),
    )
    out_specs = (
        P("dp", "tensor", None),
        P("dp", "tensor", None),
        P(),
        P("dp", None, "tensor", None),
        P("dp", None, "tensor"),
        P(None, None, "tensor", "dp"),
        P(),
        P(),
        P("tensor", "dp"),
        P("dp", None, "tensor"),
        P("tensor", "dp"),
    )
    return jax.shard_map(local, mesh=mesh, in_specs=in_specs, out_specs=out_specs, check_vma=False)
```
